128 devices in a mesh: dp: 64 (over y_lo, z, x, core), tensor: 2 (over y_hi).
Axes of the slice: x: 4, y: 4 (y_hi: 2, y_lo: 2; y = y_hi * 2 + y_lo), z: 4, core: 2. Of those that a mesh axis runs over, the one named last changes fastest.
Arguments:
- node_input: bfloat16 [16384, 64], P('dp'), may hold values from -6 to 6
- geometry: float32 [16384, 3], P('dp'), may hold values from -1 to 1
- counts: int32 [64], P('dp'), may hold values from 192 to 256, as said below
- parent_mid: int32 [16384], P('dp'), may hold values from 0 to 63
- parent_top: int32 [4096], P('dp'), may hold values from 0 to 15
- neighbours_fine: int32 [16384, 8], P('dp'), may hold values from 0 to 255
- neighbours_mid: int32 [4096, 8], P('dp'), may hold values from 0 to 63
- neighbours_top: int32 [1024, 8], P('dp'), may hold values from 0 to 15
- w_first: bfloat16 [2, 6, 256], P(None, None, 'tensor'), may hold values from -3 to 3
- b_first: bfloat16 [2, 256], P(None, 'tensor'), may hold values from -3 to 3
- w_second: bfloat16 [2, 256, 256], P(None, 'tensor'), may hold values from -0.375 to 0.375
- b_second: bfloat16 [2, 256], replicated, may hold values from -3 to 3
- w_kernel: bfloat16 [2, 256, 4096], P(None, None, 'tensor'), may hold values from -0.046875 to 0.046875
- b_kernel: bfloat16 [2, 4096], P(None, 'tensor'), may hold values from -0.359375 to 0.359375
- w_self: bfloat16 [2, 64, 64], replicated, may hold values from -0.75 to 0.75
- cotangent: bfloat16 [16384, 64], P('dp'), may hold values from -6 to 6
Outputs:
- output: bfloat16 [16384, 64], P('dp')
- input_grad: float32 [16384, 64], P('dp')
- grad_w_first: float32 [2, 6, 256], P(None, None, 'tensor')
- grad_b_first: float32 [2, 256], P(None, 'tensor')
- grad_w_second: float32 [2, 256, 256], P(None, 'tensor')
- grad_b_second: float32 [2, 256], replicated
- grad_w_kernel: float32 [2, 256, 4096], P(None, None, 'tensor')
- grad_b_kernel: float32 [2, 4096], P(None, 'tensor')
- grad_w_self: float32 [2, 64, 64], replicated
The draws below stay inside these ranges and needn't reach their ends.
Inputs may be any that keep to these rules, and one draw needn't show every extreme that they name: `counts`: each graph holds at least 192 live nodes, its first ones; some graph holds 256.
All inputs are finite; a program needn't handle non-finite values.
Results may differ from the reference program's by a relative error of at most 0.0073.
Values may be sent and summed in bfloat16 or wider, within the bound.
No kernel may reach another device: no remote copies, remote signals or barrier semaphores. Data moves between devices by JAX's collectives and lax.ppermute only.
A program may use at most 192 MiB of HBM per device.

```python
import jax
import jax.numpy as jnp
from jax import lax

C = 64
HID = 256
EDGE_IN = 6
DEG = 8
LAYERS = 2
N0 = 256
N1 = 64
N2 = 16
GRAPHS = 64
NODES0 = 16384
NODES1 = 4096
NODES2 = 1024
KCOLS = 4096


def draw_counts(key, part):
    key = jax.random.fold_in(key, 5)
    first_key, second_key = jax.random.split(key)
    values = jax.random.randint(first_key, (GRAPHS,), 3 * N0 // 4, N0 + 1)
    chosen = jax.random.randint(second_key, (), 0, GRAPHS)
    return jnp.where(jnp.arange(GRAPHS) == chosen, N0, values).astype(jnp.int32)


def draw_geometry(key, part):
    key = jax.random.fold_in(key, 7)
    scale_key, centre_key, point_key = jax.random.split(key, 3)
    spread = jnp.exp(jax.random.uniform(scale_key, (GRAPHS, 1, 3), jnp.float32, -1.2, 0.0))
    centre = (1.0 - spread) * jax.random.uniform(centre_key, (GRAPHS, 1, 3), jnp.float32, -1.0, 1.0)
    local = jax.random.uniform(point_key, (GRAPHS, N0, 3), jnp.float32, -1.0, 1.0)
    return (centre + spread * local).reshape(GRAPHS * N0, 3).astype(jnp.float32)


def with_ends(values, stream_key, smallest, top_value):
    longest = values.shape.index(max(values.shape))
    spots = []
    for shift in (0, 1):
        where = [jax.random.randint(jax.random.fold_in(stream_key, axis), (), 0, length) for axis, length in enumerate(values.shape)]
        where[longest] = (where[longest] + shift) % values.shape[longest]
        spots.append(tuple(where))
    return values.at[spots[0]].set(smallest).at[spots[1]].set(top_value)


def block_levels(stream_key, dims, pieces, least, high):
    def one(position, parts):
        heights = jax.random.uniform(jax.random.fold_in(jax.random.fold_in(stream_key, 6), position), (parts,), jnp.float32, least / len(pieces), high / len(pieces))
        return jnp.repeat(jnp.exp(heights), dims[position] // parts).reshape((-1,) + (1,) * (len(dims) - position - 1))

    level = one(*pieces[0])
    for cut in pieces[1:]:
        level = level * one(*cut)
    return level


def normal_values(rng, dims, scale, limit, pieces=(), dtype=jnp.bfloat16):
    values = scale * jax.random.normal(rng, dims, jnp.float32)
    if pieces:
        values = values * block_levels(rng, dims, pieces, -0.22, 0.18)
    return jnp.clip(values, -limit, limit).astype(dtype)


def setup_inputs(seed: int = 0) -> dict:
    key_list = jax.random.split(jax.random.key(seed), 17)
    node_input = normal_values(key_list[0], (NODES0, C), 1.0, 6.0, ((0, 64),))
    geometry = draw_geometry(jax.random.fold_in(key_list[16], 71), 0)
    counts = draw_counts(jax.random.fold_in(key_list[16], 71), 0)
    parent_mid = with_ends(jax.random.randint(key_list[3], (NODES0,), 0, N1), jax.random.fold_in(key_list[3], 1), 0, N1 - 1).astype(jnp.int32)
    parent_top = with_ends(jax.random.randint(key_list[4], (NODES1,), 0, N2), jax.random.fold_in(key_list[4], 1), 0, N2 - 1).astype(jnp.int32)
    neighbours_fine = with_ends(jax.random.randint(key_list[5], (NODES0, DEG), 0, N0), jax.random.fold_in(key_list[5], 1), 0, N0 - 1).astype(jnp.int32)
    neighbours_mid = with_ends(jax.random.randint(key_list[6], (NODES1, DEG), 0, N1), jax.random.fold_in(key_list[6], 1), 0, N1 - 1).astype(jnp.int32)
    neighbours_top = with_ends(jax.random.randint(key_list[7], (NODES2, DEG), 0, N2), jax.random.fold_in(key_list[7], 1), 0, N2 - 1).astype(jnp.int32)
    w_first = jnp.clip(jax.random.uniform(key_list[8], (LAYERS, EDGE_IN, HID), jnp.float32, -3.0, 3.0) * block_levels(key_list[8], (LAYERS, EDGE_IN, HID), ((2, 2),), -0.4, 0.0), -3.0, 3.0).astype(jnp.bfloat16)
    b_first = jnp.clip(jax.random.uniform(key_list[9], (LAYERS, HID), jnp.float32, -3.0, 3.0) * block_levels(key_list[9], (LAYERS, HID), ((1, 2),), -0.4, 0.0), -3.0, 3.0).astype(jnp.bfloat16)
    w_second = normal_values(key_list[10], (LAYERS, HID, HID), HID ** -0.5, 0.375, ((1, 2),))
    b_second = normal_values(key_list[11], (LAYERS, HID), 0.5, 3.0)
    w_kernel = normal_values(key_list[12], (LAYERS, HID, KCOLS), (HID * C) ** -0.5, 0.046875, ((2, 2),))
    b_kernel = normal_values(key_list[13], (LAYERS, KCOLS), 0.06, 0.359375, ((1, 2),))
    w_self = normal_values(key_list[14], (LAYERS, C, C), C ** -0.5, 0.75)
    cotangent = normal_values(key_list[15], (NODES0, C), 1.0, 6.0, ((0, 64),))
    return {"node_input": node_input, "geometry": geometry, "counts": counts, "parent_mid": parent_mid, "parent_top": parent_top, "neighbours_fine": neighbours_fine, "neighbours_mid": neighbours_mid, "neighbours_top": neighbours_top, "w_first": w_first, "b_first": b_first, "w_second": w_second, "b_second": b_second, "w_kernel": w_kernel, "b_kernel": b_kernel, "w_self": w_self, "cotangent": cotangent}


@jax.custom_vjp
def low(v):
    return lax.optimization_barrier(v.astype(jnp.bfloat16)).astype(jnp.float32)

@jax.custom_vjp
def low_back(v):
    return v

def low_keep(v):
    return (low(v), None)

def low_pass(kept, grad):
    return (grad,)

def back_keep(v):
    return (v, None)

def back_low(kept, grad):
    return (low(grad),)
low.defvjp(low_keep, low_pass)
low_back.defvjp(back_keep, back_low)

def gelu_fn(value):
    return jax.nn.gelu(value, approximate=True)

def matmul(left, right):
    return jnp.dot(left, right, precision=lax.Precision.HIGHEST, preferred_element_type=jnp.float32)

def restrict(values, live, parent, children, segments):
    summed = jax.ops.segment_sum(values * live[:, None], parent, num_segments=segments)
    return summed / jnp.maximum(children, 1.0)[:, None]

def kernel_apply(values, coords, neighbours, live, params):
    first, bias_one, second, bias_two, third, bias_three = params
    rows, degree = neighbours.shape
    flat_index = neighbours.reshape(-1)
    owner = jnp.repeat(jnp.arange(rows), degree)
    masked = live[:, None] * live[neighbours]
    weight = (masked / jnp.maximum(lax.optimization_barrier(jnp.sum(masked, axis=1, keepdims=True)), 1.0)).reshape(-1)
    edge = low(jnp.concatenate([coords[owner], coords[flat_index]], axis=1))
    pre_one = low_back(matmul(edge, first) + bias_one)
    hidden_one = low(gelu_fn(pre_one))
    pre_two = low_back(matmul(hidden_one, second) + bias_two)
    hidden_two = low(gelu_fn(pre_two))
    kernels = low(low_back(matmul(hidden_two, third) + bias_three)).reshape(rows * degree, C, C)
    sources = low_back(low(values))[flat_index]
    messages = jnp.einsum('eio,ei->eo', kernels, sources, precision=lax.Precision.HIGHEST)
    summed = lax.optimization_barrier(jnp.sum((messages * weight[:, None]).reshape(rows, degree, C), axis=1))
    return low_back(summed)

def graph_pass(feature, coords, count, parent_one, parent_two, near_fine, near_mid, near_top, weights):
    live_fine = (jnp.arange(N0) < count).astype(jnp.float32)
    child_mid = jax.ops.segment_sum(live_fine, parent_one, num_segments=N1)
    live_mid = (child_mid > 0.5).astype(jnp.float32)
    child_top = jax.ops.segment_sum(live_mid, parent_two, num_segments=N2)
    live_top = (child_top > 0.5).astype(jnp.float32)
    coords_mid = restrict(coords, live_fine, parent_one, child_mid, N1)
    coords_top = restrict(coords_mid, live_mid, parent_two, child_top, N2)
    state = feature
    for layer in range(LAYERS):
        params = tuple((weight_set[layer] for weight_set in weights[:6]))
        self_weight = weights[6][layer]
        values_mid = restrict(state, live_fine, parent_one, child_mid, N1)
        values_top = restrict(values_mid, live_mid, parent_two, child_top, N2)
        total_fine = kernel_apply(state, coords, near_fine, live_fine, params)
        total_mid = kernel_apply(values_mid, coords_mid, near_mid, live_mid, params)
        total_top = kernel_apply(values_top, coords_top, near_top, live_top, params)
        upward_mid = total_mid + total_top[parent_two]
        upward_fine = total_fine + upward_mid[parent_one]
        state = gelu_fn(matmul(state, self_weight) + upward_fine) * live_fine[:, None]
        if layer + 1 < LAYERS:
            state = low(state)
    return state

def reference(node_input, geometry, counts, parent_mid, parent_top, neighbours_fine, neighbours_mid, neighbours_top, w_first, b_first, w_second, b_second, w_kernel, b_kernel, w_self, cotangent):
    graph_data = (geometry.reshape(GRAPHS, N0, 3), counts, parent_mid.reshape(GRAPHS, N0), parent_top.reshape(GRAPHS, N1), neighbours_fine.reshape(GRAPHS, N0, DEG), neighbours_mid.reshape(GRAPHS, N1, DEG), neighbours_top.reshape(GRAPHS, N2, DEG))

    def forward(feature, first, bias_one, second, bias_two, third, bias_three, self_weight):
        weights = (first, bias_one, second, bias_two, third, bias_three, self_weight)

        def one_graph(item):
            return jax.checkpoint(graph_pass)(item[0], item[1], item[2], item[3], item[4], item[5], item[6], item[7], weights)
        result = lax.map(one_graph, (feature.reshape(GRAPHS, N0, C),) + graph_data)
        return result.reshape(GRAPHS * N0, C)
    primals = (node_input.astype(jnp.float32), w_first.astype(jnp.float32), b_first.astype(jnp.float32), w_second.astype(jnp.float32), b_second.astype(jnp.float32), w_kernel.astype(jnp.float32), b_kernel.astype(jnp.float32), w_self.astype(jnp.float32))
    result, pullback = jax.vjp(forward, *primals)
    grads = pullback(cotangent.astype(jnp.float32))
    return (result.astype(jnp.bfloat16), grads[0], grads[1], grads[2], grads[3], grads[4], grads[5], grads[6], grads[7])
```

```python
import functools

import jax
import jax.numpy as jnp
from jax import lax
from jax.experimental import pallas as pl
from jax.experimental.pallas import tpu as pltpu
from jax.sharding import Mesh, PartitionSpec as P

C = 64
HALF = 32
HID = 256
N0, N1, N2 = 256, 64, 16
DEG = 8
E0, E1, E2 = N0 * DEG, N1 * DEG, N2 * DEG
EDGES = 2816
TILE = 256
TILES = EDGES // TILE
AUG = HID + 16
BF = jnp.bfloat16
F32 = jnp.float32
VMEM_BYTES = 48 * 1024 * 1024
ROW_AXES = ("yl", "z", "x")
DP_AXES = ROW_AXES + ("core",)


def mm(left, right, contract=(1, 0)):
    return lax.dot_general(
        left, right, (((contract[0],), (contract[1],)), ((), ())), preferred_element_type=F32
    )


def pieces(value, count):
    parts = []
    for _ in range(count):
        part = value.astype(BF)
        parts.append(part)
        value = value - part.astype(F32)
    return parts


def mm_hot(value, hot, contract, count=2):
    rows = value.shape[0]
    product = mm(jnp.concatenate(pieces(value, count), axis=0), hot, contract)
    total = product[:rows]
    for index in range(1, count):
        total = total + product[index * rows : (index + 1) * rows]
    return total


def hot(rows, index):
    lanes = index.shape[1]
    match = lax.broadcasted_iota(jnp.int32, (rows, lanes), 0) == index
    return jnp.where(match, 1.0, 0.0).astype(BF)


def owner_hot(rows, lanes):
    index = lax.broadcasted_iota(jnp.int32, (rows, lanes), 1) & (rows - 1)
    match = lax.broadcasted_iota(jnp.int32, (rows, lanes), 0) == index
    return jnp.where(match, 1.0, 0.0).astype(BF)


def gelu_both(value):
    square = value * value
    inner = value * (0.7978845608028654 + 0.035677408136300125 * square)
    tanh = jnp.tanh(inner)
    half = 0.5 * (1.0 + tanh)
    slope = half + (0.5 * value) * (1.0 - tanh * tanh) * (
        0.7978845608028654 + 0.10703222440890037 * square
    )
    return value * half, slope


def prep_kernel(
    count_ref, geometry_ref, pm_ref, pt_ref, index_ref, node_ref, cot_ref, wk_ref,
    edge_ref, weight_ref, rows_ref, h_ref, cot_out_ref, wkt_ref,
):
    live = jnp.where(
        lax.broadcasted_iota(jnp.int32, (1, N0), 1) < count_ref[0], 1.0, 0.0
    ).astype(F32)
    parent = hot(N1, pm_ref[...])
    parent_top = hot(N2, pt_ref[...])
    live8 = jnp.broadcast_to(live, (16, N0))
    child_mid = mm(live8.astype(BF), parent, (1, 1))
    live_mid = jnp.where(child_mid > 0.5, 1.0, 0.0)
    child_top = mm(live_mid.astype(BF), parent_top, (1, 1))
    live_top = jnp.where(child_top > 0.5, 1.0, 0.0)
    child_mid = jnp.maximum(child_mid, 1.0)
    child_top = jnp.maximum(child_top, 1.0)
    rows_ref[...] = jnp.zeros_like(rows_ref)
    rows_ref[0:1, :] = live
    rows_ref[1:2, 0:N1] = child_mid[0:1]
    rows_ref[2:3, 0:N1] = live_mid[0:1]
    rows_ref[3:4, 0:N2] = child_top[0:1]
    select = jnp.where(
        lax.broadcasted_iota(jnp.int32, (16, 3), 0) == lax.broadcasted_iota(jnp.int32, (16, 3), 1),
        1.0,
        0.0,
    )
    coords = lax.dot_general(
        select,
        geometry_ref[...],
        (((1,), (1,)), ((), ())),
        precision=lax.Precision.HIGHEST,
        preferred_element_type=F32,
    )
    coords_mid = mm_hot(coords * live, parent, (1, 1), 3) / child_mid
    coords_top = mm_hot(coords_mid * live_mid, parent_top, (1, 1), 3) / child_top
    lane_row = lax.broadcasted_iota(jnp.int32, (16, 1), 0)

    def with_live(values, live_row):
        return jnp.where(lane_row == 3, live_row, values).astype(BF)

    fine_rows = with_live(coords, live)
    mid_rows = with_live(coords_mid, live_mid[0:1])
    top_rows = with_live(coords_top, live_top[0:1])

    def edges(own, near):
        low = jnp.where(lane_row < 3, own, 0.0)
        high = pltpu.roll(jnp.where(lane_row < 3, near, 0.0), 3, 0)
        return jnp.where(lane_row == 6, 1.0, low + high).astype(BF)

    fine = fine_rows.astype(F32)
    masks = []
    for slot in range(DEG):
        lanes = slice(slot * N0, (slot + 1) * N0)
        near = mm(fine_rows, hot(N0, index_ref[:, lanes]))
        edge_ref[:, lanes] = edges(fine, near)
        masks.append(live * near[3:4])
    total = masks[0]
    for mask in masks[1:]:
        total = total + mask
    total = jnp.maximum(total, 1.0)
    for slot in range(DEG):
        weight_ref[:, slot * N0 : (slot + 1) * N0] = masks[slot] / total

    def small_level(values, rows, start, lanes):
        own = mm(values, owner_hot(rows, lanes))
        near = mm(values, hot(rows, index_ref[:, start : start + lanes]))
        edge_ref[:, start : start + lanes] = edges(own, near)
        mask = own * near
        fold = jnp.where(
            (lax.broadcasted_iota(jnp.int32, (lanes, lanes), 0) & (rows - 1))
            == (lax.broadcasted_iota(jnp.int32, (lanes, lanes), 1) & (rows - 1)),
            1.0,
            0.0,
        ).astype(BF)
        total = jnp.maximum(mm(mask.astype(BF), fold), 1.0)
        weight_ref[:, start : start + lanes] = mask[3:4] / total[3:4]

    small_level(mid_rows, N1, E0, E1)
    small_level(top_rows, N2, E0 + E1, E2)
    rest = E0 + E1 + E2
    edge_ref[:, rest:] = jnp.zeros((16, EDGES - rest), BF)
    weight_ref[:, rest:] = jnp.zeros((1, EDGES - rest), F32)
    h_ref[...] = node_ref[...].astype(F32).T.astype(BF)
    cot_out_ref[...] = cot_ref[...].astype(F32).T
    for layer in range(2):
        for part in range(8):
            wkt_ref[layer, part * 256 : (part + 1) * 256, :] = wk_ref[
                layer, :, part * 256 : (part + 1) * 256
            ].T


def mlp_kernel(edge_ref, first_ref, second_ref, bias_ref, h1_ref, h2_ref, s1_ref, s2_ref):
    first = first_ref[...].astype(F32).T.astype(BF)
    second = second_ref[...].T
    bias = bias_ref[...]
    extra = jnp.where(lax.broadcasted_iota(jnp.int32, (16, TILE), 0) == 0, 1.0, 0.0).astype(BF)

    def body(tile, carry):
        lanes = pl.ds(pl.multiple_of(tile * TILE, TILE), TILE)
        value, slope = gelu_both(mm(first, edge_ref[:, lanes]))
        hidden = value.astype(BF)
        h1_ref[0:HID, lanes] = hidden
        h1_ref[HID:AUG, lanes] = extra
        s1_ref[:, lanes] = slope.astype(BF)
        value, slope = gelu_both(mm(second, hidden) + bias)
        h2_ref[0:HID, lanes] = value.astype(BF)
        h2_ref[HID:AUG, lanes] = extra
        s2_ref[:, lanes] = slope.astype(BF)
        return carry

    lax.fori_loop(0, TILES, body, 0)


def forward_pass(
    state, half_ref, pm_ref, pt_ref, index_ref, rows_ref, weight_ref, h2_ref, wkt_ref, bk_ref,
    up_ref, vw_ref, vals, msg,
):
    live = rows_ref[0:1, :]
    child_mid = rows_ref[1:2, 0:N1]
    live_mid = rows_ref[2:3, 0:N1]
    child_top = rows_ref[3:4, 0:N2]
    parent = hot(N1, pm_ref[...])
    parent_top = hot(N2, pt_ref[...])
    start = pl.multiple_of(half_ref[0] * HALF, HALF)
    mid = mm((state.astype(F32) * live).astype(BF), parent, (1, 1)) / child_mid
    top = mm_hot(mid * live_mid, parent_top, (1, 1), 3) / child_top
    vals[:, 0:N0] = state.astype(F32)
    vals[:, N0 : N0 + N1] = mid
    vals[:, N0 + 128 : N0 + 128 + N2] = top
    fine_half = vals[pl.ds(start, HALF), 0:N0].astype(BF)
    mid_half = vals[pl.ds(start, HALF), N0 : N0 + N1].astype(BF)
    top_half = vals[pl.ds(start, HALF), N0 + 128 : N0 + 128 + N2].astype(BF)
    for slot in range(DEG):
        lanes = slice(slot * N0, (slot + 1) * N0)
        vw_ref[:, lanes] = mm(fine_half, hot(N0, index_ref[:, lanes])) * weight_ref[:, lanes]
    lanes = slice(E0, E0 + E1)
    vw_ref[:, lanes] = mm(mid_half, hot(N1, index_ref[:, lanes])) * weight_ref[:, lanes]
    lanes = slice(E0 + E1, E0 + E1 + E2)
    vw_ref[:, lanes] = mm(top_half, hot(N2, index_ref[:, lanes])) * weight_ref[:, lanes]
    vw_ref[:, E0 + E1 + E2 :] = jnp.zeros((HALF, EDGES - E0 - E1 - E2), F32)
    bias = bk_ref[...]
    bias = jnp.concatenate([bias, bias], axis=1)

    def body(tile, carry):
        lanes = pl.ds(pl.multiple_of(tile * TILE, TILE), TILE)
        hidden = h2_ref[0:HID, lanes]
        source = vw_ref[:, lanes]
        total = mm(bias, jnp.concatenate(pieces(source, 2), axis=0))
        for part in range(4):
            kernels = mm(wkt_ref[part * 512 : (part + 1) * 512, :], hidden)
            for channel in range(8):
                row = part * 8 + channel
                total = total + (
                    kernels[channel * C : (channel + 1) * C] * source[row : row + 1, :]
                )
        msg[:, lanes] = total
        return carry

    lax.fori_loop(0, TILES, body, 0)
    total_fine = msg[:, 0:N0]
    for slot in range(1, DEG):
        total_fine = total_fine + msg[:, slot * N0 : (slot + 1) * N0]
    total_mid = mm_hot(msg[:, E0 : E0 + E1], owner_hot(N1, E1), (1, 1))
    total_top = mm_hot(msg[:, E0 + E1 : E0 + E1 + E2], owner_hot(N2, E2), (1, 1))
    up_mid = total_mid + mm_hot(total_top, parent_top, (1, 0))
    up_ref[...] = total_fine + mm_hot(up_mid, parent, (1, 0))


def forward_first_kernel(h_ref, *refs):
    forward_pass(h_ref[...], *refs)


def forward_next_kernel(h_ref, self_ref, up_own_ref, up_far_ref, rows_ref, *refs):
    half_ref, pm_ref, pt_ref, index_ref, weight_ref, h2_ref, wkt_ref, bk_ref = refs[:8]
    pre_ref, state_ref, up_ref, vw_ref, vals, msg = refs[8:]
    pre = mm(self_ref[...].astype(F32).T.astype(BF), h_ref[...]) + up_own_ref[...] + up_far_ref[...]
    pre_ref[...] = pre
    value, _ = gelu_both(pre)
    state = (value * rows_ref[0:1, :]).astype(BF)
    state_ref[...] = state
    forward_pass(
        state, half_ref, pm_ref, pt_ref, index_ref, rows_ref, weight_ref, h2_ref, wkt_ref, bk_ref,
        up_ref, vw_ref, vals, msg,
    )


def node_backward(
    h, pre, grad, half_ref, pm_ref, pt_ref, index_ref, rows_ref, weight_ref, self_ref, h2_ref,
    wkt_ref, bkn_ref, grad_self_ref, g_ref, dx_ref, dvw,
):
    live = rows_ref[0:1, :]
    child_mid = rows_ref[1:2, 0:N1]
    live_mid = rows_ref[2:3, 0:N1]
    child_top = rows_ref[3:4, 0:N2]
    parent = hot(N1, pm_ref[...])
    parent_top = hot(N2, pt_ref[...])
    start = pl.multiple_of(half_ref[0] * HALF, HALF)
    _, slope = gelu_both(pre)
    grad_pre = slope * (live * grad)
    high, low = pieces(grad_pre, 2)
    grad_self_ref[...] = mm(h, high, (1, 1)) + mm(h, low, (1, 1))
    self_half = self_ref[pl.ds(start, HALF), :]
    self_in = mm(self_half, high) + mm(self_half, low)
    up_mid = mm_hot(grad_pre, parent, (1, 1), 3)
    up_top = mm_hot(up_mid, parent_top, (1, 1), 3)
    g_ref[:, 0:N0] = grad_pre.astype(BF)
    g_ref[:, N0 : N0 + E1] = mm(up_mid.astype(BF), owner_hot(N1, E1)).astype(BF)
    g_ref[:, N0 + E1 : N0 + E1 + E2] = mm(up_top.astype(BF), owner_hot(N2, E2)).astype(BF)
    g_ref[:, N0 + E1 + E2 :] = jnp.zeros((C, 4 * TILE - N0 - E1 - E2), BF)
    bias = bkn_ref[...]

    def body(tile, carry):
        lanes = pl.ds(pl.multiple_of(tile * TILE, TILE), TILE)
        place = jnp.maximum(tile - (DEG - 1), 0)
        grad_tile = g_ref[:, pl.ds(pl.multiple_of(place * TILE, TILE), TILE)]
        hidden = h2_ref[0:HID, lanes]
        wide = grad_tile.astype(F32)
        offset = mm(bias, grad_tile)
        weight = weight_ref[:, lanes]
        for part in range(4):
            kernels = mm(wkt_ref[part * 512 : (part + 1) * 512, :], hidden)
            product = kernels.reshape(8, C, TILE) * wide[None]
            rows = jnp.sum(product, axis=1) + offset[part * 8 : (part + 1) * 8]
            dvw[part * 8 : (part + 1) * 8, lanes] = rows * weight
        return carry

    lax.fori_loop(0, TILES, body, 0)
    fine = jnp.zeros((HALF, N0), F32)
    for slot in range(DEG):
        lanes = slice(slot * N0, (slot + 1) * N0)
        fine = fine + mm_hot(dvw[:, lanes], hot(N0, index_ref[:, lanes]), (1, 1))
    lanes = slice(E0, E0 + E1)
    mid = mm_hot(dvw[:, lanes], hot(N1, index_ref[:, lanes]), (1, 1))
    lanes = slice(E0 + E1, E0 + E1 + E2)
    top = mm_hot(dvw[:, lanes], hot(N2, index_ref[:, lanes]), (1, 1))

    def rounded(value):
        return value.astype(BF).astype(F32)

    grad_mid = rounded(mid) + mm_hot(rounded(top) / child_top, parent_top, (1, 0), 3) * live_mid
    dx_ref[...] = (
        self_in + rounded(fine) + mm_hot(grad_mid / child_mid, parent, (1, 0), 3) * live
    )


def backward_last_kernel(h_ref, up_own_ref, up_far_ref, cot_ref, rows_ref, self_ref, *refs):
    half_ref, pm_ref, pt_ref, index_ref, weight_ref, h2_ref, wkt_ref, bkn_ref = refs[:8]
    out_ref, grad_self_ref, g_ref, dx_ref, dvw = refs[8:]
    pre = mm(self_ref[...].astype(F32).T.astype(BF), h_ref[...]) + up_own_ref[...] + up_far_ref[...]
    value, _ = gelu_both(pre)
    out_ref[...] = (value * rows_ref[0:1, :]).T.astype(BF)
    node_backward(
        h_ref[...], pre, cot_ref[...], half_ref, pm_ref, pt_ref, index_ref, rows_ref, weight_ref,
        self_ref, h2_ref, wkt_ref, bkn_ref, grad_self_ref, g_ref, dx_ref, dvw,
    )


def backward_first_kernel(h_ref, pre_ref, dx_own_ref, dx_far_ref, rows_ref, self_ref, *refs):
    half_ref, pm_ref, pt_ref, index_ref, weight_ref, h2_ref, wkt_ref, bkn_ref = refs[:8]
    grad_self_ref, g_ref, dx_ref, dvw, grad = refs[8:]
    start = pl.multiple_of(half_ref[0] * HALF, HALF)
    grad[pl.ds(start, HALF), :] = dx_own_ref[...]
    grad[pl.ds(HALF - start, HALF), :] = dx_far_ref[...]
    node_backward(
        h_ref[...], pre_ref[...], grad[...], half_ref, pm_ref, pt_ref, index_ref, rows_ref,
        weight_ref, self_ref, h2_ref, wkt_ref, bkn_ref, grad_self_ref, g_ref, dx_ref, dvw,
    )


def edge_backward_kernel(
    core_ref, g_ref, vw_ref, wk_ref, h2_ref, h1_ref, s1_ref, s2_ref, second_ref, edge_ref,
    mine_ref, other_ref, dbk_ref, dw2_ref, dw1_ref, gk, g2, g1,
):
    second = second_ref[...]

    def body(tile, carry):
        lanes = pl.ds(pl.multiple_of(tile * TILE, TILE), TILE)
        place = jnp.maximum(tile - (DEG - 1), 0)
        grad_tile = g_ref[:, pl.ds(pl.multiple_of(place * TILE, TILE), TILE)].astype(F32)
        source = vw_ref[:, lanes]
        for row in range(HALF):
            gk[row * C : (row + 1) * C, lanes] = (grad_tile * source[row : row + 1, :]).astype(BF)
        hidden_grad = mm(wk_ref[...], gk[:, lanes])
        two = (s2_ref[:, lanes].astype(F32) * hidden_grad).astype(BF)
        g2[:, lanes] = two
        g1[:, lanes] = (s1_ref[:, lanes].astype(F32) * mm(second, two)).astype(BF)
        return carry

    lax.fori_loop(0, TILES, body, 0)
    dw2_ref[...] = mm(h1_ref[...], g2[...], (1, 1))
    dw1_ref[...] = mm(edge_ref[...], g1[...], (1, 1))
    mine = core_ref[0]

    def columns(block, carry):
        rows = pl.ds(pl.multiple_of(block * 256, 256), 256)
        product = mm(h2_ref[...], gk[rows, :], (1, 1))
        dbk_ref[:, rows] = product[HID : HID + 8]
        for side in range(2):
            for part in range(2):
                value = product[side * 128 + part * 64 : side * 128 + (part + 1) * 64]
                for half in range(2):
                    piece = value[:, half * 128 : (half + 1) * 128]

                    @pl.when(mine == side)
                    def _():
                        mine_ref[part, block * 2 + half] = piece

                    @pl.when(mine != side)
                    def _():
                        other_ref[part, block * 2 + half] = piece.astype(BF)

        return carry

    lax.fori_loop(0, 8, columns, 0)


def vmem_spec():
    return pl.BlockSpec(memory_space=pltpu.VMEM)


def smem_spec():
    return pl.BlockSpec(memory_space=pltpu.SMEM)


def call(kernel, outs, args, scalars=(), scratch=(), flops=0):
    return pl.pallas_call(
        kernel,
        out_shape=[jax.ShapeDtypeStruct(shape, dtype) for shape, dtype in outs],
        in_specs=[
            smem_spec() if index in scalars else vmem_spec() for index in range(len(args))
        ],
        out_specs=[vmem_spec() for _ in outs],
        scratch_shapes=[pltpu.VMEM(shape, dtype) for shape, dtype in scratch],
        compiler_params=pltpu.CompilerParams(vmem_limit_bytes=VMEM_BYTES),
        cost_estimate=pl.CostEstimate(flops=flops, bytes_accessed=1 << 20, transcendentals=0),
    )(*args)


def swap(value, axis):
    return lax.ppermute(value, axis, [(0, 1), (1, 0)])


def sum_over_dp(mine, other):
    blocks, rows, lanes = mine.shape
    half = (mine + swap(other, "core").astype(F32)).astype(BF)
    parts = lax.all_to_all(half, ROW_AXES, 0, 0, tiled=True)
    total = jnp.sum(parts.astype(F32), axis=0).astype(BF)
    spread = jnp.broadcast_to(total[None], (blocks, rows, lanes))
    own = lax.all_to_all(spread, ROW_AXES, 0, 0, tiled=True)
    far = swap(own, "core")
    core = lax.axis_index("core")
    return jnp.where(core == 0, own, far), jnp.where(core == 0, far, own)


def per_device(
    node_input, geometry, counts, parent_mid, parent_top, neighbours_fine, neighbours_mid,
    neighbours_top, w_first, b_first, w_second, b_second, w_kernel, b_kernel, w_self, cotangent,
):
    layers = w_self.shape[0]
    half = lax.axis_index("tensor").astype(jnp.int32).reshape(1)
    core = lax.axis_index("core").astype(jnp.int32).reshape(1)
    near = jnp.concatenate(
        [neighbours_fine.T.reshape(1, E0), neighbours_mid.T.reshape(1, E1),
         neighbours_top.T.reshape(1, E2), jnp.zeros((1, EDGES - E0 - E1 - E2), jnp.int32)],
        axis=1,
    )
    pm = parent_mid.reshape(1, N0)
    pt = parent_top.reshape(1, N1)

    first_rows = jnp.concatenate(
        [w_first, b_first[:, None, :], jnp.zeros((layers, 9, 128), BF)], axis=1
    )
    packed = jnp.concatenate(
        [w_second[0], w_second[1], first_rows.transpose(1, 0, 2).reshape(16, 256)], axis=0
    )
    far = swap(packed, "tensor")
    second = [
        jnp.concatenate([w_second[l], far[l * 128 : (l + 1) * 128]], axis=0) for l in range(layers)
    ]
    far_first = far[256:].reshape(16, layers, 128)
    first = [
        jnp.concatenate([first_rows[l], far_first[:, l]], axis=1) for l in range(layers)
    ]

    edge, weight, rows, h0, cot, wkt = call(
        prep_kernel,
        [((16, EDGES), BF), ((1, EDGES), F32), ((8, N0), F32), ((C, N0), BF), ((C, N0), F32),
         ((layers, HALF * C, HID), BF)],
        [counts, geometry, pm, pt, near, node_input, cotangent, w_kernel],
        scalars=(0,),
    )
    mlp = [
        call(
            mlp_kernel,
            [((AUG, EDGES), BF), ((AUG, EDGES), BF), ((HID, EDGES), BF), ((HID, EDGES), BF)],
            [edge, first[l], second[l], b_second[l].astype(F32).reshape(HID, 1)],
        )
        for l in range(layers)
    ]
    bias_rows = b_kernel.reshape(layers, HALF, C)
    bias_cols = bias_rows.transpose(0, 2, 1)
    pass_scratch = [((C, N0 + 256), F32), ((C, EDGES), F32)]

    up0, vw0 = call(
        forward_first_kernel,
        [((C, N0), F32), ((HALF, EDGES), F32)],
        [h0, half, pm, pt, near, rows, weight, mlp[0][1], wkt[0], bias_cols[0]],
        scalars=(1,),
        scratch=pass_scratch,
    )
    up0_far = swap(up0, "tensor")
    pre0, h1, up1, vw1 = call(
        forward_next_kernel,
        [((C, N0), F32), ((C, N0), BF), ((C, N0), F32), ((HALF, EDGES), F32)],
        [h0, w_self[0], up0, up0_far, rows, half, pm, pt, near, weight, mlp[1][1], wkt[1],
         bias_cols[1]],
        scalars=(5,),
        scratch=pass_scratch,
    )
    up1_far = swap(up1, "tensor")
    out, grad_self1, g1, dx1 = call(
        backward_last_kernel,
        [((N0, C), BF), ((C, C), F32), ((C, 4 * TILE), BF), ((HALF, N0), F32)],
        [h1, up1, up1_far, cot, rows, w_self[1], half, pm, pt, near, weight, mlp[1][1], wkt[1],
         bias_rows[1]],
        scalars=(6,),
        scratch=[((HALF, EDGES), F32)],
    )
    dx1_far = swap(dx1, "tensor")

    def edge_backward(layer, g, vw):
        h1a, h2a, s1, s2 = mlp[layer]
        return call(
            edge_backward_kernel,
            [((2, 16, 64, 128), F32), ((2, 16, 64, 128), BF), ((8, HALF * C), F32),
             ((AUG, HID), F32), ((16, HID), F32)],
            [core, g, vw, w_kernel[layer], h2a, h1a, s1, s2, second[layer], edge],
            scalars=(0,),
            scratch=[((HALF * C, EDGES), BF), ((HID, EDGES), BF), ((HID, EDGES), BF)],
        )

    grads1 = edge_backward(1, g1, vw1)
    grad_self0, g0, dx0 = call(
        backward_first_kernel,
        [((C, C), F32), ((C, 4 * TILE), BF), ((HALF, N0), F32)],
        [h0, pre0, dx1, dx1_far, rows, w_self[0], half, pm, pt, near, weight, mlp[0][1], wkt[0],
         bias_rows[0]],
        scalars=(6,),
        scratch=[((HALF, EDGES), F32), ((C, N0), F32)],
    )
    dx0_far = swap(dx0, "tensor")
    grads0 = edge_backward(0, g0, vw0)
    first_half = lax.axis_index("tensor") == 0
    input_grad = jnp.where(
        first_half,
        jnp.concatenate([dx0, dx0_far], axis=0),
        jnp.concatenate([dx0_far, dx0], axis=0),
    ).T

    def small(grads, grad_self):
        _, _, dbk, dw2, dw1 = grads
        own = jnp.concatenate(
            [dw2[0:128].reshape(-1), dw1[0:7, 0:128].reshape(-1), dw2[256]]
        )
        away = jnp.concatenate(
            [dw2[128:256].reshape(-1), dw1[0:7, 128:256].reshape(-1), dw2[256]]
        )
        both = own + swap(away.astype(BF), "tensor").astype(F32)
        flat = jnp.concatenate(
            [both, dbk[0], grad_self.reshape(-1), jnp.zeros((40960 - 40064,), F32)]
        )
        return flat.reshape(2, 32, 5, 128)

    smalls = jnp.concatenate(
        [small(grads0, grad_self0), small(grads1, grad_self1), jnp.zeros((2, 32, 6, 128), F32)],
        axis=2,
    )
    own_small = jnp.where(core[0] == 0, smalls[0], smalls[1])
    other_small = jnp.where(core[0] == 0, smalls[1], smalls[0]).astype(BF)
    mine = jnp.concatenate(
        [grads0[0].reshape(32, 64, 128), grads1[0].reshape(32, 64, 128), own_small], axis=1
    )
    other = jnp.concatenate(
        [grads0[1].reshape(32, 64, 128), grads1[1].reshape(32, 64, 128), other_small], axis=1
    )
    low, high = sum_over_dp(mine, other)

    def big(layer):
        blocks = jnp.stack([low, high])[:, :, layer * 64 : (layer + 1) * 64]
        return blocks.reshape(4, 16, 64, 128).transpose(0, 2, 1, 3).reshape(HID, HALF * C)

    grad_kernel = jnp.stack([big(l) for l in range(layers)]).astype(F32)
    flat = jnp.stack(
        [
            jnp.concatenate([low[:, 128 + 5 * l : 133 + 5 * l], high[:, 128 + 5 * l : 133 + 5 * l]])
            .reshape(-1)
            .astype(F32)
            for l in range(layers)
        ]
    )
    grad_second = flat[:, 0:32768].reshape(layers, 128, 256)
    first_all = flat[:, 32768:33664].reshape(layers, 7, 128)
    grad_b_second = flat[:, 33664:33920]
    grad_b_kernel = flat[:, 33920:35968]
    grad_self = flat[:, 35968:40064].reshape(layers, C, C)
    return (
        out, input_grad, first_all[:, 0:6], first_all[:, 6], grad_second, grad_b_second,
        grad_kernel, grad_b_kernel, grad_self,
    )


def solution(mesh):
    fine = Mesh(mesh.devices.reshape(2, 4, 4, 2, 2), DP_AXES + ("tensor",))
    dp = DP_AXES
    placed = (
        P(dp, None), P(dp, None), P(dp), P(dp), P(dp), P(dp, None), P(dp, None), P(dp, None),
        P(None, None, "tensor"), P(None, "tensor"), P(None, "tensor", None), P(),
        P(None, None, "tensor"), P(None, "tensor"), P(), P(dp, None),
    )
    return jax.shard_map(
        per_device,
        mesh=fine,
        in_specs=placed,
        out_specs=(
            P(dp, None), P(dp, None), P(None, None, "tensor"), P(None, "tensor"),
            P(None, "tensor", None), P(), P(None, None, "tensor"), P(None, "tensor"), P(),
        ),
        check_vma=False,
    )
```

```python
import functools

import jax
import jax.numpy as jnp
from jax import lax
from jax.experimental import pallas as pl
from jax.experimental.pallas import tpu as pltpu
from jax.sharding import Mesh, PartitionSpec as P

C = 64
HALF = 32
HID = 256
N0, N1, N2 = 256, 64, 16
DEG = 8
E0, E1, E2 = N0 * DEG, N1 * DEG, N2 * DEG
EDGES = 2816
TILES = ((0, 1024), (1024, 1024), (2048, 768))
SMALL = 320
BLOCK = 160
QUARTER = HALF // 2
PACK = C + 3 * HALF
VMEM_MIB = 28
AUG = HID + 16
BF = jnp.bfloat16
F32 = jnp.float32
ROW_AXES = ("yl", "z", "x")
DP_AXES = ROW_AXES + ("core",)


def mm(left, right, contract=(1, 0)):
    return lax.dot_general(
        left, right, (((contract[0],), (contract[1],)), ((), ())), preferred_element_type=F32
    )


def pieces(value, count):
    parts = []
    for _ in range(count):
        part = value.astype(BF)
        parts.append(part)
        value = value - part.astype(F32)
    return parts


def mm_hot(value, hot, contract, count=2):
    rows = value.shape[0]
    product = mm(jnp.concatenate(pieces(value, count), axis=0), hot, contract)
    total = product[:rows]
    for index in range(1, count):
        total = total + product[index * rows : (index + 1) * rows]
    return total


def hot(rows, index):
    lanes = index.shape[1]
    match = lax.broadcasted_iota(jnp.int32, (rows, lanes), 0) == index
    return jnp.where(match, 1.0, 0.0).astype(BF)


def owner_hot(rows, lanes):
    index = lax.broadcasted_iota(jnp.int32, (rows, lanes), 1) & (rows - 1)
    match = lax.broadcasted_iota(jnp.int32, (rows, lanes), 0) == index
    return jnp.where(match, 1.0, 0.0).astype(BF)


def gelu(value):
    inner = value * (0.7978845608028654 + 0.035677408136300125 * (value * value))
    return value * (0.5 + 0.5 * jnp.tanh(inner))


def gelu_both(value):
    square = value * value
    inner = value * (0.7978845608028654 + 0.035677408136300125 * square)
    share = 0.5 + 0.5 * jnp.tanh(inner)
    slope = share + (share * (1.0 - share)) * (
        value * (1.5957691216057308 + 0.21406444881780074 * square)
    )
    return value * share, slope


def level_rows(rows_ref):
    return (
        rows_ref[0:1, :], rows_ref[1:2, 0:N1], rows_ref[2:3, 0:N1], rows_ref[3:4, 0:N2]
    )


def gather_sources(state, half, parent, parent_top, index_ref, rows_ref, weight_ref, vw_ref, vals):
    live, child_mid, live_mid, child_top = level_rows(rows_ref)
    start = pl.multiple_of(half * HALF, HALF)
    wide = state.astype(F32)
    mid = mm((wide * live).astype(BF), parent, (1, 1)) / child_mid
    top = mm_hot(mid * live_mid, parent_top, (1, 1), 3) / child_top
    vals[:, 0:N0] = wide
    vals[:, N0 : N0 + N1] = mid
    vals[:, N0 + 128 : N0 + 128 + N2] = top
    fine_half = vals[pl.ds(start, HALF), 0:N0].astype(BF)
    mid_half = vals[pl.ds(start, HALF), N0 : N0 + N1].astype(BF)
    top_half = vals[pl.ds(start, HALF), N0 + 128 : N0 + 128 + N2].astype(BF)
    for slot in range(DEG):
        lanes = slice(slot * N0, (slot + 1) * N0)
        vw_ref[:, lanes] = mm(fine_half, hot(N0, index_ref[:, lanes])) * weight_ref[:, lanes]
    lanes = slice(E0, E0 + E1)
    vw_ref[:, lanes] = mm(mid_half, hot(N1, index_ref[:, lanes])) * weight_ref[:, lanes]
    lanes = slice(E0 + E1, E0 + E1 + E2)
    vw_ref[:, lanes] = mm(top_half, hot(N2, index_ref[:, lanes])) * weight_ref[:, lanes]
    vw_ref[:, E0 + E1 + E2 :] = jnp.zeros((HALF, EDGES - E0 - E1 - E2), F32)


def message_pass(layer, hidden, parent, parent_top, wkt_ref, bias_ref, vw_ref, up_ref, msg):
    bias = bias_ref[layer]
    bias = jnp.concatenate([bias, bias], axis=1)
    for start, width in TILES:
        lanes = slice(start, start + width)
        tile = hidden(lanes)
        source = vw_ref[:, lanes]
        total = mm(bias, jnp.concatenate(pieces(source, 2), axis=0))
        for part in range(4):
            kernels = mm(wkt_ref[layer, part * 512 : (part + 1) * 512, :], tile)
            for channel in range(8):
                row = part * 8 + channel
                total = total + (
                    kernels[channel * C : (channel + 1) * C] * source[row : row + 1, :]
                )
        msg[:, lanes] = total
    total_fine = msg[:, 0:N0]
    for slot in range(1, DEG):
        total_fine = total_fine + msg[:, slot * N0 : (slot + 1) * N0]
    total_mid = mm_hot(msg[:, E0 : E0 + E1], owner_hot(N1, E1), (1, 1))
    total_top = mm_hot(msg[:, E0 + E1 : E0 + E1 + E2], owner_hot(N2, E2), (1, 1))
    up_mid = total_mid + mm_hot(total_top, parent_top, (1, 0))
    up_ref[...] = total_fine + mm_hot(up_mid, parent, (1, 0))


def first_columns(packed_ref, layer):
    return packed_ref[HID : HID + 16, layer * 128 : (layer + 1) * 128].astype(F32).T.astype(BF)


def second_rows(packed_ref, far_ref, layer):
    rows = slice(layer * 128, (layer + 1) * 128)
    return jnp.concatenate([packed_ref[rows, :], far_ref[rows, :]], axis=0)


def ones_rows(width):
    return jnp.where(lax.broadcasted_iota(jnp.int32, (16, width), 0) == 0, 1.0, 0.0).astype(BF)


def pack_kernel(second_ref, first_ref, bias_ref, packed_ref, second, first, bias, rows, sems):
    copies = [
        pltpu.make_async_copy(source, target, sems.at[index])
        for index, (source, target) in enumerate(
            ((second_ref, second), (first_ref, first), (bias_ref, bias))
        )
    ]
    for copy in copies:
        copy.start()
    rows[...] = jnp.zeros_like(rows)
    for copy in copies:
        copy.wait()
    packed_ref[0:128, :] = second[0]
    packed_ref[128:256, :] = second[1]
    bias_rows = bias[...].astype(F32)
    for layer in range(2):
        lanes = slice(layer * 128, (layer + 1) * 128)
        for row in range(6):
            rows[row : row + 1, lanes] = first[row].astype(F32)[layer : layer + 1]
        rows[6:7, lanes] = bias_rows[layer : layer + 1]
    packed_ref[256:272, :] = rows[...].astype(BF)


def prep_kernel(
    count_ref, half_ref, packed_ref, geometry_hbm, pm_hbm, pt_hbm, near0_hbm, near1_hbm, near2_hbm,
    node_hbm, bk_hbm, bs_hbm, wk_hbm,
    edge_ref, weight_ref, index_ref, rows_ref, wkt_ref, bias_rows_ref, bias_cols_ref, bs_cols_ref,
    hown_ref, vw_ref, pm_ref, pt_ref, node_ref,
    geometry_ref, near0_ref, near1_ref, near2_ref, bk_ref, bs_ref, wk_ref, sems, vals, bias_rows,
):
    copies = [
        pltpu.make_async_copy(source, target, sems.at[index])
        for index, (source, target) in enumerate(
            (
                (geometry_hbm, geometry_ref), (pm_hbm, pm_ref), (pt_hbm, pt_ref),
                (near0_hbm, near0_ref), (near1_hbm, near1_ref), (near2_hbm, near2_ref),
                (node_hbm, node_ref), (bk_hbm, bk_ref), (bs_hbm, bs_ref), (wk_hbm, wk_ref),
            )
        )
    ]
    for copy in copies:
        copy.start()
    for copy in copies[:-1]:
        copy.wait()
    live = jnp.where(
        lax.broadcasted_iota(jnp.int32, (1, N0), 1) < count_ref[0], 1.0, 0.0
    ).astype(F32)
    parent = hot(N1, pm_ref[...])
    parent_top = hot(N2, pt_ref[...])
    live8 = jnp.broadcast_to(live, (16, N0))
    child_mid = mm(live8.astype(BF), parent, (1, 1))
    live_mid = jnp.where(child_mid > 0.5, 1.0, 0.0)
    child_top = mm(live_mid.astype(BF), parent_top, (1, 1))
    live_top = jnp.where(child_top > 0.5, 1.0, 0.0)
    child_mid = jnp.maximum(child_mid, 1.0)
    child_top = jnp.maximum(child_top, 1.0)
    rows_ref[...] = jnp.zeros_like(rows_ref)
    rows_ref[0:1, :] = live
    rows_ref[1:2, 0:N1] = child_mid[0:1]
    rows_ref[2:3, 0:N1] = live_mid[0:1]
    rows_ref[3:4, 0:N2] = child_top[0:1]
    index_ref[...] = jnp.zeros_like(index_ref)
    for slot in range(DEG):
        row = slice(slot, slot + 1)
        index_ref[:, slot * N0 : (slot + 1) * N0] = near0_ref[row, :]
        index_ref[:, E0 + slot * N1 : E0 + (slot + 1) * N1] = near1_ref[row, :]
        start = E0 + E1 + slot * N2
        index_ref[:, start : start + N2] = near2_ref[row, :]
    vals[0:16, 0:N0] = jnp.zeros((16, N0), F32)
    vals[0:3, 0:N0] = geometry_ref[...]
    coords = vals[0:16, 0:N0]
    coords_mid = mm_hot(coords * live, parent, (1, 1), 3) / child_mid
    coords_top = mm_hot(coords_mid * live_mid, parent_top, (1, 1), 3) / child_top
    lane_row = lax.broadcasted_iota(jnp.int32, (16, 1), 0)

    def with_live(values, live_row):
        return jnp.where(lane_row == 3, live_row, values).astype(BF)

    fine_rows = with_live(coords, live)
    mid_rows = with_live(coords_mid, live_mid[0:1])
    top_rows = with_live(coords_top, live_top[0:1])

    def edges(own, near):
        low = jnp.where(lane_row < 3, own, 0.0)
        high = pltpu.roll(jnp.where(lane_row < 3, near, 0.0), 3, 0)
        return jnp.where(lane_row == 6, 1.0, low + high).astype(BF)

    fine = fine_rows.astype(F32)
    masks = []
    for slot in range(DEG):
        lanes = slice(slot * N0, (slot + 1) * N0)
        near = mm(fine_rows, hot(N0, index_ref[:, lanes]))
        edge_ref[:, lanes] = edges(fine, near)
        masks.append(live * near[3:4])
    total = masks[0]
    for mask in masks[1:]:
        total = total + mask
    total = jnp.maximum(total, 1.0)
    for slot in range(DEG):
        weight_ref[:, slot * N0 : (slot + 1) * N0] = masks[slot] / total

    def small_level(values, rows, start, lanes):
        own = mm(values, owner_hot(rows, lanes))
        near = mm(values, hot(rows, index_ref[:, start : start + lanes]))
        edge_ref[:, start : start + lanes] = edges(own, near)
        mask = own * near
        fold = jnp.where(
            (lax.broadcasted_iota(jnp.int32, (lanes, lanes), 0) & (rows - 1))
            == (lax.broadcasted_iota(jnp.int32, (lanes, lanes), 1) & (rows - 1)),
            1.0,
            0.0,
        ).astype(BF)
        total = jnp.maximum(mm(mask.astype(BF), fold), 1.0)
        weight_ref[:, start : start + lanes] = mask[3:4] / total[3:4]

    small_level(mid_rows, N1, E0, E1)
    small_level(top_rows, N2, E0 + E1, E2)
    rest = E0 + E1 + E2
    edge_ref[:, rest:] = jnp.zeros((16, EDGES - rest), BF)
    weight_ref[:, rest:] = jnp.zeros((1, EDGES - rest), F32)
    gather_sources(
        node_ref[...], half_ref[0], parent, parent_top, index_ref, rows_ref, weight_ref, vw_ref,
        vals,
    )
    bias = bk_ref[...].astype(F32)
    copies[-1].wait()
    for layer in range(2):
        for part in range(8):
            wkt_ref[layer, part * 256 : (part + 1) * 256, :] = wk_ref[
                layer, :, part * 256 : (part + 1) * 256
            ].T
        for row in range(HALF):
            bias_rows[row : row + 1, :] = bias[layer : layer + 1, row * C : (row + 1) * C]
        bias_rows_ref[layer] = bias_rows[...].astype(BF)
        bias_cols_ref[layer] = bias_rows[...].T.astype(BF)
        hown_ref[layer] = gelu(mm(first_columns(packed_ref, layer), edge_ref[...])).astype(BF)
    second_bias = jnp.concatenate([bs_ref[...].astype(F32), jnp.zeros((6, HID), F32)], axis=0)
    bs_cols_ref[...] = second_bias.T


def first_forward_kernel(
    pm_ref, pt_ref, packed_ref, far_ref, edge_ref, hown_ref, bs_ref, wkt_ref, bias_ref, vw_ref,
    h2_ref, up_ref, msg,
):
    second = second_rows(packed_ref, far_ref, 0).T
    first = first_columns(far_ref, 0)
    bias = bs_ref[:, 0:1]

    def hidden(lanes):
        away = gelu(mm(first, edge_ref[:, lanes])).astype(BF)
        one = jnp.concatenate([hown_ref[0, :, lanes], away], axis=0)
        two = gelu(mm(second, one) + bias).astype(BF)
        h2_ref[0:HID, lanes] = two
        h2_ref[HID:AUG, lanes] = ones_rows(two.shape[1])
        return two

    message_pass(
        0, hidden, hot(N1, pm_ref[...]), hot(N2, pt_ref[...]), wkt_ref, bias_ref, vw_ref, up_ref,
        msg,
    )


def mlp_kernel(layer, packed_ref, far_ref, edge_ref, bs_ref, h1_ref, s1_ref, s2_ref, *h2_refs):
    second = second_rows(packed_ref, far_ref, layer).T
    first = jnp.concatenate(
        [first_columns(packed_ref, layer), first_columns(far_ref, layer)], axis=0
    )
    bias = bs_ref[:, layer : layer + 1]
    for start, width in TILES:
        lanes = slice(start, start + width)
        value, slope = gelu_both(mm(first, edge_ref[:, lanes]))
        one = value.astype(BF)
        h1_ref[0:HID, lanes] = one
        h1_ref[HID:AUG, lanes] = ones_rows(width)
        s1_ref[:, lanes] = slope.astype(BF)
        value, slope = gelu_both(mm(second, one) + bias)
        s2_ref[:, lanes] = slope.astype(BF)
        for h2_ref in h2_refs:
            h2_ref[0:HID, lanes] = value.astype(BF)
            h2_ref[HID:AUG, lanes] = ones_rows(width)


def next_forward_kernel(
    half_ref, node_ref, self_ref, up_own_ref, up_far_ref, pm_ref, pt_ref, index_ref, rows_ref,
    weight_ref, h2_ref, wkt_ref, bias_ref,
    pre_ref, state_ref, up_ref, vw_ref, vals, msg,
):
    parent = hot(N1, pm_ref[...])
    parent_top = hot(N2, pt_ref[...])
    pre = mm(self_ref[0].astype(F32).T.astype(BF), node_ref[...])
    pre = pre + (up_own_ref[...] + up_far_ref[...])
    pre_ref[...] = pre
    state = (gelu(pre) * rows_ref[0:1, :]).astype(BF)
    state_ref[...] = state
    gather_sources(
        state, half_ref[0], parent, parent_top, index_ref, rows_ref, weight_ref, vw_ref, vals
    )
    message_pass(
        1, lambda lanes: h2_ref[0:HID, lanes], parent, parent_top, wkt_ref, bias_ref, vw_ref,
        up_ref, msg,
    )


def node_grads(layer, half, h, pre, grad, parent, parent_top, live, self_ref, own_ref, g_ref):
    start = pl.multiple_of(half * HALF, HALF)
    _, slope = gelu_both(pre)
    grad_pre = slope * (live * grad)
    high, low = pieces(grad_pre, 2)
    grad_self = mm(h, high, (1, 1)) + mm(h, low, (1, 1))
    own_ref[288:320, 0:C] = grad_self[0:HALF]
    own_ref[288:320, C : 2 * C] = grad_self[HALF:C]
    self_half = self_ref[layer, pl.ds(start, HALF), :]
    self_in = mm(self_half, high) + mm(self_half, low)
    up_mid = mm_hot(grad_pre, parent, (1, 1), 3)
    up_top = mm_hot(up_mid, parent_top, (1, 1), 3)
    g_ref[0:C, 0:N0] = grad_pre.astype(BF)
    g_ref[0:C, N0 : N0 + E1] = mm(up_mid.astype(BF), owner_hot(N1, E1)).astype(BF)
    g_ref[0:C, N0 + E1 : N0 + E1 + E2] = mm(up_top.astype(BF), owner_hot(N2, E2)).astype(BF)
    g_ref[0:C, N0 + E1 + E2 :] = jnp.zeros((C, 1024 - N0 - E1 - E2), BF)
    return self_in


def grad_tile(g_ref, start, width):
    if start < E0:
        return jnp.concatenate([g_ref[0:C, 0:N0]] * (width // N0), axis=1)
    return g_ref[0:C, N0 : N0 + width]


def value_grads(
    layer, self_in, parent, parent_top, index_ref, rows_ref, weight_ref, h2_ref, wkt_ref, bias_ref,
    g_ref, dvw,
):
    live, child_mid, live_mid, child_top = level_rows(rows_ref)
    bias = bias_ref[layer]
    for start, width in TILES:
        lanes = slice(start, start + width)
        grad = grad_tile(g_ref, start, width)
        offset = mm(bias, grad)
        grad = grad.astype(F32)
        weight = weight_ref[:, lanes]
        for part in range(4):
            kernels = mm(wkt_ref[layer, part * 512 : (part + 1) * 512, :], h2_ref[0:HID, lanes])
            rows = jnp.sum(kernels.reshape(8, C, width) * grad[None], axis=1)
            dvw[part * 8 : (part + 1) * 8, lanes] = (
                rows + offset[part * 8 : (part + 1) * 8]
            ) * weight
    fine = jnp.zeros((HALF, N0), F32)
    for slot in range(DEG):
        lanes = slice(slot * N0, (slot + 1) * N0)
        fine = fine + mm_hot(dvw[:, lanes], hot(N0, index_ref[:, lanes]), (1, 1))
    lanes = slice(E0, E0 + E1)
    mid = mm_hot(dvw[:, lanes], hot(N1, index_ref[:, lanes]), (1, 1))
    lanes = slice(E0 + E1, E0 + E1 + E2)
    top = mm_hot(dvw[:, lanes], hot(N2, index_ref[:, lanes]), (1, 1))

    def rounded(value):
        return value.astype(BF).astype(F32)

    grad_mid = rounded(mid) + mm_hot(rounded(top) / child_top, parent_top, (1, 0), 3) * live_mid
    return self_in + rounded(fine) + mm_hot(grad_mid / child_mid, parent, (1, 0), 3) * live


def fill_pack(core, vw_ref, pack_ref):
    place = pl.ds(pl.multiple_of((1 - core) * QUARTER, QUARTER), QUARTER)
    for index, (start, width) in enumerate(TILES):
        high, low = pieces(vw_ref[place, start : start + width], 2)
        base = C + index * HALF
        pack_ref[base : base + QUARTER, 0:width] = high
        pack_ref[base + QUARTER : base + HALF, 0:width] = low
    pack_ref[C + 2 * HALF : PACK, 768:1024] = jnp.zeros((HALF, 256), BF)


def far_source(pack_ref, index, width):
    base = C + index * HALF
    high = pack_ref[base : base + QUARTER, 0:width].astype(F32)
    return high + pack_ref[base + QUARTER : base + HALF, 0:width].astype(F32)


def fill_grad_kernels(g_ref, source, gk, start, width, rows):
    lanes = slice(start, start + width)
    grad = grad_tile(g_ref, start, width).astype(F32)
    for row in range(rows):
        gk[row * C : (row + 1) * C, lanes] = (grad * source[row : row + 1, :]).astype(BF)


def mlp_backward(
    layer, g_ref, vw_ref, wk_ref, h1_ref, s1_ref, s2_ref, packed_ref, far_ref, edge_ref, own_ref,
    away_ref, gk, g2, g1,
):
    second = second_rows(packed_ref, far_ref, layer)
    for start, width in TILES:
        lanes = slice(start, start + width)
        fill_grad_kernels(g_ref, vw_ref[:, lanes], gk, start, width, HALF)
        two = (s2_ref[:, lanes].astype(F32) * mm(wk_ref[layer], gk[:, lanes])).astype(BF)
        g2[:, lanes] = two
        g1[:, lanes] = (s1_ref[:, lanes].astype(F32) * mm(second, two)).astype(BF)
    grad_second = mm(h1_ref[...], g2[...], (1, 1))
    grad_first = mm(edge_ref[...], g1[...], (1, 1))
    own_ref[0:128, :] = grad_second[0:128, 0:128]
    own_ref[128:256, :] = grad_second[0:128, 128:256]
    own_ref[272:273, :] = grad_second[256:257, 0:128]
    own_ref[273:274, :] = grad_second[256:257, 128:256]
    own_ref[274:281, :] = grad_first[0:7, 0:128]
    own_ref[281:288, :] = jnp.zeros((7, 128), F32)
    away_ref[0:128, :] = grad_second[128:256, 0:128].astype(BF)
    away_ref[128:256, :] = grad_second[128:256, 128:256].astype(BF)
    tail = jnp.concatenate(
        [grad_second[256:257, 0:128], grad_second[256:257, 128:256], grad_first[0:7, 128:256],
         jnp.zeros((7, 128), F32)],
        axis=0,
    )
    away_ref[256:272, :] = tail.astype(BF)


def kernel_weight_kernel(
    core_ref, *refs
):
    layer_refs, (joined_ref, bias_ref, gk) = (refs[0:5], refs[5:10]), refs[10:]
    mine = pl.ds(pl.multiple_of(core_ref[0] * QUARTER, QUARTER), QUARTER)
    for layer, (pack_ref, far_ref, vw_ref, h2_ref, h2_far_ref) in enumerate(layer_refs):
        for index, (start, width) in enumerate(TILES):
            source = vw_ref[mine, start : start + width]
            fill_grad_kernels(pack_ref, source, gk, start, width, QUARTER)
        product = mm(h2_ref[...], gk[...], (1, 1))
        for index, (start, width) in enumerate(TILES):
            source = far_source(far_ref, index, width)
            fill_grad_kernels(far_ref, source, gk, start, width, QUARTER)
        product = product + mm(h2_far_ref[...], gk[...], (1, 1))
        for part in range(4):
            for block in range(8):
                joined_ref[part * 8 + block, layer * 64 : (layer + 1) * 64, :] = product[
                    part * 64 : (part + 1) * 64, block * 128 : (block + 1) * 128
                ].astype(BF)
        for block in range(8):
            row = layer * 8 + block
            bias_ref[row : row + 1, :] = product[HID : HID + 1, block * 128 : (block + 1) * 128]


def last_node_kernel(
    half_ref, core_ref, state_ref, self_ref, up_own_ref, up_far_ref, cot_ref, pm_ref, pt_ref,
    index_ref, rows_ref, weight_ref, h2_ref, wkt_ref, bias_ref, vw_ref,
    out_ref, own_ref, g_ref, dx_ref, dvw,
):
    fill_pack(core_ref[0], vw_ref, g_ref)
    parent = hot(N1, pm_ref[...])
    parent_top = hot(N2, pt_ref[...])
    live = rows_ref[0:1, :]
    state = state_ref[...]
    pre = mm(self_ref[1].astype(F32).T.astype(BF), state)
    pre = pre + (up_own_ref[...] + up_far_ref[...])
    out_ref[...] = (gelu(pre) * live).astype(BF)
    self_in = node_grads(
        1, half_ref[0], state, pre, cot_ref[...].astype(F32), parent, parent_top, live, self_ref,
        own_ref, g_ref,
    )
    dx_ref[...] = value_grads(
        1, self_in, parent, parent_top, index_ref, rows_ref, weight_ref, h2_ref, wkt_ref, bias_ref,
        g_ref, dvw,
    )


def last_edge_kernel(
    g_ref, vw_ref, wk_ref, h1_ref, s1_ref, s2_ref, packed_ref, far_ref, edge_ref, self_grad_ref,
    own_ref, away_ref, gk, g2, g1,
):
    mlp_backward(
        1, g_ref, vw_ref, wk_ref, h1_ref, s1_ref, s2_ref, packed_ref, far_ref, edge_ref, own_ref,
        away_ref, gk, g2, g1,
    )
    own_ref[256:272, :] = jnp.zeros((16, 128), F32)
    own_ref[288:320, :] = self_grad_ref[288:320, :]


def first_edge_kernel(
    half_ref, core_ref, node_ref, pre_ref, dx_own_ref, dx_far_ref, self_ref, pm_ref, pt_ref, rows_ref,
    vw_ref, wk_ref, h1_ref, s1_ref, s2_ref, packed_ref, far_ref, edge_ref, away1_ref,
    g_ref, self_in_ref, own_ref, away_ref, grad, gk, g2, g1,
):
    fill_pack(core_ref[0], vw_ref, g_ref)
    away_ref[AUG:, :] = away1_ref[...]
    start = pl.multiple_of(half_ref[0] * HALF, HALF)
    grad[pl.ds(start, HALF), :] = dx_own_ref[...]
    grad[pl.ds(HALF - start, HALF), :] = dx_far_ref[...]
    self_in_ref[...] = node_grads(
        0, half_ref[0], node_ref[...], pre_ref[...], grad[...], hot(N1, pm_ref[...]),
        hot(N2, pt_ref[...]), rows_ref[0:1, :], self_ref, own_ref, g_ref,
    )
    own_ref[256:272, :] = jnp.zeros((16, 128), F32)
    mlp_backward(
        0, g_ref, vw_ref, wk_ref, h1_ref, s1_ref, s2_ref, packed_ref, far_ref, edge_ref, own_ref,
        away_ref.at[0:AUG, :], gk, g2, g1,
    )


def first_node_kernel(
    self_in_ref, pm_ref, pt_ref, index_ref, rows_ref, weight_ref, h2_ref, wkt_ref, bias_ref, g_ref,
    dx_ref, dvw,
):
    dx_ref[...] = value_grads(
        0, self_in_ref[...], hot(N1, pm_ref[...]), hot(N2, pt_ref[...]), index_ref, rows_ref,
        weight_ref, h2_ref, wkt_ref, bias_ref, g_ref, dvw,
    )


def join_kernel(core_ref, own0_ref, own1_ref, away_ref, bias_ref, _, out_ref, rows, tail, sem):
    for layer, own_ref in enumerate((own0_ref, own1_ref)):
        base = layer * SMALL
        far = away_ref[layer * AUG : (layer + 1) * AUG, :].astype(F32)
        rows[base : base + 256, :] = own_ref[0:256, :] + far[0:256]
        rows[base + 256 : base + 272, :] = jnp.zeros((16, 128), F32)
        place = pl.ds(pl.multiple_of(base + 256 + core_ref[0] * 8, 8), 8)
        rows[place, :] = bias_ref[layer * 8 : (layer + 1) * 8, :]
        rows[base + 272 : base + 288, :] = own_ref[272:288, :] + far[256:272]
        rows[base + 288 : base + 320, :] = own_ref[288:320, :]
    for block in range(32):
        if block < 2 * SMALL // 32:
            tail[block] = rows[block * 32 : (block + 1) * 32, :].astype(BF)
        else:
            tail[block] = jnp.zeros((32, 128), BF)
    copy = pltpu.make_async_copy(tail, out_ref.at[:, 128:BLOCK, :], sem.at[0])
    copy.start()
    copy.wait()


def sum_kernel(parts_ref, out_ref):
    total = parts_ref[0].astype(F32)
    for peer in range(1, 32):
        total = total + parts_ref[peer].astype(F32)
    total = total.astype(BF)
    for peer in range(32):
        out_ref[peer] = total


def spread_kernel(
    core_ref, own_ref, far_ref,
    kernel_ref, second_ref, second_bias_ref, first_ref, first_bias_ref, kernel_bias_ref, self_ref,
    rows,
):
    core, part = core_ref[0], pl.program_id(0)
    for side_ref, side in ((own_ref, core), (far_ref, 1 - core)):
        for block in range(8):
            lanes = pl.ds(pl.multiple_of(side * 1024 + block * 128, 128), 128)
            for layer in range(2):
                kernel_ref[layer, :, lanes] = side_ref[
                    part * 8 + block, layer * 64 : (layer + 1) * 64, :
                ].astype(F32)

    @pl.when(part == 0)
    def _():
        spread_small(
            own_ref, far_ref, second_ref, second_bias_ref, first_ref, first_bias_ref,
            kernel_bias_ref, self_ref, rows,
        )


def spread_small(
    own_ref, far_ref, second_ref, second_bias_ref, first_ref, first_bias_ref, kernel_bias_ref,
    self_ref, rows,
):
    for block in range(2 * SMALL // 32):
        rows[block * 32 : (block + 1) * 32, :] = own_ref[block, 128:BLOCK, :].astype(
            F32
        ) + far_ref[block, 128:BLOCK, :].astype(F32)
    for layer in range(2):
        base = layer * SMALL
        second_ref[layer, :, 0:128] = rows[base : base + 128, :]
        second_ref[layer, :, 128:256] = rows[base + 128 : base + 256, :]
        for block in range(16):
            lanes = slice(block * 128, (block + 1) * 128)
            row = base + 256 + block
            kernel_bias_ref[layer : layer + 1, lanes] = rows[row : row + 1, :]
        second_bias_ref[layer : layer + 1, 0:128] = rows[base + 272 : base + 273, :]
        second_bias_ref[layer : layer + 1, 128:256] = rows[base + 273 : base + 274, :]
        for row in range(6):
            first_ref[row, layer : layer + 1, :] = rows[base + 274 + row : base + 275 + row, :]
        first_bias_ref[layer : layer + 1, :] = rows[base + 280 : base + 281, :]
        self_ref[layer, 0:HALF, :] = rows[base + 288 : base + 320, 0:C]
        self_ref[layer, HALF:C, :] = rows[base + 288 : base + 320, C : 2 * C]


def input_kernel(half_ref, own_ref, far_ref, out_ref):
    start = pl.multiple_of(half_ref[0] * HALF, HALF)
    out_ref[pl.ds(start, HALF), :] = own_ref[...]
    out_ref[pl.ds(HALF - start, HALF), :] = far_ref[...]


def vmem_spec():
    return pl.BlockSpec(memory_space=pltpu.VMEM)


def smem_spec():
    return pl.BlockSpec(memory_space=pltpu.SMEM)


def call(kernel, outs, args, scalars=0, scratch=(), us=1, far=0, aliases=None):
    count = len(args)
    specs = [smem_spec()] * scalars + [vmem_spec()] * (count - scalars - far)
    args = list(args[: count - far]) + [
        pltpu.with_memory_space_constraint(value, pltpu.HBM) for value in args[count - far :]
    ]
    return pl.pallas_call(
        kernel,
        out_shape=[jax.ShapeDtypeStruct(*out) for out in outs],
        in_specs=specs + [pl.BlockSpec(memory_space=pltpu.HBM)] * far,
        out_specs=[
            pl.BlockSpec(memory_space=pltpu.HBM) if aliases else vmem_spec() for _ in outs
        ],
        scratch_shapes=[
            pltpu.SemaphoreType.DMA(entry[0]) if entry[1] is None else pltpu.VMEM(*entry)
            for entry in scratch
        ],
        input_output_aliases=aliases or {},
        compiler_params=pltpu.CompilerParams(vmem_limit_bytes=VMEM_MIB << 20),
        cost_estimate=pl.CostEstimate(
            flops=us * 1000000000, bytes_accessed=1 << 20, transcendentals=0
        ),
    )(*args)


def swap(value, axis):
    return lax.ppermute(value, axis, [(0, 1), (1, 0)])


def per_device(
    node_input, geometry, counts, parent_mid, parent_top, neighbours_fine, neighbours_mid,
    neighbours_top, w_first, b_first, w_second, b_second, w_kernel, b_kernel, w_self, cotangent,
):
    half = lax.axis_index("tensor").astype(jnp.int32).reshape(1)
    core = lax.axis_index("core").astype(jnp.int32).reshape(1)
    counts, half, core, w_second = lax.optimization_barrier((counts, half, core, w_second))
    pm = parent_mid.reshape(1, N0)
    pt = parent_top.reshape(1, N1)
    node = node_input.T
    wide = (AUG, EDGES)
    edges = (HID, EDGES)
    sources = (HALF, EDGES)

    (packed,) = call(
        pack_kernel,
        [((AUG, HID), BF)],
        [w_second, w_first.transpose(1, 0, 2), b_first],
        scratch=[((2, 128, HID), BF), ((6, 2, 128), BF), ((2, 128), BF), ((16, HID), F32),
                 ((3,), None)],
        far=3,
    )
    far = swap(packed, "tensor")
    (edge, weight, near, rows, wkt, bias_rows, bias_cols, bs_cols, hown, vw0, pm, pt, node) = call(
        prep_kernel,
        [((16, EDGES), BF), ((1, EDGES), F32), ((1, EDGES), jnp.int32), ((8, N0), F32),
         ((2, HALF * C, HID), BF), ((2, HALF, C), BF), ((2, C, HALF), BF), ((HID, 8), F32),
         ((2, 128, EDGES), BF), (sources, F32), ((1, N0), jnp.int32), ((1, N1), jnp.int32),
         ((C, N0), BF)],
        [counts, half, packed, geometry.T, pm, pt, neighbours_fine.T, neighbours_mid.T,
         neighbours_top.T, node, b_kernel, b_second, w_kernel],
        scalars=2,
        far=10,
        scratch=[((3, N0), F32), ((8, N0), jnp.int32), ((8, N1), jnp.int32), ((8, N2), jnp.int32),
                 ((2, HALF * C), BF), ((2, HID), BF), ((2, HID, HALF * C), BF), ((10,), None),
                 ((C, N0 + 256), F32), ((HALF, C), F32)],
        us=4,
    )
    h2_0, up0 = call(
        first_forward_kernel,
        [(wide, BF), ((C, N0), F32)],
        [pm, pt, packed, far, edge, hown, bs_cols, wkt, bias_cols, vw0],
        scratch=[((C, EDGES), F32)],
        us=8,
    )
    up0_far = swap(up0, "tensor")
    h2_0_far = swap(h2_0, "core")

    def mlp(layer, outs):
        return call(
            functools.partial(mlp_kernel, layer), outs, [packed, far, edge, bs_cols], us=5
        )

    h1_1, s1_1, s2_1, h2_1 = mlp(1, [(wide, BF), (edges, BF), (edges, BF), (wide, BF)])
    pre0, state, up1, vw1 = call(
        next_forward_kernel,
        [((C, N0), F32), ((C, N0), BF), ((C, N0), F32), (sources, F32)],
        [half, node, w_self, up0, up0_far, pm, pt, near, rows, weight, h2_1, wkt, bias_cols],
        scalars=1,
        scratch=[((C, N0 + 256), F32), ((C, EDGES), F32)],
        us=5,
    )
    up1_far = swap(up1, "tensor")
    h2_1_far = swap(h2_1, "core")
    up1, edge = lax.optimization_barrier((up1, edge))
    h1_0, s1_0, s2_0 = mlp(0, [(wide, BF), (edges, BF), (edges, BF)])
    out, self_grad1, g1, dx1 = call(
        last_node_kernel,
        [((C, N0), BF), ((SMALL, 128), F32), ((PACK, 1024), BF), ((HALF, N0), F32)],
        [half, core, state, w_self, up1, up1_far, cotangent.T, pm, pt, near, rows, weight, h2_1,
         wkt, bias_rows, vw1],
        scalars=2,
        scratch=[(sources, F32)],
        us=5,
    )
    dx1_far = swap(dx1, "tensor")
    g1_far = swap(g1, "core")
    edge_scratch = [((HALF * C, EDGES), BF), (edges, BF), (edges, BF)]
    own1, away1 = call(
        last_edge_kernel,
        [((SMALL, 128), F32), ((AUG, 128), BF)],
        [g1, vw1, w_kernel, h1_1, s1_1, s2_1, packed, far, edge, self_grad1],
        scratch=edge_scratch,
        us=5,
    )
    g0, self_in0, own0, away = call(
        first_edge_kernel,
        [((PACK, 1024), BF), ((HALF, N0), F32), ((SMALL, 128), F32), ((2 * AUG, 128), BF)],
        [half, core, node, pre0, dx1, dx1_far, w_self, pm, pt, rows, vw0, w_kernel, h1_0, s1_0, s2_0,
         packed, far, edge, away1],
        scalars=2,
        scratch=[((C, N0), F32)] + edge_scratch,
        us=6,
    )
    away_far = swap(away, "tensor")
    g0_far = swap(g0, "core")
    blocks = (32, BLOCK, 128)
    joined, bias = call(
        kernel_weight_kernel,
        [(blocks, BF), ((16, 128), F32)],
        [core, g0, g0_far, vw0, h2_0, h2_0_far, g1, g1_far, vw1, h2_1, h2_1_far],
        scalars=1,
        scratch=[((QUARTER * C, EDGES), BF)],
        us=8,
    )
    (joined,) = call(
        join_kernel, [(blocks, BF)], [core, own0, own1, away_far, bias, joined],
        scalars=1,
        far=1,
        scratch=[((2 * SMALL, 128), F32), ((32, 32, 128), BF), ((1,), None)],
        aliases={5: 0},
    )
    joined, g0 = lax.optimization_barrier((joined, g0))
    parts = lax.all_to_all(joined, ROW_AXES, 0, 0, tiled=True)
    (dx0,) = call(
        first_node_kernel,
        [((HALF, N0), F32)],
        [self_in0, pm, pt, near, rows, weight, h2_0, wkt, bias_rows, g0],
        scratch=[(sources, F32)],
        us=5,
    )
    (total,) = call(sum_kernel, [(blocks, BF)], [parts])
    dx0_far = swap(dx0, "tensor")
    total, dx0_far = lax.optimization_barrier((total, dx0_far))
    (input_grad,) = call(
        input_kernel, [((C, N0), F32)], [half, dx0, dx0_far], scalars=1
    )
    whole = lax.all_to_all(total, ROW_AXES, 0, 0, tiled=True)
    whole_far = swap(whole, "core")
    small_shapes = (
        (2, 128, HID), (2, HID), (6, 2, 128), (2, 128), (2, HALF * C), (2, C, C)
    )
    grad_kernel, grad_second, grad_b_second, grad_first, grad_b_first, grad_b_kernel, grad_self = (
        pl.pallas_call(
            spread_kernel,
            grid=(4,),
            out_shape=[
                jax.ShapeDtypeStruct(shape, F32)
                for shape in ((2, HID, HALF * C),) + small_shapes
            ],
            in_specs=[smem_spec(), vmem_spec(), vmem_spec()],
            out_specs=[pl.BlockSpec((2, 64, HALF * C), lambda part: (0, part, 0))]
            + [vmem_spec() for _ in small_shapes],
            scratch_shapes=[pltpu.VMEM((2 * SMALL, 128), F32)],
            compiler_params=pltpu.CompilerParams(vmem_limit_bytes=VMEM_MIB << 20),
        )(core, whole, whole_far)
    )
    return (
        out.T, input_grad.T, grad_first.transpose(1, 0, 2), grad_b_first, grad_second,
        grad_b_second, grad_kernel, grad_b_kernel, grad_self,
    )


def solution(mesh):
    fine = Mesh(mesh.devices.reshape(2, 4, 4, 2, 2), DP_AXES + ("tensor",))
    dp = DP_AXES
    placed = (
        P(dp, None), P(dp, None), P(dp), P(dp), P(dp), P(dp, None), P(dp, None), P(dp, None),
        P(None, None, "tensor"), P(None, "tensor"), P(None, "tensor", None), P(),
        P(None, None, "tensor"), P(None, "tensor"), P(), P(dp, None),
    )
    return jax.shard_map(
        per_device,
        mesh=fine,
        in_specs=placed,
        out_specs=(
            P(dp, None), P(dp, None), P(None, None, "tensor"), P(None, "tensor"),
            P(None, "tensor", None), P(), P(None, None, "tensor"), P(None, "tensor"), P(),
        ),
        check_vma=False,
    )
```

```python
import functools

import jax
import jax.numpy as jnp
from jax import lax
from jax.experimental import pallas as pl
from jax.experimental.pallas import tpu as pltpu
from jax.sharding import Mesh, PartitionSpec as P

C = 64
HALF = 32
HID = 256
N0, N1, N2 = 256, 64, 16
DEG = 8
E0, E1, E2 = N0 * DEG, N1 * DEG, N2 * DEG
EDGES = 2816
TILES = ((0, 1024), (1024, 1024), (2048, 768))
WIDE = EDGES // 2
PARTS = 2
SMALL = 320
BLOCK = 160
QUARTER = HALF // 2
PACK = C + 3 * HALF
VMEM_MIB = 28
AUG = HID + 16
BF = jnp.bfloat16
F32 = jnp.float32
ROW_AXES = ("yl", "z", "x")
DP_AXES = ROW_AXES + ("core",)


def mm(left, right, contract=(1, 0)):
    return lax.dot_general(
        left, right, (((contract[0],), (contract[1],)), ((), ())), preferred_element_type=F32
    )


def pieces(value, count):
    parts = []
    for _ in range(count):
        part = value.astype(BF)
        parts.append(part)
        value = value - part.astype(F32)
    return parts


def mm_hot(value, hot, contract, count=2):
    rows = value.shape[0]
    product = mm(jnp.concatenate(pieces(value, count), axis=0), hot, contract)
    total = product[:rows]
    for index in range(1, count):
        total = total + product[index * rows : (index + 1) * rows]
    return total


def hot(rows, index):
    lanes = index.shape[1]
    match = lax.broadcasted_iota(jnp.int32, (rows, lanes), 0) == index
    return jnp.where(match, 1.0, 0.0).astype(BF)


def owner_hot(rows, lanes):
    index = lax.broadcasted_iota(jnp.int32, (rows, lanes), 1) & (rows - 1)
    match = lax.broadcasted_iota(jnp.int32, (rows, lanes), 0) == index
    return jnp.where(match, 1.0, 0.0).astype(BF)


def gelu(value):
    inner = value * (0.7978845608028654 + 0.035677408136300125 * (value * value))
    return value * (0.5 + 0.5 * jnp.tanh(inner))


def gelu_both(value):
    square = value * value
    inner = value * (0.7978845608028654 + 0.035677408136300125 * square)
    share = 0.5 + 0.5 * jnp.tanh(inner)
    slope = share + (share * (1.0 - share)) * (
        value * (1.5957691216057308 + 0.21406444881780074 * square)
    )
    return value * share, slope


def level_rows(rows_ref):
    return (
        rows_ref[0:1, :], rows_ref[1:2, 0:N1], rows_ref[2:3, 0:N1], rows_ref[3:4, 0:N2]
    )


def gather_sources(state, half, parent, parent_top, index_ref, rows_ref, weight_ref, vw_ref, vals):
    live, child_mid, live_mid, child_top = level_rows(rows_ref)
    start = pl.multiple_of(half * HALF, HALF)
    wide = state.astype(F32)
    mid = mm((wide * live).astype(BF), parent, (1, 1)) / child_mid
    top = mm_hot(mid * live_mid, parent_top, (1, 1), 3) / child_top
    vals[:, 0:N0] = wide
    vals[:, N0 : N0 + N1] = mid
    vals[:, N0 + 128 : N0 + 128 + N2] = top
    fine_half = vals[pl.ds(start, HALF), 0:N0].astype(BF)
    mid_half = vals[pl.ds(start, HALF), N0 : N0 + N1].astype(BF)
    top_half = vals[pl.ds(start, HALF), N0 + 128 : N0 + 128 + N2].astype(BF)
    for slot in range(DEG):
        lanes = slice(slot * N0, (slot + 1) * N0)
        vw_ref[:, lanes] = mm(fine_half, hot(N0, index_ref[:, lanes])) * weight_ref[:, lanes]
    lanes = slice(E0, E0 + E1)
    vw_ref[:, lanes] = mm(mid_half, hot(N1, index_ref[:, lanes])) * weight_ref[:, lanes]
    lanes = slice(E0 + E1, E0 + E1 + E2)
    vw_ref[:, lanes] = mm(top_half, hot(N2, index_ref[:, lanes])) * weight_ref[:, lanes]
    vw_ref[:, E0 + E1 + E2 :] = jnp.zeros((HALF, EDGES - E0 - E1 - E2), F32)


def halves(body):
    def step(index, carry):
        body(pl.ds(pl.multiple_of(index * WIDE, WIDE), WIDE))
        return carry

    lax.fori_loop(0, 2, step, 0)


def channel_parts(body, parts):
    def step(index, carry):
        rows, channels = HALF * C // parts, HALF // parts
        body(
            pl.ds(pl.multiple_of(index * rows, rows), rows),
            pl.ds(pl.multiple_of(index * channels, channels), channels),
        )
        return carry

    lax.fori_loop(0, parts, step, 0)


def message_pass(layer, h2_ref, parent, parent_top, wkt_ref, bias_ref, vw_ref, up_ref, msg):
    bias = bias_ref[layer]
    bias = jnp.concatenate([bias, bias], axis=1)
    for start, width in TILES:
        lanes = slice(start, start + width)
        msg[:, lanes] = mm(bias, jnp.concatenate(pieces(vw_ref[:, lanes], 2), axis=0))

    def part(rows, channels):
        for start, width in TILES:
            lanes = slice(start, start + width)
            source = vw_ref[channels, lanes]
            kernels = mm(wkt_ref[layer, rows, :], h2_ref[0:HID, lanes])
            total = msg[:, lanes]
            for channel in range(HALF // PARTS):
                total = total + (
                    kernels[channel * C : (channel + 1) * C] * source[channel : channel + 1, :]
                )
            msg[:, lanes] = total

    channel_parts(part, PARTS)
    total_fine = msg[:, 0:N0]
    for slot in range(1, DEG):
        total_fine = total_fine + msg[:, slot * N0 : (slot + 1) * N0]
    total_mid = mm_hot(msg[:, E0 : E0 + E1], owner_hot(N1, E1), (1, 1))
    total_top = mm_hot(msg[:, E0 + E1 : E0 + E1 + E2], owner_hot(N2, E2), (1, 1))
    up_mid = total_mid + mm_hot(total_top, parent_top, (1, 0))
    up_ref[...] = total_fine + mm_hot(up_mid, parent, (1, 0))


def first_columns(packed_ref, layer):
    return packed_ref[HID : HID + 16, layer * 128 : (layer + 1) * 128].astype(F32).T.astype(BF)


def second_rows(packed_ref, far_ref, layer):
    rows = slice(layer * 128, (layer + 1) * 128)
    return jnp.concatenate([packed_ref[rows, :], far_ref[rows, :]], axis=0)


def ones_rows(width):
    return jnp.where(lax.broadcasted_iota(jnp.int32, (16, width), 0) == 0, 1.0, 0.0).astype(BF)


def pack_kernel(second_ref, first_ref, bias_ref, packed_ref, second, first, bias, rows, sems):
    copies = [
        pltpu.make_async_copy(source, target, sems.at[index])
        for index, (source, target) in enumerate(
            ((second_ref, second), (first_ref, first), (bias_ref, bias))
        )
    ]
    for copy in copies:
        copy.start()
    rows[...] = jnp.zeros_like(rows)
    for copy in copies:
        copy.wait()
    packed_ref[0:128, :] = second[0]
    packed_ref[128:256, :] = second[1]
    bias_rows = bias[...].astype(F32)
    for layer in range(2):
        lanes = slice(layer * 128, (layer + 1) * 128)
        for row in range(6):
            rows[row : row + 1, lanes] = first[row].astype(F32)[layer : layer + 1]
        rows[6:7, lanes] = bias_rows[layer : layer + 1]
    packed_ref[256:272, :] = rows[...].astype(BF)


def prep_kernel(
    count_ref, half_ref, packed_ref, geometry_hbm, pm_hbm, pt_hbm, near0_hbm, near1_hbm, near2_hbm,
    node_hbm, bk_hbm, bs_hbm, wk_hbm,
    edge_ref, weight_ref, index_ref, rows_ref, wkt_ref, bias_rows_ref, bias_cols_ref, bs_cols_ref,
    hown_ref, vw_ref, pm_ref, pt_ref, node_ref,
    geometry_ref, near0_ref, near1_ref, near2_ref, bk_ref, bs_ref, wk_ref, sems, vals, bias_rows,
):
    copies = [
        pltpu.make_async_copy(source, target, sems.at[index])
        for index, (source, target) in enumerate(
            (
                (geometry_hbm, geometry_ref), (pm_hbm, pm_ref), (pt_hbm, pt_ref),
                (near0_hbm, near0_ref), (near1_hbm, near1_ref), (near2_hbm, near2_ref),
                (node_hbm, node_ref), (bk_hbm, bk_ref), (bs_hbm, bs_ref), (wk_hbm, wk_ref),
            )
        )
    ]
    for copy in copies:
        copy.start()
    for copy in copies[:-1]:
        copy.wait()
    live = jnp.where(
        lax.broadcasted_iota(jnp.int32, (1, N0), 1) < count_ref[0], 1.0, 0.0
    ).astype(F32)
    parent = hot(N1, pm_ref[...])
    parent_top = hot(N2, pt_ref[...])
    live8 = jnp.broadcast_to(live, (16, N0))
    child_mid = mm(live8.astype(BF), parent, (1, 1))
    live_mid = jnp.where(child_mid > 0.5, 1.0, 0.0)
    child_top = mm(live_mid.astype(BF), parent_top, (1, 1))
    live_top = jnp.where(child_top > 0.5, 1.0, 0.0)
    child_mid = jnp.maximum(child_mid, 1.0)
    child_top = jnp.maximum(child_top, 1.0)
    rows_ref[...] = jnp.zeros_like(rows_ref)
    rows_ref[0:1, :] = live
    rows_ref[1:2, 0:N1] = child_mid[0:1]
    rows_ref[2:3, 0:N1] = live_mid[0:1]
    rows_ref[3:4, 0:N2] = child_top[0:1]
    index_ref[...] = jnp.zeros_like(index_ref)
    for slot in range(DEG):
        row = slice(slot, slot + 1)
        index_ref[:, slot * N0 : (slot + 1) * N0] = near0_ref[row, :]
        index_ref[:, E0 + slot * N1 : E0 + (slot + 1) * N1] = near1_ref[row, :]
        start = E0 + E1 + slot * N2
        index_ref[:, start : start + N2] = near2_ref[row, :]
    vals[0:16, 0:N0] = jnp.zeros((16, N0), F32)
    vals[0:3, 0:N0] = geometry_ref[...]
    coords = vals[0:16, 0:N0]
    coords_mid = mm_hot(coords * live, parent, (1, 1), 3) / child_mid
    coords_top = mm_hot(coords_mid * live_mid, parent_top, (1, 1), 3) / child_top
    lane_row = lax.broadcasted_iota(jnp.int32, (16, 1), 0)

    def with_live(values, live_row):
        return jnp.where(lane_row == 3, live_row, values).astype(BF)

    fine_rows = with_live(coords, live)
    mid_rows = with_live(coords_mid, live_mid[0:1])
    top_rows = with_live(coords_top, live_top[0:1])

    def edges(own, near):
        low = jnp.where(lane_row < 3, own, 0.0)
        high = pltpu.roll(jnp.where(lane_row < 3, near, 0.0), 3, 0)
        return jnp.where(lane_row == 6, 1.0, low + high).astype(BF)

    fine = fine_rows.astype(F32)
    masks = []
    for slot in range(DEG):
        lanes = slice(slot * N0, (slot + 1) * N0)
        near = mm(fine_rows, hot(N0, index_ref[:, lanes]))
        edge_ref[:, lanes] = edges(fine, near)
        masks.append(live * near[3:4])
    total = masks[0]
    for mask in masks[1:]:
        total = total + mask
    total = jnp.maximum(total, 1.0)
    for slot in range(DEG):
        weight_ref[:, slot * N0 : (slot + 1) * N0] = masks[slot] / total

    def small_level(values, rows, start, lanes):
        own = mm(values, owner_hot(rows, lanes))
        near = mm(values, hot(rows, index_ref[:, start : start + lanes]))
        edge_ref[:, start : start + lanes] = edges(own, near)
        mask = own * near
        fold = jnp.where(
            (lax.broadcasted_iota(jnp.int32, (lanes, lanes), 0) & (rows - 1))
            == (lax.broadcasted_iota(jnp.int32, (lanes, lanes), 1) & (rows - 1)),
            1.0,
            0.0,
        ).astype(BF)
        total = jnp.maximum(mm(mask.astype(BF), fold), 1.0)
        weight_ref[:, start : start + lanes] = mask[3:4] / total[3:4]

    small_level(mid_rows, N1, E0, E1)
    small_level(top_rows, N2, E0 + E1, E2)
    rest = E0 + E1 + E2
    edge_ref[:, rest:] = jnp.zeros((16, EDGES - rest), BF)
    weight_ref[:, rest:] = jnp.zeros((1, EDGES - rest), F32)
    gather_sources(
        node_ref[...], half_ref[0], parent, parent_top, index_ref, rows_ref, weight_ref, vw_ref,
        vals,
    )
    bias = bk_ref[...].astype(F32)
    copies[-1].wait()
    for layer in range(2):
        for part in range(8):
            wkt_ref[layer, part * 256 : (part + 1) * 256, :] = wk_ref[
                layer, :, part * 256 : (part + 1) * 256
            ].T
        for row in range(HALF):
            bias_rows[row : row + 1, :] = bias[layer : layer + 1, row * C : (row + 1) * C]
        bias_rows_ref[layer] = bias_rows[...].astype(BF)
        bias_cols_ref[layer] = bias_rows[...].T.astype(BF)
    hown_ref[...] = gelu(mm(first_columns(packed_ref, 0), edge_ref[...])).astype(BF)
    second_bias = jnp.concatenate([bs_ref[...].astype(F32), jnp.zeros((6, HID), F32)], axis=0)
    bs_cols_ref[...] = second_bias.T


def first_forward_kernel(
    pm_ref, pt_ref, packed_ref, far_ref, edge_ref, hown_ref, bs_ref, wkt_ref, bias_ref, vw_ref,
    h2_ref, up_ref, msg,
):
    second = second_rows(packed_ref, far_ref, 0).T
    first = first_columns(far_ref, 0)
    bias = bs_ref[:, 0:1]

    def body(lanes):
        away = gelu(mm(first, edge_ref[:, lanes])).astype(BF)
        one = jnp.concatenate([hown_ref[:, lanes], away], axis=0)
        h2_ref[0:HID, lanes] = gelu(mm(second, one) + bias).astype(BF)

    halves(body)
    h2_ref[HID:AUG, :] = ones_rows(EDGES)
    message_pass(
        0, h2_ref, hot(N1, pm_ref[...]), hot(N2, pt_ref[...]), wkt_ref, bias_ref, vw_ref, up_ref,
        msg,
    )


def mlp_kernel(layer, packed_ref, far_ref, edge_ref, bs_ref, h1_ref, s1_ref, s2_ref, *h2_refs):
    second = second_rows(packed_ref, far_ref, layer).T
    first = jnp.concatenate(
        [first_columns(packed_ref, layer), first_columns(far_ref, layer)], axis=0
    )
    bias = bs_ref[:, layer : layer + 1]

    def body(lanes):
        value, slope = gelu_both(mm(first, edge_ref[:, lanes]))
        one = value.astype(BF)
        h1_ref[0:HID, lanes] = one
        s1_ref[:, lanes] = slope.astype(BF)
        value, slope = gelu_both(mm(second, one) + bias)
        s2_ref[:, lanes] = slope.astype(BF)
        for h2_ref in h2_refs:
            h2_ref[0:HID, lanes] = value.astype(BF)

    halves(body)
    for ref in (h1_ref,) + h2_refs:
        ref[HID:AUG, :] = ones_rows(EDGES)


def next_forward_kernel(
    half_ref, node_ref, self_ref, up_own_ref, up_far_ref, pm_ref, pt_ref, index_ref, rows_ref,
    weight_ref, h2_ref, wkt_ref, bias_ref,
    pre_ref, state_ref, up_ref, vw_ref, vals, msg,
):
    parent = hot(N1, pm_ref[...])
    parent_top = hot(N2, pt_ref[...])
    pre = mm(self_ref[0].astype(F32).T.astype(BF), node_ref[...])
    pre = pre + (up_own_ref[...] + up_far_ref[...])
    pre_ref[...] = pre
    state = (gelu(pre) * rows_ref[0:1, :]).astype(BF)
    state_ref[...] = state
    gather_sources(
        state, half_ref[0], parent, parent_top, index_ref, rows_ref, weight_ref, vw_ref, vals
    )
    message_pass(
        1, h2_ref, parent, parent_top, wkt_ref, bias_ref, vw_ref, up_ref, msg,
    )


def node_grads(layer, half, h, pre, grad, parent, parent_top, live, self_ref, own_ref, g_ref):
    start = pl.multiple_of(half * HALF, HALF)
    _, slope = gelu_both(pre)
    grad_pre = slope * (live * grad)
    high, low = pieces(grad_pre, 2)
    grad_self = mm(h, high, (1, 1)) + mm(h, low, (1, 1))
    own_ref[288:320, 0:C] = grad_self[0:HALF]
    own_ref[288:320, C : 2 * C] = grad_self[HALF:C]
    self_half = self_ref[layer, pl.ds(start, HALF), :]
    self_in = mm(self_half, high) + mm(self_half, low)
    up_mid = mm_hot(grad_pre, parent, (1, 1), 3)
    up_top = mm_hot(up_mid, parent_top, (1, 1), 3)
    g_ref[0:C, 0:N0] = grad_pre.astype(BF)
    g_ref[0:C, N0 : N0 + E1] = mm(up_mid.astype(BF), owner_hot(N1, E1)).astype(BF)
    g_ref[0:C, N0 + E1 : N0 + E1 + E2] = mm(up_top.astype(BF), owner_hot(N2, E2)).astype(BF)
    g_ref[0:C, N0 + E1 + E2 :] = jnp.zeros((C, 1024 - N0 - E1 - E2), BF)
    return self_in


def grad_tile(g_ref, start, width):
    if start < E0:
        return jnp.concatenate([g_ref[0:C, 0:N0]] * (width // N0), axis=1)
    return g_ref[0:C, N0 : N0 + width]


def value_grads(
    layer, self_in, parent, parent_top, index_ref, rows_ref, weight_ref, h2_ref, wkt_ref, bias_ref,
    g_ref, dvw,
):
    live, child_mid, live_mid, child_top = level_rows(rows_ref)

    def part(rows, channels):
        for start, width in TILES:
            lanes = slice(start, start + width)
            grad = grad_tile(g_ref, start, width)
            offset = mm(bias_ref[layer, channels, :], grad)
            kernels = mm(wkt_ref[layer, rows, :], h2_ref[0:HID, lanes])
            product = kernels.reshape(HALF // PARTS, C, width) * grad.astype(F32)[None]
            dvw[channels, lanes] = (jnp.sum(product, axis=1) + offset) * weight_ref[:, lanes]

    channel_parts(part, PARTS)
    fine = jnp.zeros((HALF, N0), F32)
    for slot in range(DEG):
        lanes = slice(slot * N0, (slot + 1) * N0)
        fine = fine + mm_hot(dvw[:, lanes], hot(N0, index_ref[:, lanes]), (1, 1))
    lanes = slice(E0, E0 + E1)
    mid = mm_hot(dvw[:, lanes], hot(N1, index_ref[:, lanes]), (1, 1))
    lanes = slice(E0 + E1, E0 + E1 + E2)
    top = mm_hot(dvw[:, lanes], hot(N2, index_ref[:, lanes]), (1, 1))

    def rounded(value):
        return value.astype(BF).astype(F32)

    grad_mid = rounded(mid) + mm_hot(rounded(top) / child_top, parent_top, (1, 0), 3) * live_mid
    return self_in + rounded(fine) + mm_hot(grad_mid / child_mid, parent, (1, 0), 3) * live


def fill_pack(core, vw_ref, pack_ref):
    place = pl.ds(pl.multiple_of((1 - core) * QUARTER, QUARTER), QUARTER)
    for index, (start, width) in enumerate(TILES):
        high, low = pieces(vw_ref[place, start : start + width], 2)
        base = C + index * HALF
        pack_ref[base : base + QUARTER, 0:width] = high
        pack_ref[base + QUARTER : base + HALF, 0:width] = low
    pack_ref[C + 2 * HALF : PACK, 768:1024] = jnp.zeros((HALF, 256), BF)


def far_source(pack_ref, index, width):
    base = C + index * HALF
    high = pack_ref[base : base + QUARTER, 0:width].astype(F32)
    return high + pack_ref[base + QUARTER : base + HALF, 0:width].astype(F32)


def fill_grad_kernels(g_ref, source, gk, start, width, rows):
    lanes = slice(start, start + width)
    grad = grad_tile(g_ref, start, width).astype(F32)
    for row in range(rows):
        gk[row * C : (row + 1) * C, lanes] = (grad * source[row : row + 1, :]).astype(BF)


def mlp_backward(
    layer, g_ref, vw_ref, wk_ref, h1_ref, s1_ref, s2_ref, packed_ref, far_ref, edge_ref, own_ref,
    away_ref, gk, g2, g1, wide,
):
    second = second_rows(packed_ref, far_ref, layer)
    for start, width in TILES:
        wide[:, start : start + width] = grad_tile(g_ref, start, width)

    def body(lanes):
        grad = wide[:, lanes].astype(F32)
        source = vw_ref[:, lanes]
        for row in range(HALF):
            gk[row * C : (row + 1) * C, lanes] = (grad * source[row : row + 1, :]).astype(BF)
        two = (s2_ref[:, lanes].astype(F32) * mm(wk_ref[layer], gk[:, lanes])).astype(BF)
        g2[:, lanes] = two
        g1[:, lanes] = (s1_ref[:, lanes].astype(F32) * mm(second, two)).astype(BF)

    halves(body)
    grad_second = mm(h1_ref[...], g2[...], (1, 1))
    grad_first = mm(edge_ref[...], g1[...], (1, 1))
    own_ref[0:128, :] = grad_second[0:128, 0:128]
    own_ref[128:256, :] = grad_second[0:128, 128:256]
    own_ref[272:273, :] = grad_second[256:257, 0:128]
    own_ref[273:274, :] = grad_second[256:257, 128:256]
    own_ref[274:281, :] = grad_first[0:7, 0:128]
    own_ref[281:288, :] = jnp.zeros((7, 128), F32)
    away_ref[0:128, :] = grad_second[128:256, 0:128].astype(BF)
    away_ref[128:256, :] = grad_second[128:256, 128:256].astype(BF)
    tail = jnp.concatenate(
        [grad_second[256:257, 0:128], grad_second[256:257, 128:256], grad_first[0:7, 128:256],
         jnp.zeros((7, 128), F32)],
        axis=0,
    )
    away_ref[256:272, :] = tail.astype(BF)


def kernel_weight_kernel(
    core_ref, *refs
):
    layer_refs = (refs[0:5], refs[5:10])
    bias_ref, joined_hbm, gk, joined_ref, sems = refs[10:]
    mine = pl.ds(pl.multiple_of(core_ref[0] * QUARTER, QUARTER), QUARTER)
    copies = []
    for layer in (1, 0):
        pack_ref, far_ref, vw_ref, h2_ref, h2_far_ref = layer_refs[layer]
        for index, (start, width) in enumerate(TILES):
            source = vw_ref[mine, start : start + width]
            fill_grad_kernels(pack_ref, source, gk, start, width, QUARTER)
        product = mm(h2_ref[...], gk[...], (1, 1))
        for index, (start, width) in enumerate(TILES):
            source = far_source(far_ref, index, width)
            fill_grad_kernels(far_ref, source, gk, start, width, QUARTER)
        product = product + mm(h2_far_ref[...], gk[...], (1, 1))
        for part in range(4):
            for block in range(8):
                joined_ref[layer, part * 8 + block] = product[
                    part * 64 : (part + 1) * 64, block * 128 : (block + 1) * 128
                ].astype(BF)
        copy = pltpu.make_async_copy(
            joined_ref.at[layer], joined_hbm.at[:, layer * 64 : (layer + 1) * 64, :], sems.at[layer]
        )
        copy.start()
        copies.append(copy)
        for block in range(8):
            row = layer * 8 + block
            bias_ref[row : row + 1, :] = product[HID : HID + 1, block * 128 : (block + 1) * 128]
    for copy in copies:
        copy.wait()


def last_node_kernel(
    half_ref, core_ref, state_ref, self_ref, up_own_ref, up_far_ref, cot_ref, pm_ref, pt_ref,
    index_ref, rows_ref, weight_ref, h2_ref, wkt_ref, bias_ref, vw_ref,
    out_ref, own_ref, g_ref, dx_ref, dvw,
):
    fill_pack(core_ref[0], vw_ref, g_ref)
    parent = hot(N1, pm_ref[...])
    parent_top = hot(N2, pt_ref[...])
    live = rows_ref[0:1, :]
    state = state_ref[...]
    pre = mm(self_ref[1].astype(F32).T.astype(BF), state)
    pre = pre + (up_own_ref[...] + up_far_ref[...])
    out_ref[...] = (gelu(pre) * live).astype(BF)
    self_in = node_grads(
        1, half_ref[0], state, pre, cot_ref[...].astype(F32), parent, parent_top, live, self_ref,
        own_ref, g_ref,
    )
    dx_ref[...] = value_grads(
        1, self_in, parent, parent_top, index_ref, rows_ref, weight_ref, h2_ref, wkt_ref, bias_ref,
        g_ref, dvw,
    )


def last_edge_kernel(
    g_ref, vw_ref, wk_ref, h1_ref, s1_ref, s2_ref, packed_ref, far_ref, edge_ref, self_grad_ref,
    own_ref, away_ref, gk, g2, g1, wide,
):
    mlp_backward(
        1, g_ref, vw_ref, wk_ref, h1_ref, s1_ref, s2_ref, packed_ref, far_ref, edge_ref, own_ref,
        away_ref, gk, g2, g1, wide,
    )
    own_ref[256:272, :] = jnp.zeros((16, 128), F32)
    own_ref[288:320, :] = self_grad_ref[288:320, :]


def first_edge_kernel(
    half_ref, core_ref, node_ref, pre_ref, dx_own_ref, dx_far_ref, self_ref, pm_ref, pt_ref, rows_ref,
    vw_ref, wk_ref, h1_ref, s1_ref, s2_ref, packed_ref, far_ref, edge_ref, away1_ref,
    g_ref, self_in_ref, own_ref, away_ref, grad, gk, g2, g1, wide,
):
    fill_pack(core_ref[0], vw_ref, g_ref)
    away_ref[AUG:, :] = away1_ref[...]
    start = pl.multiple_of(half_ref[0] * HALF, HALF)
    grad[pl.ds(start, HALF), :] = dx_own_ref[...]
    grad[pl.ds(HALF - start, HALF), :] = dx_far_ref[...]
    self_in_ref[...] = node_grads(
        0, half_ref[0], node_ref[...], pre_ref[...], grad[...], hot(N1, pm_ref[...]),
        hot(N2, pt_ref[...]), rows_ref[0:1, :], self_ref, own_ref, g_ref,
    )
    own_ref[256:272, :] = jnp.zeros((16, 128), F32)
    mlp_backward(
        0, g_ref, vw_ref, wk_ref, h1_ref, s1_ref, s2_ref, packed_ref, far_ref, edge_ref, own_ref,
        away_ref.at[0:AUG, :], gk, g2, g1, wide,
    )


def first_node_kernel(
    self_in_ref, pm_ref, pt_ref, index_ref, rows_ref, weight_ref, h2_ref, wkt_ref, bias_ref, g_ref,
    dx_ref, dvw,
):
    dx_ref[...] = value_grads(
        0, self_in_ref[...], hot(N1, pm_ref[...]), hot(N2, pt_ref[...]), index_ref, rows_ref,
        weight_ref, h2_ref, wkt_ref, bias_ref, g_ref, dvw,
    )


def join_kernel(core_ref, own0_ref, own1_ref, away_ref, bias_ref, _, out_ref, rows, tail, sem):
    for layer, own_ref in enumerate((own0_ref, own1_ref)):
        base = layer * SMALL
        far = away_ref[layer * AUG : (layer + 1) * AUG, :].astype(F32)
        rows[base : base + 256, :] = own_ref[0:256, :] + far[0:256]
        rows[base + 256 : base + 272, :] = jnp.zeros((16, 128), F32)
        place = pl.ds(pl.multiple_of(base + 256 + core_ref[0] * 8, 8), 8)
        rows[place, :] = bias_ref[layer * 8 : (layer + 1) * 8, :]
        rows[base + 272 : base + 288, :] = own_ref[272:288, :] + far[256:272]
        rows[base + 288 : base + 320, :] = own_ref[288:320, :]
    for block in range(32):
        if block < 2 * SMALL // 32:
            tail[block] = rows[block * 32 : (block + 1) * 32, :].astype(BF)
        else:
            tail[block] = jnp.zeros((32, 128), BF)
    copy = pltpu.make_async_copy(tail, out_ref.at[:, 128:BLOCK, :], sem.at[0])
    copy.start()
    copy.wait()


def sum_kernel(parts_ref, out_ref):
    total = parts_ref[0].astype(F32)
    for peer in range(1, 32):
        total = total + parts_ref[peer].astype(F32)
    total = total.astype(BF)
    for peer in range(32):
        out_ref[peer] = total


def spread_blocks(side_ref, kernel_ref):
    part = pl.program_id(0)
    for block in range(8):
        for layer in range(2):
            kernel_ref[layer, :, block * 128 : (block + 1) * 128] = side_ref[
                part * 8 + block, layer * 64 : (layer + 1) * 64, :
            ].astype(F32)


def spread_own_kernel(core_ref, own_ref, kernel_ref):
    spread_blocks(own_ref, kernel_ref)


def spread_far_kernel(
    core_ref, own_ref, far_ref, _,
    kernel_ref, second_ref, second_bias_ref, first_ref, first_bias_ref, kernel_bias_ref, self_ref,
    rows,
):
    spread_blocks(far_ref, kernel_ref)

    @pl.when(pl.program_id(0) == 0)
    def _():
        spread_small(
            own_ref, far_ref, second_ref, second_bias_ref, first_ref, first_bias_ref,
            kernel_bias_ref, self_ref, rows,
        )


def spread_small(
    own_ref, far_ref, second_ref, second_bias_ref, first_ref, first_bias_ref, kernel_bias_ref,
    self_ref, rows,
):
    for block in range(2 * SMALL // 32):
        rows[block * 32 : (block + 1) * 32, :] = own_ref[block, 128:BLOCK, :].astype(
            F32
        ) + far_ref[block, 128:BLOCK, :].astype(F32)
    for layer in range(2):
        base = layer * SMALL
        second_ref[layer, :, 0:128] = rows[base : base + 128, :]
        second_ref[layer, :, 128:256] = rows[base + 128 : base + 256, :]
        for block in range(16):
            lanes = slice(block * 128, (block + 1) * 128)
            row = base + 256 + block
            kernel_bias_ref[layer : layer + 1, lanes] = rows[row : row + 1, :]
        second_bias_ref[layer : layer + 1, 0:128] = rows[base + 272 : base + 273, :]
        second_bias_ref[layer : layer + 1, 128:256] = rows[base + 273 : base + 274, :]
        for row in range(6):
            first_ref[row, layer : layer + 1, :] = rows[base + 274 + row : base + 275 + row, :]
        first_bias_ref[layer : layer + 1, :] = rows[base + 280 : base + 281, :]
        self_ref[layer, 0:HALF, :] = rows[base + 288 : base + 320, 0:C]
        self_ref[layer, HALF:C, :] = rows[base + 288 : base + 320, C : 2 * C]


def input_kernel(half_ref, own_ref, far_ref, out_ref):
    start = pl.multiple_of(half_ref[0] * HALF, HALF)
    out_ref[pl.ds(start, HALF), :] = own_ref[...]
    out_ref[pl.ds(HALF - start, HALF), :] = far_ref[...]


def vmem_spec():
    return pl.BlockSpec(memory_space=pltpu.VMEM)


def smem_spec():
    return pl.BlockSpec(memory_space=pltpu.SMEM)


def call(kernel, outs, args, scalars=0, scratch=(), us=1, far=0, far_outs=0, aliases=None):
    count = len(args)
    specs = [smem_spec()] * scalars + [vmem_spec()] * (count - scalars - far)
    args = list(args[: count - far]) + [
        pltpu.with_memory_space_constraint(value, pltpu.HBM) for value in args[count - far :]
    ]
    return pl.pallas_call(
        kernel,
        out_shape=[
            pltpu.HBM(*out) if index >= len(outs) - far_outs else jax.ShapeDtypeStruct(*out)
            for index, out in enumerate(outs)
        ],
        in_specs=specs + [pl.BlockSpec(memory_space=pltpu.HBM)] * far,
        out_specs=[
            pl.BlockSpec(memory_space=pltpu.HBM) if index >= len(outs) - far_outs else vmem_spec()
            for index in range(len(outs))
        ],
        scratch_shapes=[
            pltpu.SemaphoreType.DMA(entry[0]) if entry[1] is None else pltpu.VMEM(*entry)
            for entry in scratch
        ],
        input_output_aliases=aliases or {},
        compiler_params=pltpu.CompilerParams(vmem_limit_bytes=VMEM_MIB << 20),
        cost_estimate=pl.CostEstimate(
            flops=us * 1000000000, bytes_accessed=1 << 20, transcendentals=0
        ),
    )(*args)


def swap(value, axis):
    return lax.ppermute(value, axis, [(0, 1), (1, 0)])


def per_device(
    node_input, geometry, counts, parent_mid, parent_top, neighbours_fine, neighbours_mid,
    neighbours_top, w_first, b_first, w_second, b_second, w_kernel, b_kernel, w_self, cotangent,
):
    half = lax.axis_index("tensor").astype(jnp.int32).reshape(1)
    core = lax.axis_index("core").astype(jnp.int32).reshape(1)
    counts, half, core, w_second = lax.optimization_barrier((counts, half, core, w_second))
    pm = parent_mid.reshape(1, N0)
    pt = parent_top.reshape(1, N1)
    node = node_input.T
    wide = (AUG, EDGES)
    edges = (HID, EDGES)
    sources = (HALF, EDGES)

    (packed,) = call(
        pack_kernel,
        [((AUG, HID), BF)],
        [w_second, w_first.transpose(1, 0, 2), b_first],
        scratch=[((2, 128, HID), BF), ((6, 2, 128), BF), ((2, 128), BF), ((16, HID), F32),
                 ((3,), None)],
        far=3,
    )
    far = swap(packed, "tensor")
    (edge, weight, near, rows, wkt, bias_rows, bias_cols, bs_cols, hown, vw0, pm, pt, node) = call(
        prep_kernel,
        [((16, EDGES), BF), ((1, EDGES), F32), ((1, EDGES), jnp.int32), ((8, N0), F32),
         ((2, HALF * C, HID), BF), ((2, HALF, C), BF), ((2, C, HALF), BF), ((HID, 8), F32),
         ((128, EDGES), BF), (sources, F32), ((1, N0), jnp.int32), ((1, N1), jnp.int32),
         ((C, N0), BF)],
        [counts, half, packed, geometry.T, pm, pt, neighbours_fine.T, neighbours_mid.T,
         neighbours_top.T, node, b_kernel, b_second, w_kernel],
        scalars=2,
        far=10,
        scratch=[((3, N0), F32), ((8, N0), jnp.int32), ((8, N1), jnp.int32), ((8, N2), jnp.int32),
                 ((2, HALF * C), BF), ((2, HID), BF), ((2, HID, HALF * C), BF), ((10,), None),
                 ((C, N0 + 256), F32), ((HALF, C), F32)],
        us=4,
    )
    h2_0, up0 = call(
        first_forward_kernel,
        [(wide, BF), ((C, N0), F32)],
        [pm, pt, packed, far, edge, hown, bs_cols, wkt, bias_cols, vw0],
        scratch=[((C, EDGES), F32)],
        us=8,
    )
    up0_far = swap(up0, "tensor")
    h2_0_far = swap(h2_0, "core")

    def mlp(layer, outs):
        return call(
            functools.partial(mlp_kernel, layer), outs, [packed, far, edge, bs_cols], us=5
        )

    h1_1, s1_1, s2_1, h2_1 = mlp(1, [(wide, BF), (edges, BF), (edges, BF), (wide, BF)])
    pre0, state, up1, vw1 = call(
        next_forward_kernel,
        [((C, N0), F32), ((C, N0), BF), ((C, N0), F32), (sources, F32)],
        [half, node, w_self, up0, up0_far, pm, pt, near, rows, weight, h2_1, wkt, bias_cols],
        scalars=1,
        scratch=[((C, N0 + 256), F32), ((C, EDGES), F32)],
        us=5,
    )
    up1_far = swap(up1, "tensor")
    h2_1_far = swap(h2_1, "core")
    up1, edge = lax.optimization_barrier((up1, edge))
    h1_0, s1_0, s2_0 = mlp(0, [(wide, BF), (edges, BF), (edges, BF)])
    out, self_grad1, g1, dx1 = call(
        last_node_kernel,
        [((C, N0), BF), ((SMALL, 128), F32), ((PACK, 1024), BF), ((HALF, N0), F32)],
        [half, core, state, w_self, up1, up1_far, cotangent.T, pm, pt, near, rows, weight, h2_1,
         wkt, bias_rows, vw1],
        scalars=2,
        scratch=[(sources, F32)],
        us=5,
    )
    dx1_far = swap(dx1, "tensor")
    g1_far = swap(g1, "core")
    edge_scratch = [((HALF * C, EDGES), BF), (edges, BF), (edges, BF), ((C, EDGES), BF)]
    own1, away1 = call(
        last_edge_kernel,
        [((SMALL, 128), F32), ((AUG, 128), BF)],
        [g1, vw1, w_kernel, h1_1, s1_1, s2_1, packed, far, edge, self_grad1],
        scratch=edge_scratch,
        us=5,
    )
    g0, self_in0, own0, away = call(
        first_edge_kernel,
        [((PACK, 1024), BF), ((HALF, N0), F32), ((SMALL, 128), F32), ((2 * AUG, 128), BF)],
        [half, core, node, pre0, dx1, dx1_far, w_self, pm, pt, rows, vw0, w_kernel, h1_0, s1_0, s2_0,
         packed, far, edge, away1],
        scalars=2,
        scratch=[((C, N0), F32)] + edge_scratch,
        us=6,
    )
    away_far = swap(away, "tensor")
    g0_far = swap(g0, "core")
    blocks = (32, BLOCK, 128)
    bias, joined = call(
        kernel_weight_kernel,
        [((16, 128), F32), (blocks, BF)],
        [core, g0, g0_far, vw0, h2_0, h2_0_far, g1, g1_far, vw1, h2_1, h2_1_far],
        scalars=1,
        scratch=[((QUARTER * C, EDGES), BF), ((2, 32, 64, 128), BF), ((2,), None)],
        us=8,
        far_outs=1,
    )
    (joined,) = call(
        join_kernel, [(blocks, BF)], [core, own0, own1, away_far, bias, joined],
        scalars=1,
        far=1,
        far_outs=1,
        scratch=[((2 * SMALL, 128), F32), ((32, 32, 128), BF), ((1,), None)],
        aliases={5: 0},
    )
    joined, g0 = lax.optimization_barrier((joined, g0))
    parts = lax.all_to_all(joined, ROW_AXES, 0, 0, tiled=True)
    (dx0,) = call(
        first_node_kernel,
        [((HALF, N0), F32)],
        [self_in0, pm, pt, near, rows, weight, h2_0, wkt, bias_rows, g0],
        scratch=[(sources, F32)],
        us=5,
    )
    (total,) = call(sum_kernel, [(blocks, BF)], [parts])
    dx0_far = swap(dx0, "tensor")
    total, dx0_far = lax.optimization_barrier((total, dx0_far))
    whole = lax.all_to_all(total, ROW_AXES, 0, 0, tiled=True)
    whole_far = swap(whole, "core")
    (input_grad,) = call(
        input_kernel, [((C, N0), F32)], [half, dx0, dx0_far], scalars=1
    )
    grad_shape = jax.ShapeDtypeStruct((2, HID, HALF * C), F32)
    params = pltpu.CompilerParams(vmem_limit_bytes=VMEM_MIB << 20)
    (grad_kernel,) = pl.pallas_call(
        spread_own_kernel,
        out_shape=[grad_shape],
        grid_spec=pltpu.PrefetchScalarGridSpec(
            num_scalar_prefetch=1,
            grid=(4,),
            in_specs=[vmem_spec()],
            out_specs=[
                pl.BlockSpec((2, 64, QUARTER * C), lambda part, core: (0, part, core[0]))
            ],
        ),
        compiler_params=params,
    )(core, whole)
    small_shapes = (
        (2, 128, HID), (2, HID), (6, 2, 128), (2, 128), (2, HALF * C), (2, C, C)
    )
    grad_kernel, grad_second, grad_b_second, grad_first, grad_b_first, grad_b_kernel, grad_self = (
        pl.pallas_call(
            spread_far_kernel,
            out_shape=[grad_shape]
            + [jax.ShapeDtypeStruct(shape, F32) for shape in small_shapes],
            grid_spec=pltpu.PrefetchScalarGridSpec(
                num_scalar_prefetch=1,
                grid=(4,),
                in_specs=[vmem_spec(), vmem_spec(), pl.BlockSpec(memory_space=pl.ANY)],
                out_specs=[
                    pl.BlockSpec((2, 64, QUARTER * C), lambda part, core: (0, part, 1 - core[0]))
                ]
                + [vmem_spec() for _ in small_shapes],
                scratch_shapes=[pltpu.VMEM((2 * SMALL, 128), F32)],
            ),
            input_output_aliases={3: 0},
            compiler_params=params,
        )(core, whole, whole_far, grad_kernel)
    )
    return (
        out.T, input_grad.T, grad_first.transpose(1, 0, 2), grad_b_first, grad_second,
        grad_b_second, grad_kernel, grad_b_kernel, grad_self,
    )


def solution(mesh):
    fine = Mesh(mesh.devices.reshape(2, 4, 4, 2, 2), DP_AXES + ("tensor",))
    dp = DP_AXES
    placed = (
        P(dp, None), P(dp, None), P(dp), P(dp), P(dp), P(dp, None), P(dp, None), P(dp, None),
        P(None, None, "tensor"), P(None, "tensor"), P(None, "tensor", None), P(),
        P(None, None, "tensor"), P(None, "tensor"), P(), P(dp, None),
    )
    return jax.shard_map(
        per_device,
        mesh=fine,
        in_specs=placed,
        out_specs=(
            P(dp, None), P(dp, None), P(None, None, "tensor"), P(None, "tensor"),
            P(None, "tensor", None), P(), P(None, None, "tensor"), P(None, "tensor"), P(),
        ),
        check_vma=False,
    )
```

```python
import functools

import jax
import jax.numpy as jnp
from jax import lax
from jax.experimental import pallas as pl
from jax.experimental.pallas import tpu as pltpu
from jax.sharding import Mesh, PartitionSpec as P

C = 64
HALF = 32
HID = 256
N0, N1, N2 = 256, 64, 16
DEG = 8
E0, E1, E2 = N0 * DEG, N1 * DEG, N2 * DEG
EDGES = 2816
TILES = ((0, 1024), (1024, 1024), (2048, 768))
WIDE = EDGES // 2
PARTS = 2
SMALL = 320
COARSE = N1 + N2
BLOCK = 160
QUARTER = HALF // 2
PACK = C + 3 * HALF
VMEM_MIB = 24
AUG = HID + 16
BF = jnp.bfloat16
F32 = jnp.float32
ROW_AXES = ("yl", "z", "x")
DP_AXES = ROW_AXES + ("core",)


def mm(left, right, contract=(1, 0)):
    return lax.dot_general(
        left, right, (((contract[0],), (contract[1],)), ((), ())), preferred_element_type=F32
    )


def pieces(value, count):
    parts = []
    for _ in range(count):
        part = value.astype(BF)
        parts.append(part)
        value = value - part.astype(F32)
    return parts


def mm_hot(value, hot, contract, count=2):
    rows = value.shape[0]
    product = mm(jnp.concatenate(pieces(value, count), axis=0), hot, contract)
    total = product[:rows]
    for index in range(1, count):
        total = total + product[index * rows : (index + 1) * rows]
    return total


def hot(rows, index):
    lanes = index.shape[1]
    match = lax.broadcasted_iota(jnp.int32, (rows, lanes), 0) == index
    return jnp.where(match, 1.0, 0.0).astype(BF)


def owner_hot(rows, lanes):
    index = lax.broadcasted_iota(jnp.int32, (rows, lanes), 1) & (rows - 1)
    match = lax.broadcasted_iota(jnp.int32, (rows, lanes), 0) == index
    return jnp.where(match, 1.0, 0.0).astype(BF)


def gelu(value):
    inner = value * (0.7978845608028654 + 0.035677408136300125 * (value * value))
    return value * (0.5 + 0.5 * jnp.tanh(inner))


def gelu_both(value):
    square = value * value
    inner = value * (0.7978845608028654 + 0.035677408136300125 * square)
    share = 0.5 + 0.5 * jnp.tanh(inner)
    slope = share + (share * (1.0 - share)) * (
        value * (1.5957691216057308 + 0.21406444881780074 * square)
    )
    return value * share, slope


def level_rows(rows_ref):
    return (
        rows_ref[0:1, :], rows_ref[1:2, 0:N1], rows_ref[3:4, 0:N2], rows_ref[4:5, :]
    )


def gather_sources(state, half, hot_refs, parents_ref, rows_ref, weight_ref, vw_ref, vals):
    live, child_mid, child_top, share = level_rows(rows_ref)
    start = pl.multiple_of(half * HALF, HALF)
    wide = state.astype(F32)
    mid = mm((wide * live).astype(BF), parents_ref[0:N1, :], (1, 1)) / child_mid
    top = mm_hot(wide * share, parents_ref[N1:COARSE, :], (1, 1), 3) / child_top
    vals[:, 0:N0] = wide
    vals[:, N0 : N0 + N1] = mid
    vals[:, N0 + 128 : N0 + 128 + N2] = top
    place = pl.ds(start, HALF)
    values = (
        vals[place, 0:N0], vals[place, N0 : N0 + N1], vals[place, N0 + 128 : N0 + 128 + N2]
    )
    lanes = 0
    for hot_ref, value in zip(hot_refs, values):
        count = hot_ref.shape[1]
        vw_ref[:, lanes : lanes + count] = (
            mm(value.astype(BF), hot_ref[...]) * weight_ref[:, lanes : lanes + count]
        )
        lanes += count
    vw_ref[:, lanes:] = jnp.zeros((HALF, EDGES - lanes), F32)


def halves(body):
    def step(index, carry):
        body(pl.ds(pl.multiple_of(index * WIDE, WIDE), WIDE))
        return carry

    lax.fori_loop(0, 2, step, 0)


def channel_parts(body, parts):
    def step(index, carry):
        rows, channels = HALF * C // parts, HALF // parts
        body(
            pl.ds(pl.multiple_of(index * rows, rows), rows),
            pl.ds(pl.multiple_of(index * channels, channels), channels),
        )
        return carry

    lax.fori_loop(0, parts, step, 0)


def message_pass(
    layer, h2_ref, parents_ref, owner_ref, wkt_ref, bias_ref, vw_ref, up_ref, msg, *kept_refs
):
    bias = bias_ref[layer]
    bias = jnp.concatenate([bias, bias], axis=1)
    for start, width in TILES:
        lanes = slice(start, start + width)
        msg[:, lanes] = mm(bias, jnp.concatenate(pieces(vw_ref[:, lanes], 2), axis=0))

    def part(rows, channels):
        for start, width in TILES:
            lanes = slice(start, start + width)
            source = vw_ref[channels, lanes]
            kernels = mm(wkt_ref[layer, rows, :], h2_ref[0:HID, lanes])
            for kept_ref in kept_refs:
                kept_ref[rows, lanes] = kernels.astype(BF)
            total = msg[:, lanes]
            for channel in range(HALF // PARTS):
                total = total + (
                    kernels[channel * C : (channel + 1) * C] * source[channel : channel + 1, :]
                )
            msg[:, lanes] = total

    channel_parts(part, PARTS)
    total_fine = msg[:, 0:N0]
    for slot in range(1, DEG):
        total_fine = total_fine + msg[:, slot * N0 : (slot + 1) * N0]
    coarse = mm_hot(msg[:, E0:EDGES], owner_ref[...], (1, 1))
    up_ref[...] = total_fine + mm_hot(coarse, parents_ref[...], (1, 0))


def first_columns(packed_ref, layer):
    return packed_ref[HID : HID + 16, layer * 128 : (layer + 1) * 128].astype(F32).T.astype(BF)


def second_rows(packed_ref, far_ref, layer):
    rows = slice(layer * 128, (layer + 1) * 128)
    return jnp.concatenate([packed_ref[rows, :], far_ref[rows, :]], axis=0)


def ones_rows(width):
    return jnp.where(lax.broadcasted_iota(jnp.int32, (16, width), 0) == 0, 1.0, 0.0).astype(BF)


def pack_kernel(second_ref, first_ref, bias_ref, packed_ref, second, first, bias, rows, sems):
    copies = [
        pltpu.make_async_copy(source, target, sems.at[index])
        for index, (source, target) in enumerate(
            ((second_ref, second), (first_ref, first), (bias_ref, bias))
        )
    ]
    for copy in copies:
        copy.start()
    rows[...] = jnp.zeros_like(rows)
    for copy in copies:
        copy.wait()
    packed_ref[0:128, :] = second[0]
    packed_ref[128:256, :] = second[1]
    bias_rows = bias[...].astype(F32)
    for layer in range(2):
        lanes = slice(layer * 128, (layer + 1) * 128)
        for row in range(6):
            rows[row : row + 1, lanes] = first[row].astype(F32)[layer : layer + 1]
        rows[6:7, lanes] = bias_rows[layer : layer + 1]
    packed_ref[256:272, :] = rows[...].astype(BF)


def prep_kernel(
    count_ref, half_ref, packed_ref, geometry_hbm, pm_hbm, pt_hbm, near0_hbm, near1_hbm, near2_hbm,
    node_hbm, bk_hbm, bs_hbm, wk_hbm,
    edge_ref, weight_ref, hot0_ref, hot1_ref, hot2_ref, parents_ref, owner_ref, rows_ref, wkt_ref,
    bias_rows_ref, bias_cols_ref, bs_cols_ref, hown_ref, vw_ref, node_ref,
    index_ref, pm_ref, pt_ref, geometry_ref, near0_ref, near1_ref, near2_ref, bk_ref, bs_ref, wk_ref, sems, vals, bias_rows,
):
    copies = [
        pltpu.make_async_copy(source, target, sems.at[index])
        for index, (source, target) in enumerate(
            (
                (geometry_hbm, geometry_ref), (pm_hbm, pm_ref), (pt_hbm, pt_ref),
                (near0_hbm, near0_ref), (near1_hbm, near1_ref), (near2_hbm, near2_ref),
                (node_hbm, node_ref), (bk_hbm, bk_ref), (bs_hbm, bs_ref), (wk_hbm, wk_ref),
            )
        )
    ]
    for copy in copies:
        copy.start()
    for copy in copies[:-1]:
        copy.wait()
    live = jnp.where(
        lax.broadcasted_iota(jnp.int32, (1, N0), 1) < count_ref[0], 1.0, 0.0
    ).astype(F32)
    parent = hot(N1, pm_ref[...])
    parent_top = hot(N2, pt_ref[...])
    live8 = jnp.broadcast_to(live, (16, N0))
    child_mid = mm(live8.astype(BF), parent, (1, 1))
    live_mid = jnp.where(child_mid > 0.5, 1.0, 0.0)
    child_top = mm(live_mid.astype(BF), parent_top, (1, 1))
    live_top = jnp.where(child_top > 0.5, 1.0, 0.0)
    child_mid = jnp.maximum(child_mid, 1.0)
    child_top = jnp.maximum(child_top, 1.0)
    rows_ref[...] = jnp.zeros_like(rows_ref)
    rows_ref[0:1, :] = live
    rows_ref[1:2, 0:N1] = child_mid[0:1]
    rows_ref[2:3, 0:N1] = live_mid[0:1]
    rows_ref[3:4, 0:N2] = child_top[0:1]
    share = mm_hot(live_mid / child_mid, parent, (1, 0), 3)[0:1] * live
    rows_ref[4:5, :] = share
    parents_ref[0:N1, :] = parent
    composite = mm(parent_top, parent).astype(BF)
    parents_ref[N1:COARSE, :] = composite
    row = lax.broadcasted_iota(jnp.int32, owner_ref.shape, 0)
    lane = lax.broadcasted_iota(jnp.int32, owner_ref.shape, 1)
    mid_own = (lane < E1) & (row == (lane & (N1 - 1)))
    top_own = (lane >= E1) & (lane < E1 + E2) & (row == N1 + (lane & (N2 - 1)))
    owner_ref[...] = jnp.where(mid_own | top_own, 1.0, 0.0).astype(BF)
    index_ref[...] = jnp.zeros_like(index_ref)
    for slot in range(DEG):
        row = slice(slot, slot + 1)
        index_ref[:, slot * N0 : (slot + 1) * N0] = near0_ref[row, :]
        index_ref[:, E0 + slot * N1 : E0 + (slot + 1) * N1] = near1_ref[row, :]
        start = E0 + E1 + slot * N2
        index_ref[:, start : start + N2] = near2_ref[row, :]
    vals[0:16, 0:N0] = jnp.zeros((16, N0), F32)
    vals[0:3, 0:N0] = geometry_ref[...]
    coords = vals[0:16, 0:N0]
    coords_mid = mm_hot(coords * live, parent, (1, 1), 3) / child_mid
    coords_top = mm_hot(coords * share, composite, (1, 1), 3) / child_top
    lane_row = lax.broadcasted_iota(jnp.int32, (16, 1), 0)

    def with_live(values, live_row):
        return jnp.where(lane_row == 3, live_row, values).astype(BF)

    fine_rows = with_live(coords, live)
    mid_rows = with_live(coords_mid, live_mid[0:1])
    top_rows = with_live(coords_top, live_top[0:1])

    def edges(own, near):
        low = jnp.where(lane_row < 3, own, 0.0)
        high = pltpu.roll(jnp.where(lane_row < 3, near, 0.0), 3, 0)
        return jnp.where(lane_row == 6, 1.0, low + high).astype(BF)

    fine = fine_rows.astype(F32)
    masks = []
    for slot in range(DEG):
        lanes = slice(slot * N0, (slot + 1) * N0)
        hot0_ref[:, lanes] = hot(N0, index_ref[:, lanes])
        near = mm(fine_rows, hot0_ref[:, lanes])
        edge_ref[:, lanes] = edges(fine, near)
        masks.append(live * near[3:4])
    total = masks[0]
    for mask in masks[1:]:
        total = total + mask
    total = jnp.maximum(total, 1.0)
    for slot in range(DEG):
        weight_ref[:, slot * N0 : (slot + 1) * N0] = masks[slot] / total

    def small_level(values, rows, start, lanes, hot_ref):
        own = mm(values, owner_hot(rows, lanes))
        hot_ref[...] = hot(rows, index_ref[:, start : start + lanes])
        near = mm(values, hot_ref[...])
        edge_ref[:, start : start + lanes] = edges(own, near)
        mask = own * near
        fold = jnp.where(
            (lax.broadcasted_iota(jnp.int32, (lanes, lanes), 0) & (rows - 1))
            == (lax.broadcasted_iota(jnp.int32, (lanes, lanes), 1) & (rows - 1)),
            1.0,
            0.0,
        ).astype(BF)
        total = jnp.maximum(mm(mask.astype(BF), fold), 1.0)
        weight_ref[:, start : start + lanes] = mask[3:4] / total[3:4]

    small_level(mid_rows, N1, E0, E1, hot1_ref)
    small_level(top_rows, N2, E0 + E1, E2, hot2_ref)
    rest = E0 + E1 + E2
    edge_ref[:, rest:] = jnp.zeros((16, EDGES - rest), BF)
    weight_ref[:, rest:] = jnp.zeros((1, EDGES - rest), F32)
    gather_sources(
        node_ref[...], half_ref[0], (hot0_ref, hot1_ref, hot2_ref), parents_ref, rows_ref,
        weight_ref, vw_ref, vals,
    )
    bias = bk_ref[...].astype(F32)
    copies[-1].wait()
    for layer in range(2):
        for part in range(8):
            wkt_ref[layer, part * 256 : (part + 1) * 256, :] = wk_ref[
                layer, :, part * 256 : (part + 1) * 256
            ].T
        for row in range(HALF):
            bias_rows[row : row + 1, :] = bias[layer : layer + 1, row * C : (row + 1) * C]
        bias_rows_ref[layer] = bias_rows[...].astype(BF)
        bias_cols_ref[layer] = bias_rows[...].T.astype(BF)
    hown_ref[...] = gelu(mm(first_columns(packed_ref, 0), edge_ref[...])).astype(BF)
    second_bias = jnp.concatenate([bs_ref[...].astype(F32), jnp.zeros((6, HID), F32)], axis=0)
    bs_cols_ref[...] = second_bias.T


def first_forward_kernel(
    parents_ref, owner_ref, packed_ref, far_ref, edge_ref, hown_ref, bs_ref, wkt_ref, bias_ref, vw_ref,
    h2_ref, up_ref, msg,
):
    second = second_rows(packed_ref, far_ref, 0).T
    first = first_columns(far_ref, 0)
    bias = bs_ref[:, 0:1]

    def body(lanes):
        away = gelu(mm(first, edge_ref[:, lanes])).astype(BF)
        one = jnp.concatenate([hown_ref[:, lanes], away], axis=0)
        h2_ref[0:HID, lanes] = gelu(mm(second, one) + bias).astype(BF)

    halves(body)
    h2_ref[HID:AUG, :] = ones_rows(EDGES)
    message_pass(
        0, h2_ref, parents_ref, owner_ref, wkt_ref, bias_ref, vw_ref, up_ref, msg,
    )


def mlp_kernel(layer, packed_ref, far_ref, edge_ref, bs_ref, h1_ref, s1_ref, s2_ref, *h2_refs):
    second = second_rows(packed_ref, far_ref, layer).T
    first = jnp.concatenate(
        [first_columns(packed_ref, layer), first_columns(far_ref, layer)], axis=0
    )
    bias = bs_ref[:, layer : layer + 1]

    def body(lanes):
        value, slope = gelu_both(mm(first, edge_ref[:, lanes]))
        one = value.astype(BF)
        h1_ref[0:HID, lanes] = one
        s1_ref[:, lanes] = slope.astype(BF)
        value, slope = gelu_both(mm(second, one) + bias)
        s2_ref[:, lanes] = slope.astype(BF)
        for h2_ref in h2_refs:
            h2_ref[0:HID, lanes] = value.astype(BF)

    halves(body)
    for ref in (h1_ref,) + h2_refs:
        ref[HID:AUG, :] = ones_rows(EDGES)


def next_forward_kernel(
    half_ref, node_ref, self_ref, up_own_ref, up_far_ref, hot0_ref, hot1_ref, hot2_ref, parents_ref,
    owner_ref, rows_ref, weight_ref, h2_ref, wkt_ref, bias_ref,
    pre_ref, state_ref, up_ref, vw_ref, kept_ref, vals, msg,
):
    pre = mm(self_ref[0].astype(F32).T.astype(BF), node_ref[...])
    pre = pre + (up_own_ref[...] + up_far_ref[...])
    pre_ref[...] = pre
    state = (gelu(pre) * rows_ref[0:1, :]).astype(BF)
    state_ref[...] = state
    gather_sources(
        state, half_ref[0], (hot0_ref, hot1_ref, hot2_ref), parents_ref, rows_ref, weight_ref,
        vw_ref, vals,
    )
    message_pass(
        1, h2_ref, parents_ref, owner_ref, wkt_ref, bias_ref, vw_ref, up_ref, msg, kept_ref,
    )


def node_grads(
    layer, half, h, pre, grad, parents_ref, owner_ref, live, self_ref, own_ref, g_ref
):
    start = pl.multiple_of(half * HALF, HALF)
    _, slope = gelu_both(pre)
    grad_pre = slope * (live * grad)
    high, low = pieces(grad_pre, 2)
    grad_self = mm(h, high, (1, 1)) + mm(h, low, (1, 1))
    own_ref[288:320, 0:C] = grad_self[0:HALF]
    own_ref[288:320, C : 2 * C] = grad_self[HALF:C]
    self_half = self_ref[layer, pl.ds(start, HALF), :]
    self_in = mm(self_half, high) + mm(self_half, low)
    coarse = mm_hot(grad_pre, parents_ref[...], (1, 1), 3).astype(BF)
    g_ref[0:C, 0:N0] = grad_pre.astype(BF)
    g_ref[0:C, N0:] = mm(coarse, owner_ref[...]).astype(BF)
    return self_in


def grad_tile(g_ref, start, width):
    if start < E0:
        return jnp.concatenate([g_ref[0:C, 0:N0]] * (width // N0), axis=1)
    return g_ref[0:C, N0 : N0 + width]


def source_grads(self_in, hot_refs, parents_ref, rows_ref, dvw):
    live, child_mid, child_top, share = level_rows(rows_ref)
    sums = []
    lanes = 0
    for hot_ref in hot_refs:
        count = hot_ref.shape[1]
        total = mm_hot(dvw[:, lanes : lanes + count], hot_ref[...], (1, 1))
        sums.append(total.astype(BF).astype(F32))
        lanes += count
    fine, mid, top = sums
    return (
        self_in
        + fine
        + mm_hot(mid / child_mid, parents_ref[0:N1, :], (1, 0), 3) * live
        + mm_hot(top / child_top, parents_ref[N1:COARSE, :], (1, 0), 3) * share
    )


def fill_pack(core, vw_ref, pack_ref):
    place = pl.ds(pl.multiple_of((1 - core) * QUARTER, QUARTER), QUARTER)
    for index, (start, width) in enumerate(TILES):
        high, low = pieces(vw_ref[place, start : start + width], 2)
        base = C + index * HALF
        pack_ref[base : base + QUARTER, 0:width] = high
        pack_ref[base + QUARTER : base + HALF, 0:width] = low
    pack_ref[C + 2 * HALF : PACK, 768:1024] = jnp.zeros((HALF, 256), BF)


def far_source(pack_ref, index, width):
    base = C + index * HALF
    high = pack_ref[base : base + QUARTER, 0:width].astype(F32)
    return high + pack_ref[base + QUARTER : base + HALF, 0:width].astype(F32)


def fill_grad_kernels(g_ref, source, gk, start, width, rows):
    lanes = slice(start, start + width)
    grad = grad_tile(g_ref, start, width).astype(F32)
    for row in range(rows):
        gk[row * C : (row + 1) * C, lanes] = (grad * source[row : row + 1, :]).astype(BF)


def mlp_backward(
    layer, g_ref, vw_ref, wk_ref, h1_ref, s1_ref, s2_ref, packed_ref, far_ref, edge_ref, own_ref,
    away_ref, gk, g2, g1, wide,
):
    second = second_rows(packed_ref, far_ref, layer)
    for start, width in TILES:
        wide[:, start : start + width] = grad_tile(g_ref, start, width)

    def body(lanes):
        grad = wide[:, lanes].astype(F32)
        source = vw_ref[:, lanes]
        for row in range(HALF):
            gk[row * C : (row + 1) * C, lanes] = (grad * source[row : row + 1, :]).astype(BF)
        two = (s2_ref[:, lanes].astype(F32) * mm(wk_ref[layer], gk[:, lanes])).astype(BF)
        g2[:, lanes] = two
        g1[:, lanes] = (s1_ref[:, lanes].astype(F32) * mm(second, two)).astype(BF)

    halves(body)
    grad_second = mm(h1_ref[...], g2[...], (1, 1))
    grad_first = mm(edge_ref[...], g1[...], (1, 1))
    own_ref[0:128, :] = grad_second[0:128, 0:128]
    own_ref[128:256, :] = grad_second[0:128, 128:256]
    own_ref[272:273, :] = grad_second[256:257, 0:128]
    own_ref[273:274, :] = grad_second[256:257, 128:256]
    own_ref[274:281, :] = grad_first[0:7, 0:128]
    own_ref[281:288, :] = jnp.zeros((7, 128), F32)
    away_ref[0:128, :] = grad_second[128:256, 0:128].astype(BF)
    away_ref[128:256, :] = grad_second[128:256, 128:256].astype(BF)
    tail = jnp.concatenate(
        [grad_second[256:257, 0:128], grad_second[256:257, 128:256], grad_first[0:7, 128:256],
         jnp.zeros((7, 128), F32)],
        axis=0,
    )
    away_ref[256:272, :] = tail.astype(BF)


def kernel_weight_kernel(
    core_ref, *refs
):
    layer_refs = (refs[0:5], refs[5:10])
    bias_ref, joined_hbm, gk, joined_ref, sems = refs[10:]
    mine = pl.ds(pl.multiple_of(core_ref[0] * QUARTER, QUARTER), QUARTER)
    copies = []
    for layer in (1, 0):
        pack_ref, far_ref, vw_ref, h2_ref, h2_far_ref = layer_refs[layer]
        for index, (start, width) in enumerate(TILES):
            source = vw_ref[mine, start : start + width]
            fill_grad_kernels(pack_ref, source, gk, start, width, QUARTER)
        product = mm(h2_ref[...], gk[...], (1, 1))
        for index, (start, width) in enumerate(TILES):
            source = far_source(far_ref, index, width)
            fill_grad_kernels(far_ref, source, gk, start, width, QUARTER)
        product = product + mm(h2_far_ref[...], gk[...], (1, 1))
        for part in range(4):
            for block in range(8):
                joined_ref[layer, part * 8 + block] = product[
                    part * 64 : (part + 1) * 64, block * 128 : (block + 1) * 128
                ].astype(BF)
        copy = pltpu.make_async_copy(
            joined_ref.at[layer], joined_hbm.at[:, layer * 64 : (layer + 1) * 64, :], sems.at[layer]
        )
        copy.start()
        copies.append(copy)
        for block in range(8):
            row = layer * 8 + block
            bias_ref[row : row + 1, :] = product[HID : HID + 1, block * 128 : (block + 1) * 128]
    for copy in copies:
        copy.wait()


def last_node_kernel(
    half_ref, core_ref, state_ref, self_ref, up_own_ref, up_far_ref, cot_ref, hot0_ref, hot1_ref,
    hot2_ref, parents_ref, owner_ref, rows_ref, weight_ref, kept_ref, bias_ref, vw_ref,
    out_ref, own_ref, g_ref, dx_ref, dvw, wide,
):
    fill_pack(core_ref[0], vw_ref, g_ref)
    live = rows_ref[0:1, :]
    state = state_ref[...]
    pre = mm(self_ref[1].astype(F32).T.astype(BF), state)
    pre = pre + (up_own_ref[...] + up_far_ref[...])
    out_ref[...] = (gelu(pre) * live).astype(BF)
    self_in = node_grads(
        1, half_ref[0], state, pre, cot_ref[...].astype(F32), parents_ref, owner_ref, live,
        self_ref, own_ref, g_ref,
    )
    for start, width in TILES:
        wide[:, start : start + width] = grad_tile(g_ref, start, width)
    offset = mm(bias_ref[1], wide[...])
    for start, width in TILES:
        lanes = slice(start, start + width)
        grad = wide[:, lanes].astype(F32)
        for part in range(4):
            channels = slice(part * 8, (part + 1) * 8)
            kernels = kept_ref[part * 512 : (part + 1) * 512, lanes].astype(F32)
            total = jnp.sum(kernels.reshape(8, C, width) * grad[None], axis=1)
            dvw[channels, lanes] = (total + offset[channels, lanes]) * weight_ref[:, lanes]
    dx_ref[...] = source_grads(
        self_in, (hot0_ref, hot1_ref, hot2_ref), parents_ref, rows_ref, dvw
    )


def last_edge_kernel(
    g_ref, vw_ref, wk_ref, h1_ref, s1_ref, s2_ref, packed_ref, far_ref, edge_ref, self_grad_ref,
    own_ref, away_ref, gk, g2, g1, wide,
):
    mlp_backward(
        1, g_ref, vw_ref, wk_ref, h1_ref, s1_ref, s2_ref, packed_ref, far_ref, edge_ref, own_ref,
        away_ref, gk, g2, g1, wide,
    )
    own_ref[256:272, :] = jnp.zeros((16, 128), F32)
    own_ref[288:320, :] = self_grad_ref[288:320, :]


def first_edge_kernel(
    half_ref, core_ref, node_ref, pre_ref, dx_own_ref, dx_far_ref, self_ref, parents_ref, owner_ref,
    rows_ref,
    vw_ref, wk_ref, h1_ref, s1_ref, s2_ref, packed_ref, far_ref, edge_ref, away1_ref,
    g_ref, self_in_ref, own_ref, away_ref, grad, gk, g2, g1, wide,
):
    fill_pack(core_ref[0], vw_ref, g_ref)
    away_ref[AUG:, :] = away1_ref[...]
    start = pl.multiple_of(half_ref[0] * HALF, HALF)
    grad[pl.ds(start, HALF), :] = dx_own_ref[...]
    grad[pl.ds(HALF - start, HALF), :] = dx_far_ref[...]
    self_in_ref[...] = node_grads(
        0, half_ref[0], node_ref[...], pre_ref[...], grad[...], parents_ref, owner_ref,
        rows_ref[0:1, :], self_ref, own_ref, g_ref,
    )
    own_ref[256:272, :] = jnp.zeros((16, 128), F32)
    mlp_backward(
        0, g_ref, vw_ref, wk_ref, h1_ref, s1_ref, s2_ref, packed_ref, far_ref, edge_ref, own_ref,
        away_ref.at[0:AUG, :], gk, g2, g1, wide,
    )


def first_node_kernel(
    self_in_ref, hot0_ref, hot1_ref, hot2_ref, parents_ref, rows_ref, weight_ref, h2_ref, wkt_ref,
    bias_ref, g_ref,
    dx_ref, dvw,
):

    def part(rows, channels):
        for start, width in TILES:
            lanes = slice(start, start + width)
            grad = grad_tile(g_ref, start, width)
            offset = mm(bias_ref[0, channels, :], grad)
            kernels = mm(wkt_ref[0, rows, :], h2_ref[0:HID, lanes])
            product = kernels.reshape(HALF // PARTS, C, width) * grad.astype(F32)[None]
            dvw[channels, lanes] = (jnp.sum(product, axis=1) + offset) * weight_ref[:, lanes]

    channel_parts(part, PARTS)
    dx_ref[...] = source_grads(
        self_in_ref[...], (hot0_ref, hot1_ref, hot2_ref), parents_ref, rows_ref, dvw
    )


def join_kernel(core_ref, own0_ref, own1_ref, away_ref, bias_ref, _, out_ref, rows, tail, sem):
    for layer, own_ref in enumerate((own0_ref, own1_ref)):
        base = layer * SMALL
        far = away_ref[layer * AUG : (layer + 1) * AUG, :].astype(F32)
        rows[base : base + 256, :] = own_ref[0:256, :] + far[0:256]
        rows[base + 256 : base + 272, :] = jnp.zeros((16, 128), F32)
        place = pl.ds(pl.multiple_of(base + 256 + core_ref[0] * 8, 8), 8)
        rows[place, :] = bias_ref[layer * 8 : (layer + 1) * 8, :]
        rows[base + 272 : base + 288, :] = own_ref[272:288, :] + far[256:272]
        rows[base + 288 : base + 320, :] = own_ref[288:320, :]
    for block in range(32):
        if block < 2 * SMALL // 32:
            tail[block] = rows[block * 32 : (block + 1) * 32, :].astype(BF)
        else:
            tail[block] = jnp.zeros((32, 128), BF)
    copy = pltpu.make_async_copy(tail, out_ref.at[:, 128:BLOCK, :], sem.at[0])
    copy.start()
    copy.wait()


def sum_kernel(parts_ref, out_ref):
    total = parts_ref[0].astype(F32)
    for peer in range(1, 32):
        total = total + parts_ref[peer].astype(F32)
    total = total.astype(BF)
    for peer in range(32):
        out_ref[peer] = total


def spread_blocks(side_ref, kernel_ref):
    part = pl.program_id(0)
    for block in range(8):
        for layer in range(2):
            kernel_ref[layer, :, block * 128 : (block + 1) * 128] = side_ref[
                part * 8 + block, layer * 64 : (layer + 1) * 64, :
            ].astype(F32)


def spread_own_kernel(core_ref, own_ref, kernel_ref):
    spread_blocks(own_ref, kernel_ref)


def spread_far_kernel(
    core_ref, own_ref, far_ref, _,
    kernel_ref, second_ref, second_bias_ref, first_ref, first_bias_ref, kernel_bias_ref, self_ref,
    rows,
):
    spread_blocks(far_ref, kernel_ref)

    @pl.when(pl.program_id(0) == 0)
    def _():
        spread_small(
            own_ref, far_ref, second_ref, second_bias_ref, first_ref, first_bias_ref,
            kernel_bias_ref, self_ref, rows,
        )


def spread_small(
    own_ref, far_ref, second_ref, second_bias_ref, first_ref, first_bias_ref, kernel_bias_ref,
    self_ref, rows,
):
    for block in range(2 * SMALL // 32):
        rows[block * 32 : (block + 1) * 32, :] = own_ref[block, 128:BLOCK, :].astype(
            F32
        ) + far_ref[block, 128:BLOCK, :].astype(F32)
    for layer in range(2):
        base = layer * SMALL
        second_ref[layer, :, 0:128] = rows[base : base + 128, :]
        second_ref[layer, :, 128:256] = rows[base + 128 : base + 256, :]
        for block in range(16):
            lanes = slice(block * 128, (block + 1) * 128)
            row = base + 256 + block
            kernel_bias_ref[layer : layer + 1, lanes] = rows[row : row + 1, :]
        second_bias_ref[layer : layer + 1, 0:128] = rows[base + 272 : base + 273, :]
        second_bias_ref[layer : layer + 1, 128:256] = rows[base + 273 : base + 274, :]
        for row in range(6):
            first_ref[row, layer : layer + 1, :] = rows[base + 274 + row : base + 275 + row, :]
        first_bias_ref[layer : layer + 1, :] = rows[base + 280 : base + 281, :]
        self_ref[layer, 0:HALF, :] = rows[base + 288 : base + 320, 0:C]
        self_ref[layer, HALF:C, :] = rows[base + 288 : base + 320, C : 2 * C]


def input_kernel(half_ref, own_ref, far_ref, out_ref):
    start = pl.multiple_of(half_ref[0] * HALF, HALF)
    out_ref[pl.ds(start, HALF), :] = own_ref[...]
    out_ref[pl.ds(HALF - start, HALF), :] = far_ref[...]


def vmem_spec():
    return pl.BlockSpec(memory_space=pltpu.VMEM)


def smem_spec():
    return pl.BlockSpec(memory_space=pltpu.SMEM)


def call(kernel, outs, args, scalars=0, scratch=(), us=1, far=0, far_outs=0, aliases=None):
    count = len(args)
    specs = [smem_spec()] * scalars + [vmem_spec()] * (count - scalars - far)
    args = list(args[: count - far]) + [
        pltpu.with_memory_space_constraint(value, pltpu.HBM) for value in args[count - far :]
    ]
    return pl.pallas_call(
        kernel,
        out_shape=[
            pltpu.HBM(*out) if index >= len(outs) - far_outs else jax.ShapeDtypeStruct(*out)
            for index, out in enumerate(outs)
        ],
        in_specs=specs + [pl.BlockSpec(memory_space=pltpu.HBM)] * far,
        out_specs=[
            pl.BlockSpec(memory_space=pltpu.HBM) if index >= len(outs) - far_outs else vmem_spec()
            for index in range(len(outs))
        ],
        scratch_shapes=[
            pltpu.SemaphoreType.DMA(entry[0]) if entry[1] is None else pltpu.VMEM(*entry)
            for entry in scratch
        ],
        input_output_aliases=aliases or {},
        compiler_params=pltpu.CompilerParams(vmem_limit_bytes=VMEM_MIB << 20),
        cost_estimate=pl.CostEstimate(
            flops=us * 1000000000, bytes_accessed=1 << 20, transcendentals=0
        ),
    )(*args)


def swap(value, axis):
    return lax.ppermute(value, axis, [(0, 1), (1, 0)])


def per_device(
    node_input, geometry, counts, parent_mid, parent_top, neighbours_fine, neighbours_mid,
    neighbours_top, w_first, b_first, w_second, b_second, w_kernel, b_kernel, w_self, cotangent,
):
    half = lax.axis_index("tensor").astype(jnp.int32).reshape(1)
    core = lax.axis_index("core").astype(jnp.int32).reshape(1)
    counts, half, core, w_second = lax.optimization_barrier((counts, half, core, w_second))
    pm = parent_mid.reshape(1, N0)
    pt = parent_top.reshape(1, N1)
    node = node_input.T
    wide = (AUG, EDGES)
    edges = (HID, EDGES)
    sources = (HALF, EDGES)

    (packed,) = call(
        pack_kernel,
        [((AUG, HID), BF)],
        [w_second, w_first.transpose(1, 0, 2), b_first],
        scratch=[((2, 128, HID), BF), ((6, 2, 128), BF), ((2, 128), BF), ((16, HID), F32),
                 ((3,), None)],
        far=3,
    )
    far = swap(packed, "tensor")
    (
        edge, weight, hot0, hot1, hot2, parents, owner, rows, wkt, bias_rows, bias_cols, bs_cols,
        hown, vw0, node,
    ) = call(
        prep_kernel,
        [((16, EDGES), BF), ((1, EDGES), F32), ((N0, E0), BF), ((N1, E1), BF), ((N2, E2), BF),
         ((COARSE, N0), BF), ((COARSE, EDGES - E0), BF), ((8, N0), F32), ((2, HALF * C, HID), BF), ((2, HALF, C), BF), ((2, C, HALF), BF), ((HID, 8), F32),
         ((128, EDGES), BF), (sources, F32), ((C, N0), BF)],
        [counts, half, packed, geometry.T, pm, pt, neighbours_fine.T, neighbours_mid.T,
         neighbours_top.T, node, b_kernel, b_second, w_kernel],
        scalars=2,
        far=10,
        scratch=[((1, EDGES), jnp.int32), ((1, N0), jnp.int32), ((1, N1), jnp.int32),
                 ((3, N0), F32), ((8, N0), jnp.int32), ((8, N1), jnp.int32), ((8, N2), jnp.int32),
                 ((2, HALF * C), BF), ((2, HID), BF), ((2, HID, HALF * C), BF), ((10,), None),
                 ((C, N0 + 256), F32), ((HALF, C), F32)],
        us=4,
    )
    h2_0, up0 = call(
        first_forward_kernel,
        [(wide, BF), ((C, N0), F32)],
        [parents, owner, packed, far, edge, hown, bs_cols, wkt, bias_cols, vw0],
        scratch=[((C, EDGES), F32)],
        us=8,
    )
    up0_far = swap(up0, "tensor")
    h2_0_far = swap(h2_0, "core")

    def mlp(layer, outs):
        return call(
            functools.partial(mlp_kernel, layer), outs, [packed, far, edge, bs_cols], us=5
        )

    h1_1, s1_1, s2_1, h2_1 = mlp(1, [(wide, BF), (edges, BF), (edges, BF), (wide, BF)])
    pre0, state, up1, vw1, kept = call(
        next_forward_kernel,
        [((C, N0), F32), ((C, N0), BF), ((C, N0), F32), (sources, F32), ((HALF * C, EDGES), BF)],
        [half, node, w_self, up0, up0_far, hot0, hot1, hot2, parents, owner, rows, weight, h2_1, wkt,
         bias_cols],
        scalars=1,
        scratch=[((C, N0 + 256), F32), ((C, EDGES), F32)],
        us=5,
    )
    up1_far = swap(up1, "tensor")
    h2_1_far = swap(h2_1, "core")
    up1, edge = lax.optimization_barrier((up1, edge))
    h1_0, s1_0, s2_0 = mlp(0, [(wide, BF), (edges, BF), (edges, BF)])
    out, self_grad1, g1, dx1 = call(
        last_node_kernel,
        [((C, N0), BF), ((SMALL, 128), F32), ((PACK, 1024), BF), ((HALF, N0), F32)],
        [half, core, state, w_self, up1, up1_far, cotangent.T, hot0, hot1, hot2, parents, owner,
         rows, weight, kept, bias_rows, vw1],
        scalars=2,
        scratch=[(sources, F32), ((C, EDGES), BF)],
        us=5,
    )
    dx1_far = swap(dx1, "tensor")
    g1_far = swap(g1, "core")
    edge_scratch = [((HALF * C, EDGES), BF), (edges, BF), (edges, BF), ((C, EDGES), BF)]
    own1, away1 = call(
        last_edge_kernel,
        [((SMALL, 128), F32), ((AUG, 128), BF)],
        [g1, vw1, w_kernel, h1_1, s1_1, s2_1, packed, far, edge, self_grad1],
        scratch=edge_scratch,
        us=5,
    )
    g0, self_in0, own0, away = call(
        first_edge_kernel,
        [((PACK, 1024), BF), ((HALF, N0), F32), ((SMALL, 128), F32), ((2 * AUG, 128), BF)],
        [half, core, node, pre0, dx1, dx1_far, w_self, parents, owner, rows, vw0, w_kernel, h1_0, s1_0, s2_0,
         packed, far, edge, away1],
        scalars=2,
        scratch=[((C, N0), F32)] + edge_scratch,
        us=6,
    )
    away_far = swap(away, "tensor")
    g0_far = swap(g0, "core")
    blocks = (32, BLOCK, 128)
    bias, joined = call(
        kernel_weight_kernel,
        [((16, 128), F32), (blocks, BF)],
        [core, g0, g0_far, vw0, h2_0, h2_0_far, g1, g1_far, vw1, h2_1, h2_1_far],
        scalars=1,
        scratch=[((QUARTER * C, EDGES), BF), ((2, 32, 64, 128), BF), ((2,), None)],
        us=8,
        far_outs=1,
    )
    (joined,) = call(
        join_kernel, [(blocks, BF)], [core, own0, own1, away_far, bias, joined],
        scalars=1,
        far=1,
        far_outs=1,
        scratch=[((2 * SMALL, 128), F32), ((32, 32, 128), BF), ((1,), None)],
        aliases={5: 0},
    )
    joined, g0 = lax.optimization_barrier((joined, g0))
    parts = lax.all_to_all(joined, ROW_AXES, 0, 0, tiled=True)
    (dx0,) = call(
        first_node_kernel,
        [((HALF, N0), F32)],
        [self_in0, hot0, hot1, hot2, parents, rows, weight, h2_0, wkt, bias_rows, g0],
        scratch=[(sources, F32)],
        us=5,
    )
    (total,) = call(sum_kernel, [(blocks, BF)], [parts])
    dx0_far = swap(dx0, "tensor")
    total, dx0_far = lax.optimization_barrier((total, dx0_far))
    whole = lax.all_to_all(total, ROW_AXES, 0, 0, tiled=True)
    whole_far = swap(whole, "core")
    (input_grad,) = call(
        input_kernel, [((C, N0), F32)], [half, dx0, dx0_far], scalars=1
    )
    grad_shape = jax.ShapeDtypeStruct((2, HID, HALF * C), F32)
    params = pltpu.CompilerParams(vmem_limit_bytes=VMEM_MIB << 20)
    (grad_kernel,) = pl.pallas_call(
        spread_own_kernel,
        out_shape=[grad_shape],
        grid_spec=pltpu.PrefetchScalarGridSpec(
            num_scalar_prefetch=1,
            grid=(4,),
            in_specs=[vmem_spec()],
            out_specs=[
                pl.BlockSpec((2, 64, QUARTER * C), lambda part, core: (0, part, core[0]))
            ],
        ),
        compiler_params=params,
    )(core, whole)
    small_shapes = (
        (2, 128, HID), (2, HID), (6, 2, 128), (2, 128), (2, HALF * C), (2, C, C)
    )
    grad_kernel, grad_second, grad_b_second, grad_first, grad_b_first, grad_b_kernel, grad_self = (
        pl.pallas_call(
            spread_far_kernel,
            out_shape=[grad_shape]
            + [jax.ShapeDtypeStruct(shape, F32) for shape in small_shapes],
            grid_spec=pltpu.PrefetchScalarGridSpec(
                num_scalar_prefetch=1,
                grid=(4,),
                in_specs=[vmem_spec(), vmem_spec(), pl.BlockSpec(memory_space=pl.ANY)],
                out_specs=[
                    pl.BlockSpec((2, 64, QUARTER * C), lambda part, core: (0, part, 1 - core[0]))
                ]
                + [vmem_spec() for _ in small_shapes],
                scratch_shapes=[pltpu.VMEM((2 * SMALL, 128), F32)],
            ),
            input_output_aliases={3: 0},
            compiler_params=params,
        )(core, whole, whole_far, grad_kernel)
    )
    return (
        out.T, input_grad.T, grad_first.transpose(1, 0, 2), grad_b_first, grad_second,
        grad_b_second, grad_kernel, grad_b_kernel, grad_self,
    )


def solution(mesh):
    fine = Mesh(mesh.devices.reshape(2, 4, 4, 2, 2), DP_AXES + ("tensor",))
    dp = DP_AXES
    placed = (
        P(dp, None), P(dp, None), P(dp), P(dp), P(dp), P(dp, None), P(dp, None), P(dp, None),
        P(None, None, "tensor"), P(None, "tensor"), P(None, "tensor", None), P(),
        P(None, None, "tensor"), P(None, "tensor"), P(), P(dp, None),
    )
    return jax.shard_map(
        per_device,
        mesh=fine,
        in_specs=placed,
        out_specs=(
            P(dp, None), P(dp, None), P(None, None, "tensor"), P(None, "tensor"),
            P(None, "tensor", None), P(), P(None, None, "tensor"), P(None, "tensor"), P(),
        ),
        check_vma=False,
    )
```

```python
import functools

import jax
import jax.numpy as jnp
from jax import lax
from jax.experimental import pallas as pl
from jax.experimental.pallas import tpu as pltpu
from jax.sharding import Mesh, PartitionSpec as P

C = 64
HALF = 32
HID = 256
N0, N1, N2 = 256, 64, 16
DEG = 8
E0, E1, E2 = N0 * DEG, N1 * DEG, N2 * DEG
EDGES = 2816
TILES = ((0, 1024), (1024, 1024), (2048, 768))
WIDE = EDGES // 2
PARTS = 2
SMALL = 320
COARSE = N1 + N2
BLOCK = 160
QUARTER = HALF // 2
PACK = C + 3 * HALF
VMEM_MIB = 24
AUG = HID + 16
BF = jnp.bfloat16
F32 = jnp.float32
ROW_AXES = ("yl", "z", "x")
DP_AXES = ROW_AXES + ("core",)


def mm(left, right, contract=(1, 0)):
    return lax.dot_general(
        left, right, (((contract[0],), (contract[1],)), ((), ())), preferred_element_type=F32
    )


def pieces(value, count):
    parts = []
    for _ in range(count):
        part = value.astype(BF)
        parts.append(part)
        value = value - part.astype(F32)
    return parts


def mm_hot(value, hot, contract, count=2):
    rows = value.shape[0]
    product = mm(jnp.concatenate(pieces(value, count), axis=0), hot, contract)
    total = product[:rows]
    for index in range(1, count):
        total = total + product[index * rows : (index + 1) * rows]
    return total


def hot(rows, index):
    lanes = index.shape[1]
    match = lax.broadcasted_iota(jnp.int32, (rows, lanes), 0) == index
    return jnp.where(match, 1.0, 0.0).astype(BF)


def owner_hot(rows, lanes):
    index = lax.broadcasted_iota(jnp.int32, (rows, lanes), 1) & (rows - 1)
    match = lax.broadcasted_iota(jnp.int32, (rows, lanes), 0) == index
    return jnp.where(match, 1.0, 0.0).astype(BF)


def gelu(value):
    inner = value * (0.7978845608028654 + 0.035677408136300125 * (value * value))
    return value * (0.5 + 0.5 * jnp.tanh(inner))


def gelu_both(value):
    square = value * value
    inner = value * (0.7978845608028654 + 0.035677408136300125 * square)
    share = 0.5 + 0.5 * jnp.tanh(inner)
    slope = share + (share * (1.0 - share)) * (
        value * (1.5957691216057308 + 0.21406444881780074 * square)
    )
    return value * share, slope


def level_rows(rows_ref):
    return (
        rows_ref[0:1, :], rows_ref[1:2, 0:N1], rows_ref[3:4, 0:N2], rows_ref[4:5, :]
    )


def gather_sources(state, half, hot_refs, parents_ref, rows_ref, weight_ref, vw_ref, vals):
    live, child_mid, child_top, share = level_rows(rows_ref)
    start = pl.multiple_of(half * HALF, HALF)
    wide = state.astype(F32)
    mid = mm((wide * live).astype(BF), parents_ref[0:N1, :], (1, 1)) / child_mid
    top = mm_hot(wide * share, parents_ref[N1:COARSE, :], (1, 1), 3) / child_top
    vals[:, 0:N0] = wide
    vals[:, N0 : N0 + N1] = mid
    vals[:, N0 + 128 : N0 + 128 + N2] = top
    place = pl.ds(start, HALF)
    values = (
        vals[place, 0:N0], vals[place, N0 : N0 + N1], vals[place, N0 + 128 : N0 + 128 + N2]
    )
    lanes = 0
    for hot_ref, value in zip(hot_refs, values):
        count = hot_ref.shape[1]
        vw_ref[:, lanes : lanes + count] = (
            mm(value.astype(BF), hot_ref[...]) * weight_ref[:, lanes : lanes + count]
        )
        lanes += count
    vw_ref[:, lanes:] = jnp.zeros((HALF, EDGES - lanes), F32)


def halves(body):
    def step(index, carry):
        body(pl.ds(pl.multiple_of(index * WIDE, WIDE), WIDE))
        return carry

    lax.fori_loop(0, 2, step, 0)


def channel_parts(body, parts):
    def step(index, carry):
        rows, channels = HALF * C // parts, HALF // parts
        body(
            pl.ds(pl.multiple_of(index * rows, rows), rows),
            pl.ds(pl.multiple_of(index * channels, channels), channels),
        )
        return carry

    lax.fori_loop(0, parts, step, 0)


def message_pass(
    layer, h2_ref, parents_ref, owner_ref, wkt_ref, bias_ref, vw_ref, up_ref, msg, *kept_refs
):
    bias = bias_ref[layer]
    bias = jnp.concatenate([bias, bias], axis=1)
    for start, width in TILES:
        lanes = slice(start, start + width)
        msg[:, lanes] = mm(bias, jnp.concatenate(pieces(vw_ref[:, lanes], 2), axis=0))

    def part(rows, channels):
        for start, width in TILES:
            lanes = slice(start, start + width)
            source = vw_ref[channels, lanes]
            kernels = mm(wkt_ref[rows, :], h2_ref[0:HID, lanes])
            for kept_ref in kept_refs:
                kept_ref[rows, lanes] = kernels.astype(BF)
            total = msg[:, lanes]
            for channel in range(HALF // PARTS):
                total = total + (
                    kernels[channel * C : (channel + 1) * C] * source[channel : channel + 1, :]
                )
            msg[:, lanes] = total

    channel_parts(part, PARTS)
    total_fine = msg[:, 0:N0]
    for slot in range(1, DEG):
        total_fine = total_fine + msg[:, slot * N0 : (slot + 1) * N0]
    coarse = mm_hot(msg[:, E0:EDGES], owner_ref[...], (1, 1))
    up_ref[...] = total_fine + mm_hot(coarse, parents_ref[...], (1, 0))


def first_columns(packed_ref, layer):
    return packed_ref[HID : HID + 16, layer * 128 : (layer + 1) * 128].astype(F32).T.astype(BF)


def second_rows(packed_ref, far_ref, layer):
    rows = slice(layer * 128, (layer + 1) * 128)
    return jnp.concatenate([packed_ref[rows, :], far_ref[rows, :]], axis=0)


def ones_rows(width):
    return jnp.where(lax.broadcasted_iota(jnp.int32, (16, width), 0) == 0, 1.0, 0.0).astype(BF)


def pack_kernel(second_ref, first_ref, bias_ref, packed_ref, second, first, bias, rows, sems):
    copies = [
        pltpu.make_async_copy(source, target, sems.at[index])
        for index, (source, target) in enumerate(
            ((second_ref, second), (first_ref, first), (bias_ref, bias))
        )
    ]
    for copy in copies:
        copy.start()
    rows[...] = jnp.zeros_like(rows)
    for copy in copies:
        copy.wait()
    packed_ref[0:128, :] = second[0]
    packed_ref[128:256, :] = second[1]
    bias_rows = bias[...].astype(F32)
    for layer in range(2):
        lanes = slice(layer * 128, (layer + 1) * 128)
        for row in range(6):
            rows[row : row + 1, lanes] = first[row].astype(F32)[layer : layer + 1]
        rows[6:7, lanes] = bias_rows[layer : layer + 1]
    packed_ref[256:272, :] = rows[...].astype(BF)


def prep_kernel(
    count_ref, half_ref, packed_ref, geometry_hbm, pm_hbm, pt_hbm, near0_hbm, near1_hbm, near2_hbm,
    node_hbm, bk_hbm, bs_hbm, wk_hbm,
    edge_ref, weight_ref, hot0_ref, hot1_ref, hot2_ref, parents_ref, owner_ref, rows_ref, wkt0_ref,
    wkt1_ref,    bias_rows_ref, bias_cols_ref, bs_cols_ref, hown_ref, vw_ref, node_ref,
    index_ref, pm_ref, pt_ref, geometry_ref, near0_ref, near1_ref, near2_ref, bk_ref, bs_ref, wk_ref, sems, vals, bias_rows,
):
    copies = [
        pltpu.make_async_copy(source, target, sems.at[index])
        for index, (source, target) in enumerate(
            (
                (geometry_hbm, geometry_ref), (pm_hbm, pm_ref), (pt_hbm, pt_ref),
                (near0_hbm, near0_ref), (near1_hbm, near1_ref), (near2_hbm, near2_ref),
                (node_hbm, node_ref), (bk_hbm, bk_ref), (bs_hbm, bs_ref), (wk_hbm, wk_ref),
            )
        )
    ]
    for copy in copies:
        copy.start()
    for copy in copies[:-1]:
        copy.wait()
    live = jnp.where(
        lax.broadcasted_iota(jnp.int32, (1, N0), 1) < count_ref[0], 1.0, 0.0
    ).astype(F32)
    parent = hot(N1, pm_ref[...])
    parent_top = hot(N2, pt_ref[...])
    live8 = jnp.broadcast_to(live, (16, N0))
    child_mid = mm(live8.astype(BF), parent, (1, 1))
    live_mid = jnp.where(child_mid > 0.5, 1.0, 0.0)
    child_top = mm(live_mid.astype(BF), parent_top, (1, 1))
    live_top = jnp.where(child_top > 0.5, 1.0, 0.0)
    child_mid = jnp.maximum(child_mid, 1.0)
    child_top = jnp.maximum(child_top, 1.0)
    rows_ref[...] = jnp.zeros_like(rows_ref)
    rows_ref[0:1, :] = live
    rows_ref[1:2, 0:N1] = child_mid[0:1]
    rows_ref[2:3, 0:N1] = live_mid[0:1]
    rows_ref[3:4, 0:N2] = child_top[0:1]
    share = mm_hot(live_mid / child_mid, parent, (1, 0), 3)[0:1] * live
    rows_ref[4:5, :] = share
    parents_ref[0:N1, :] = parent
    composite = mm(parent_top, parent).astype(BF)
    parents_ref[N1:COARSE, :] = composite
    row = lax.broadcasted_iota(jnp.int32, owner_ref.shape, 0)
    lane = lax.broadcasted_iota(jnp.int32, owner_ref.shape, 1)
    mid_own = (lane < E1) & (row == (lane & (N1 - 1)))
    top_own = (lane >= E1) & (lane < E1 + E2) & (row == N1 + (lane & (N2 - 1)))
    owner_ref[...] = jnp.where(mid_own | top_own, 1.0, 0.0).astype(BF)
    index_ref[...] = jnp.zeros_like(index_ref)
    for slot in range(DEG):
        row = slice(slot, slot + 1)
        index_ref[:, slot * N0 : (slot + 1) * N0] = near0_ref[row, :]
        index_ref[:, E0 + slot * N1 : E0 + (slot + 1) * N1] = near1_ref[row, :]
        start = E0 + E1 + slot * N2
        index_ref[:, start : start + N2] = near2_ref[row, :]
    vals[0:16, 0:N0] = jnp.zeros((16, N0), F32)
    vals[0:3, 0:N0] = geometry_ref[...]
    coords = vals[0:16, 0:N0]
    coords_mid = mm_hot(coords * live, parent, (1, 1), 3) / child_mid
    coords_top = mm_hot(coords * share, composite, (1, 1), 3) / child_top
    lane_row = lax.broadcasted_iota(jnp.int32, (16, 1), 0)

    def with_live(values, live_row):
        return jnp.where(lane_row == 3, live_row, values).astype(BF)

    fine_rows = with_live(coords, live)
    mid_rows = with_live(coords_mid, live_mid[0:1])
    top_rows = with_live(coords_top, live_top[0:1])

    def edges(own, near):
        low = jnp.where(lane_row < 3, own, 0.0)
        high = pltpu.roll(jnp.where(lane_row < 3, near, 0.0), 3, 0)
        return jnp.where(lane_row == 6, 1.0, low + high).astype(BF)

    fine = fine_rows.astype(F32)
    masks = []
    for slot in range(DEG):
        lanes = slice(slot * N0, (slot + 1) * N0)
        hot0_ref[:, lanes] = hot(N0, index_ref[:, lanes])
        near = mm(fine_rows, hot0_ref[:, lanes])
        edge_ref[:, lanes] = edges(fine, near)
        masks.append(live * near[3:4])
    total = masks[0]
    for mask in masks[1:]:
        total = total + mask
    total = jnp.maximum(total, 1.0)
    for slot in range(DEG):
        weight_ref[:, slot * N0 : (slot + 1) * N0] = masks[slot] / total

    def small_level(values, rows, start, lanes, hot_ref):
        own = mm(values, owner_hot(rows, lanes))
        hot_ref[...] = hot(rows, index_ref[:, start : start + lanes])
        near = mm(values, hot_ref[...])
        edge_ref[:, start : start + lanes] = edges(own, near)
        mask = own * near
        fold = jnp.where(
            (lax.broadcasted_iota(jnp.int32, (lanes, lanes), 0) & (rows - 1))
            == (lax.broadcasted_iota(jnp.int32, (lanes, lanes), 1) & (rows - 1)),
            1.0,
            0.0,
        ).astype(BF)
        total = jnp.maximum(mm(mask.astype(BF), fold), 1.0)
        weight_ref[:, start : start + lanes] = mask[3:4] / total[3:4]

    small_level(mid_rows, N1, E0, E1, hot1_ref)
    small_level(top_rows, N2, E0 + E1, E2, hot2_ref)
    rest = E0 + E1 + E2
    edge_ref[:, rest:] = jnp.zeros((16, EDGES - rest), BF)
    weight_ref[:, rest:] = jnp.zeros((1, EDGES - rest), F32)
    gather_sources(
        node_ref[...], half_ref[0], (hot0_ref, hot1_ref, hot2_ref), parents_ref, rows_ref,
        weight_ref, vw_ref, vals,
    )
    bias = bk_ref[...].astype(F32)
    copies[-1].wait()
    for layer in range(2):
        for part in range(8):
            (wkt0_ref, wkt1_ref)[layer][part * 256 : (part + 1) * 256, :] = wk_ref[
                layer, :, part * 256 : (part + 1) * 256
            ].T
        for row in range(HALF):
            bias_rows[row : row + 1, :] = bias[layer : layer + 1, row * C : (row + 1) * C]
        bias_rows_ref[layer] = bias_rows[...].astype(BF)
        bias_cols_ref[layer] = bias_rows[...].T.astype(BF)
    hown_ref[...] = gelu(mm(first_columns(packed_ref, 0), edge_ref[...])).astype(BF)
    second_bias = jnp.concatenate([bs_ref[...].astype(F32), jnp.zeros((6, HID), F32)], axis=0)
    bs_cols_ref[...] = second_bias.T


def first_forward_kernel(
    parents_ref, owner_ref, packed_ref, far_ref, edge_ref, hown_ref, bs_ref, wkt_ref, bias_ref, vw_ref,
    h2_ref, up_ref, msg,
):
    second = second_rows(packed_ref, far_ref, 0).T
    first = first_columns(far_ref, 0)
    bias = bs_ref[:, 0:1]

    def body(lanes):
        away = gelu(mm(first, edge_ref[:, lanes])).astype(BF)
        one = jnp.concatenate([hown_ref[:, lanes], away], axis=0)
        h2_ref[0:HID, lanes] = gelu(mm(second, one) + bias).astype(BF)

    halves(body)
    h2_ref[HID:AUG, :] = ones_rows(EDGES)
    message_pass(
        0, h2_ref, parents_ref, owner_ref, wkt_ref, bias_ref, vw_ref, up_ref, msg,
    )


def mlp_kernel(layer, packed_ref, far_ref, edge_ref, bs_ref, h1_ref, s1_ref, s2_ref, *h2_refs):
    second = second_rows(packed_ref, far_ref, layer).T
    first = jnp.concatenate(
        [first_columns(packed_ref, layer), first_columns(far_ref, layer)], axis=0
    )
    bias = bs_ref[:, layer : layer + 1]

    def body(lanes):
        value, slope = gelu_both(mm(first, edge_ref[:, lanes]))
        one = value.astype(BF)
        h1_ref[0:HID, lanes] = one
        s1_ref[:, lanes] = slope.astype(BF)
        value, slope = gelu_both(mm(second, one) + bias)
        s2_ref[:, lanes] = slope.astype(BF)
        for h2_ref in h2_refs:
            h2_ref[0:HID, lanes] = value.astype(BF)

    halves(body)
    h1_ref[HID:AUG, :] = edge_ref[...]
    for h2_ref in h2_refs:
        h2_ref[HID:AUG, :] = ones_rows(EDGES)


def next_forward_kernel(
    half_ref, node_ref, self_ref, up_own_ref, up_far_ref, hot0_ref, hot1_ref, hot2_ref, parents_ref,
    owner_ref, rows_ref, weight_ref, h2_ref, wkt_ref, bias_ref,
    pre_ref, state_ref, up_ref, vw_ref, kept_ref, vals, msg,
):
    pre = mm(self_ref[0].astype(F32).T.astype(BF), node_ref[...])
    pre = pre + (up_own_ref[...] + up_far_ref[...])
    pre_ref[...] = pre
    state = (gelu(pre) * rows_ref[0:1, :]).astype(BF)
    state_ref[...] = state
    gather_sources(
        state, half_ref[0], (hot0_ref, hot1_ref, hot2_ref), parents_ref, rows_ref, weight_ref,
        vw_ref, vals,
    )
    message_pass(
        1, h2_ref, parents_ref, owner_ref, wkt_ref, bias_ref, vw_ref, up_ref, msg, kept_ref,
    )


def node_grads(
    layer, half, h, pre, grad, parents_ref, owner_ref, live, self_ref, own_ref, g_ref
):
    start = pl.multiple_of(half * HALF, HALF)
    _, slope = gelu_both(pre)
    grad_pre = slope * (live * grad)
    high, low = pieces(grad_pre, 2)
    grad_self = mm(h, high, (1, 1)) + mm(h, low, (1, 1))
    own_ref[288:320, 0:C] = grad_self[0:HALF]
    own_ref[288:320, C : 2 * C] = grad_self[HALF:C]
    self_half = self_ref[layer, pl.ds(start, HALF), :]
    self_in = mm(self_half, high) + mm(self_half, low)
    coarse = mm_hot(grad_pre, parents_ref[...], (1, 1), 3).astype(BF)
    g_ref[0:C, 0:N0] = grad_pre.astype(BF)
    g_ref[0:C, N0:] = mm(coarse, owner_ref[...]).astype(BF)
    return self_in


def grad_tile(g_ref, start, width):
    if start < E0:
        return jnp.concatenate([g_ref[0:C, 0:N0]] * (width // N0), axis=1)
    return g_ref[0:C, N0 : N0 + width]


def source_grads(self_in, hot_refs, parents_ref, rows_ref, dvw):
    live, child_mid, child_top, share = level_rows(rows_ref)
    sums = []
    lanes = 0
    for hot_ref in hot_refs:
        count = hot_ref.shape[1]
        total = mm_hot(dvw[:, lanes : lanes + count], hot_ref[...], (1, 1))
        sums.append(total.astype(BF).astype(F32))
        lanes += count
    fine, mid, top = sums
    return (
        self_in
        + fine
        + mm_hot(mid / child_mid, parents_ref[0:N1, :], (1, 0), 3) * live
        + mm_hot(top / child_top, parents_ref[N1:COARSE, :], (1, 0), 3) * share
    )


def fill_pack(core, vw_ref, pack_ref):
    place = pl.ds(pl.multiple_of((1 - core) * QUARTER, QUARTER), QUARTER)
    for index, (start, width) in enumerate(TILES):
        high, low = pieces(vw_ref[place, start : start + width], 2)
        base = C + index * HALF
        pack_ref[base : base + QUARTER, 0:width] = high
        pack_ref[base + QUARTER : base + HALF, 0:width] = low
    pack_ref[C + 2 * HALF : PACK, 768:1024] = jnp.zeros((HALF, 256), BF)


def far_source(pack_ref, index, width):
    base = C + index * HALF
    high = pack_ref[base : base + QUARTER, 0:width].astype(F32)
    return high + pack_ref[base + QUARTER : base + HALF, 0:width].astype(F32)


def fill_grad_kernels(g_ref, source, gk, start, width, rows):
    lanes = slice(start, start + width)
    grad = grad_tile(g_ref, start, width).astype(F32)
    for row in range(rows):
        gk[row * C : (row + 1) * C, lanes] = (grad * source[row : row + 1, :]).astype(BF)


def mlp_backward(
    layer, g_ref, vw_ref, wk_ref, h1_ref, s1_ref, s2_ref, packed_ref, far_ref, own_ref, away_ref,
    gk, both,
):
    second = second_rows(packed_ref, far_ref, layer)
    for start, width in TILES:
        lanes = slice(start, start + width)
        fill_grad_kernels(g_ref, vw_ref[:, lanes], gk, start, width, HALF)
        two = (s2_ref[:, lanes].astype(F32) * mm(wk_ref[layer], gk[:, lanes])).astype(BF)
        both[0:HID, lanes] = two
        both[HID:, lanes] = (s1_ref[:, lanes].astype(F32) * mm(second, two)).astype(BF)
    product = mm(h1_ref[...], both[...], (1, 1))
    grad_second = product[0:HID, 0:HID]
    grad_first = product[HID : HID + 7, HID:]
    grad_bias = product[HID + 6 : HID + 7, 0:HID]
    own_ref[0:128, :] = grad_second[0:128, 0:128]
    own_ref[128:256, :] = grad_second[0:128, 128:256]
    own_ref[272:273, :] = grad_bias[:, 0:128]
    own_ref[273:274, :] = grad_bias[:, 128:256]
    own_ref[274:281, :] = grad_first[:, 0:128]
    own_ref[281:288, :] = jnp.zeros((7, 128), F32)
    away_ref[0:128, :] = grad_second[128:256, 0:128].astype(BF)
    away_ref[128:256, :] = grad_second[128:256, 128:256].astype(BF)
    tail = jnp.concatenate(
        [grad_bias[:, 0:128], grad_bias[:, 128:256], grad_first[:, 128:256],
         jnp.zeros((7, 128), F32)],
        axis=0,
    )
    away_ref[256:272, :] = tail.astype(BF)


def kernel_weight_kernel(
    core_ref, *refs
):
    layer_refs = (refs[0:5], refs[5:10])
    bias_ref, joined_hbm, gk, joined_ref, sems = refs[10:]
    mine = pl.ds(pl.multiple_of(core_ref[0] * QUARTER, QUARTER), QUARTER)
    copies = []
    for layer in (1, 0):
        pack_ref, far_ref, vw_ref, h2_ref, h2_far_ref = layer_refs[layer]
        for index, (start, width) in enumerate(TILES):
            source = vw_ref[mine, start : start + width]
            fill_grad_kernels(pack_ref, source, gk, start, width, QUARTER)
        product = mm(h2_ref[...], gk[...], (1, 1))
        for index, (start, width) in enumerate(TILES):
            source = far_source(far_ref, index, width)
            fill_grad_kernels(far_ref, source, gk, start, width, QUARTER)
        product = product + mm(h2_far_ref[...], gk[...], (1, 1))
        for part in range(4):
            for block in range(8):
                joined_ref[layer, part * 8 + block] = product[
                    part * 64 : (part + 1) * 64, block * 128 : (block + 1) * 128
                ].astype(BF)
        copy = pltpu.make_async_copy(
            joined_ref.at[layer], joined_hbm.at[:, layer * 64 : (layer + 1) * 64, :], sems.at[layer]
        )
        copy.start()
        copies.append(copy)
        for block in range(8):
            row = layer * 8 + block
            bias_ref[row : row + 1, :] = product[HID : HID + 1, block * 128 : (block + 1) * 128]
    for copy in copies:
        copy.wait()


def last_node_kernel(
    half_ref, core_ref, state_ref, self_ref, up_own_ref, up_far_ref, cot_ref, hot0_ref, hot1_ref,
    hot2_ref, parents_ref, owner_ref, rows_ref, weight_ref, kept_ref, bias_ref, vw_ref,
    out_ref, own_ref, g_ref, dx_ref, dvw, wide,
):
    fill_pack(core_ref[0], vw_ref, g_ref)
    live = rows_ref[0:1, :]
    state = state_ref[...]
    pre = mm(self_ref[1].astype(F32).T.astype(BF), state)
    pre = pre + (up_own_ref[...] + up_far_ref[...])
    out_ref[...] = (gelu(pre) * live).astype(BF)
    self_in = node_grads(
        1, half_ref[0], state, pre, cot_ref[...].astype(F32), parents_ref, owner_ref, live,
        self_ref, own_ref, g_ref,
    )
    for start, width in TILES:
        wide[:, start : start + width] = grad_tile(g_ref, start, width)
    offset = mm(bias_ref[1], wide[...])
    for start, width in TILES:
        lanes = slice(start, start + width)
        grad = wide[:, lanes].astype(F32)
        for part in range(4):
            channels = slice(part * 8, (part + 1) * 8)
            kernels = kept_ref[part * 512 : (part + 1) * 512, lanes].astype(F32)
            total = jnp.sum(kernels.reshape(8, C, width) * grad[None], axis=1)
            dvw[channels, lanes] = (total + offset[channels, lanes]) * weight_ref[:, lanes]
    dx_ref[...] = source_grads(
        self_in, (hot0_ref, hot1_ref, hot2_ref), parents_ref, rows_ref, dvw
    )


def last_edge_kernel(
    g_ref, vw_ref, wk_ref, h1_ref, s1_ref, s2_ref, packed_ref, far_ref, self_grad_ref,
    own_ref, away_ref, gk, both,
):
    mlp_backward(
        1, g_ref, vw_ref, wk_ref, h1_ref, s1_ref, s2_ref, packed_ref, far_ref, own_ref, away_ref,
        gk, both,
    )
    own_ref[256:272, :] = jnp.zeros((16, 128), F32)
    own_ref[288:320, :] = self_grad_ref[288:320, :]


def first_edge_kernel(
    half_ref, core_ref, node_ref, pre_ref, dx_own_ref, dx_far_ref, self_ref, parents_ref, owner_ref,
    rows_ref,
    vw_ref, wk_ref, h1_ref, s1_ref, s2_ref, packed_ref, far_ref, away1_ref,
    g_ref, self_in_ref, own_ref, away_ref, grad, gk, both,
):
    fill_pack(core_ref[0], vw_ref, g_ref)
    away_ref[AUG:, :] = away1_ref[...]
    start = pl.multiple_of(half_ref[0] * HALF, HALF)
    grad[pl.ds(start, HALF), :] = dx_own_ref[...]
    grad[pl.ds(HALF - start, HALF), :] = dx_far_ref[...]
    self_in_ref[...] = node_grads(
        0, half_ref[0], node_ref[...], pre_ref[...], grad[...], parents_ref, owner_ref,
        rows_ref[0:1, :], self_ref, own_ref, g_ref,
    )
    own_ref[256:272, :] = jnp.zeros((16, 128), F32)
    mlp_backward(
        0, g_ref, vw_ref, wk_ref, h1_ref, s1_ref, s2_ref, packed_ref, far_ref, own_ref,
        away_ref.at[0:AUG, :], gk, both,
    )


def first_node_kernel(
    self_in_ref, hot0_ref, hot1_ref, hot2_ref, parents_ref, rows_ref, weight_ref, h2_ref, wkt_ref,
    bias_ref, g_ref,
    dx_ref, dvw,
):

    def part(rows, channels):
        for start, width in TILES:
            lanes = slice(start, start + width)
            grad = grad_tile(g_ref, start, width)
            offset = mm(bias_ref[0, channels, :], grad)
            kernels = mm(wkt_ref[rows, :], h2_ref[0:HID, lanes])
            product = kernels.reshape(HALF // PARTS, C, width) * grad.astype(F32)[None]
            dvw[channels, lanes] = (jnp.sum(product, axis=1) + offset) * weight_ref[:, lanes]

    channel_parts(part, PARTS)
    dx_ref[...] = source_grads(
        self_in_ref[...], (hot0_ref, hot1_ref, hot2_ref), parents_ref, rows_ref, dvw
    )


def join_kernel(core_ref, own0_ref, own1_ref, away_ref, bias_ref, _, out_ref, rows, tail, sem):
    for layer, own_ref in enumerate((own0_ref, own1_ref)):
        base = layer * SMALL
        far = away_ref[layer * AUG : (layer + 1) * AUG, :].astype(F32)
        rows[base : base + 256, :] = own_ref[0:256, :] + far[0:256]
        rows[base + 256 : base + 272, :] = jnp.zeros((16, 128), F32)
        place = pl.ds(pl.multiple_of(base + 256 + core_ref[0] * 8, 8), 8)
        rows[place, :] = bias_ref[layer * 8 : (layer + 1) * 8, :]
        rows[base + 272 : base + 288, :] = own_ref[272:288, :] + far[256:272]
        rows[base + 288 : base + 320, :] = own_ref[288:320, :]
    for block in range(32):
        if block < 2 * SMALL // 32:
            tail[block] = rows[block * 32 : (block + 1) * 32, :].astype(BF)
        else:
            tail[block] = jnp.zeros((32, 128), BF)
    copy = pltpu.make_async_copy(tail, out_ref.at[:, 128:BLOCK, :], sem.at[0])
    copy.start()
    copy.wait()


def sum_kernel(parts_ref, out_ref):
    total = parts_ref[0].astype(F32)
    for peer in range(1, 32):
        total = total + parts_ref[peer].astype(F32)
    total = total.astype(BF)
    for peer in range(32):
        out_ref[peer] = total


def spread_blocks(side_ref, kernel_ref):
    part = pl.program_id(0)
    for block in range(8):
        for layer in range(2):
            kernel_ref[layer, :, block * 128 : (block + 1) * 128] = side_ref[
                part * 8 + block, layer * 64 : (layer + 1) * 64, :
            ].astype(F32)


def spread_own_kernel(core_ref, own_ref, kernel_ref):
    spread_blocks(own_ref, kernel_ref)


def spread_far_kernel(
    core_ref, own_ref, far_ref, _,
    kernel_ref, second_ref, second_bias_ref, first_ref, first_bias_ref, kernel_bias_ref, self_ref,
    rows,
):
    spread_blocks(far_ref, kernel_ref)

    @pl.when(pl.program_id(0) == 0)
    def _():
        spread_small(
            own_ref, far_ref, second_ref, second_bias_ref, first_ref, first_bias_ref,
            kernel_bias_ref, self_ref, rows,
        )


def spread_small(
    own_ref, far_ref, second_ref, second_bias_ref, first_ref, first_bias_ref, kernel_bias_ref,
    self_ref, rows,
):
    for block in range(2 * SMALL // 32):
        rows[block * 32 : (block + 1) * 32, :] = own_ref[block, 128:BLOCK, :].astype(
            F32
        ) + far_ref[block, 128:BLOCK, :].astype(F32)
    for layer in range(2):
        base = layer * SMALL
        second_ref[layer, :, 0:128] = rows[base : base + 128, :]
        second_ref[layer, :, 128:256] = rows[base + 128 : base + 256, :]
        for block in range(16):
            lanes = slice(block * 128, (block + 1) * 128)
            row = base + 256 + block
            kernel_bias_ref[layer : layer + 1, lanes] = rows[row : row + 1, :]
        second_bias_ref[layer : layer + 1, 0:128] = rows[base + 272 : base + 273, :]
        second_bias_ref[layer : layer + 1, 128:256] = rows[base + 273 : base + 274, :]
        for row in range(6):
            first_ref[row, layer : layer + 1, :] = rows[base + 274 + row : base + 275 + row, :]
        first_bias_ref[layer : layer + 1, :] = rows[base + 280 : base + 281, :]
        self_ref[layer, 0:HALF, :] = rows[base + 288 : base + 320, 0:C]
        self_ref[layer, HALF:C, :] = rows[base + 288 : base + 320, C : 2 * C]


def input_kernel(half_ref, own_ref, far_ref, out_ref):
    start = pl.multiple_of(half_ref[0] * HALF, HALF)
    out_ref[pl.ds(start, HALF), :] = own_ref[...]
    out_ref[pl.ds(HALF - start, HALF), :] = far_ref[...]


def vmem_spec():
    return pl.BlockSpec(memory_space=pltpu.VMEM)


def smem_spec():
    return pl.BlockSpec(memory_space=pltpu.SMEM)


def call(kernel, outs, args, scalars=0, scratch=(), us=1, far=0, far_outs=0, aliases=None):
    count = len(args)
    specs = [smem_spec()] * scalars + [vmem_spec()] * (count - scalars - far)
    args = list(args[: count - far]) + [
        pltpu.with_memory_space_constraint(value, pltpu.HBM) for value in args[count - far :]
    ]
    return pl.pallas_call(
        kernel,
        out_shape=[
            pltpu.HBM(*out) if index >= len(outs) - far_outs else jax.ShapeDtypeStruct(*out)
            for index, out in enumerate(outs)
        ],
        in_specs=specs + [pl.BlockSpec(memory_space=pltpu.HBM)] * far,
        out_specs=[
            pl.BlockSpec(memory_space=pltpu.HBM) if index >= len(outs) - far_outs else vmem_spec()
            for index in range(len(outs))
        ],
        scratch_shapes=[
            pltpu.SemaphoreType.DMA(entry[0]) if entry[1] is None else pltpu.VMEM(*entry)
            for entry in scratch
        ],
        input_output_aliases=aliases or {},
        compiler_params=pltpu.CompilerParams(vmem_limit_bytes=VMEM_MIB << 20),
        cost_estimate=pl.CostEstimate(
            flops=us * 1000000000, bytes_accessed=1 << 20, transcendentals=0
        ),
    )(*args)


def swap(value, axis):
    return lax.ppermute(value, axis, [(0, 1), (1, 0)])


def per_device(
    node_input, geometry, counts, parent_mid, parent_top, neighbours_fine, neighbours_mid,
    neighbours_top, w_first, b_first, w_second, b_second, w_kernel, b_kernel, w_self, cotangent,
):
    half = lax.axis_index("tensor").astype(jnp.int32).reshape(1)
    core = lax.axis_index("core").astype(jnp.int32).reshape(1)
    counts, half, core, w_second = lax.optimization_barrier((counts, half, core, w_second))
    pm = parent_mid.reshape(1, N0)
    pt = parent_top.reshape(1, N1)
    node = node_input.T
    wide = (AUG, EDGES)
    edges = (HID, EDGES)
    sources = (HALF, EDGES)

    (packed,) = call(
        pack_kernel,
        [((AUG, HID), BF)],
        [w_second, w_first.transpose(1, 0, 2), b_first],
        scratch=[((2, 128, HID), BF), ((6, 2, 128), BF), ((2, 128), BF), ((16, HID), F32),
                 ((3,), None)],
        far=3,
    )
    far = swap(packed, "tensor")
    (
        edge, weight, hot0, hot1, hot2, parents, owner, rows, wkt0, wkt1, bias_rows, bias_cols,
        bs_cols,
        hown, vw0, node,
    ) = call(
        prep_kernel,
        [((16, EDGES), BF), ((1, EDGES), F32), ((N0, E0), BF), ((N1, E1), BF), ((N2, E2), BF),
         ((COARSE, N0), BF), ((COARSE, EDGES - E0), BF), ((8, N0), F32), ((HALF * C, HID), BF), ((HALF * C, HID), BF), ((2, HALF, C), BF), ((2, C, HALF), BF), ((HID, 8), F32),
         ((128, EDGES), BF), (sources, F32), ((C, N0), BF)],
        [counts, half, packed, geometry.T, pm, pt, neighbours_fine.T, neighbours_mid.T,
         neighbours_top.T, node, b_kernel, b_second, w_kernel],
        scalars=2,
        far=10,
        scratch=[((1, EDGES), jnp.int32), ((1, N0), jnp.int32), ((1, N1), jnp.int32),
                 ((3, N0), F32), ((8, N0), jnp.int32), ((8, N1), jnp.int32), ((8, N2), jnp.int32),
                 ((2, HALF * C), BF), ((2, HID), BF), ((2, HID, HALF * C), BF), ((10,), None),
                 ((C, N0 + 256), F32), ((HALF, C), F32)],
        us=4,
    )
    h2_0, up0 = call(
        first_forward_kernel,
        [(wide, BF), ((C, N0), F32)],
        [parents, owner, packed, far, edge, hown, bs_cols, wkt0, bias_cols, vw0],
        scratch=[((C, EDGES), F32)],
        us=8,
    )
    up0_far = swap(up0, "tensor")
    h2_0_far = swap(h2_0, "core")

    def mlp(layer, outs):
        return call(
            functools.partial(mlp_kernel, layer), outs, [packed, far, edge, bs_cols], us=5
        )

    h1_1, s1_1, s2_1, h2_1 = mlp(1, [(wide, BF), (edges, BF), (edges, BF), (wide, BF)])
    pre0, state, up1, vw1, kept = call(
        next_forward_kernel,
        [((C, N0), F32), ((C, N0), BF), ((C, N0), F32), (sources, F32), ((HALF * C, EDGES), BF)],
        [half, node, w_self, up0, up0_far, hot0, hot1, hot2, parents, owner, rows, weight, h2_1, wkt1,
         bias_cols],
        scalars=1,
        scratch=[((C, N0 + 256), F32), ((C, EDGES), F32)],
        us=5,
    )
    up1_far = swap(up1, "tensor")
    h2_1_far = swap(h2_1, "core")
    up1, edge = lax.optimization_barrier((up1, edge))
    h1_0, s1_0, s2_0 = mlp(0, [(wide, BF), (edges, BF), (edges, BF)])
    out, self_grad1, g1, dx1 = call(
        last_node_kernel,
        [((C, N0), BF), ((SMALL, 128), F32), ((PACK, 1024), BF), ((HALF, N0), F32)],
        [half, core, state, w_self, up1, up1_far, cotangent.T, hot0, hot1, hot2, parents, owner,
         rows, weight, kept, bias_rows, vw1],
        scalars=2,
        scratch=[(sources, F32), ((C, EDGES), BF)],
        us=5,
    )
    dx1_far = swap(dx1, "tensor")
    g1_far = swap(g1, "core")
    edge_scratch = [((HALF * C, EDGES), BF), ((2 * HID, EDGES), BF)]
    own1, away1 = call(
        last_edge_kernel,
        [((SMALL, 128), F32), ((AUG, 128), BF)],
        [g1, vw1, w_kernel, h1_1, s1_1, s2_1, packed, far, self_grad1],
        scratch=edge_scratch,
        us=5,
    )
    g0, self_in0, own0, away = call(
        first_edge_kernel,
        [((PACK, 1024), BF), ((HALF, N0), F32), ((SMALL, 128), F32), ((2 * AUG, 128), BF)],
        [half, core, node, pre0, dx1, dx1_far, w_self, parents, owner, rows, vw0, w_kernel, h1_0, s1_0, s2_0,
         packed, far, away1],
        scalars=2,
        scratch=[((C, N0), F32)] + edge_scratch,
        us=6,
    )
    away_far = swap(away, "tensor")
    g0_far = swap(g0, "core")
    blocks = (32, BLOCK, 128)
    bias, joined = call(
        kernel_weight_kernel,
        [((16, 128), F32), (blocks, BF)],
        [core, g0, g0_far, vw0, h2_0, h2_0_far, g1, g1_far, vw1, h2_1, h2_1_far],
        scalars=1,
        scratch=[((QUARTER * C, EDGES), BF), ((2, 32, 64, 128), BF), ((2,), None)],
        us=8,
        far_outs=1,
    )
    (joined,) = call(
        join_kernel, [(blocks, BF)], [core, own0, own1, away_far, bias, joined],
        scalars=1,
        far=1,
        far_outs=1,
        scratch=[((2 * SMALL, 128), F32), ((32, 32, 128), BF), ((1,), None)],
        aliases={5: 0},
    )
    joined, g0 = lax.optimization_barrier((joined, g0))
    parts = lax.all_to_all(joined, ROW_AXES, 0, 0, tiled=True)
    (dx0,) = call(
        first_node_kernel,
        [((HALF, N0), F32)],
        [self_in0, hot0, hot1, hot2, parents, rows, weight, h2_0, wkt0, bias_rows, g0],
        scratch=[(sources, F32)],
        us=5,
    )
    (total,) = call(sum_kernel, [(blocks, BF)], [parts])
    dx0_far = swap(dx0, "tensor")
    total, dx0_far = lax.optimization_barrier((total, dx0_far))
    whole = lax.all_to_all(total, ROW_AXES, 0, 0, tiled=True)
    whole_far = swap(whole, "core")
    (input_grad,) = call(
        input_kernel, [((C, N0), F32)], [half, dx0, dx0_far], scalars=1
    )
    grad_shape = jax.ShapeDtypeStruct((2, HID, HALF * C), F32)
    params = pltpu.CompilerParams(vmem_limit_bytes=VMEM_MIB << 20)
    (grad_kernel,) = pl.pallas_call(
        spread_own_kernel,
        out_shape=[grad_shape],
        grid_spec=pltpu.PrefetchScalarGridSpec(
            num_scalar_prefetch=1,
            grid=(4,),
            in_specs=[vmem_spec()],
            out_specs=[
                pl.BlockSpec((2, 64, QUARTER * C), lambda part, core: (0, part, core[0]))
            ],
        ),
        compiler_params=params,
    )(core, whole)
    small_shapes = (
        (2, 128, HID), (2, HID), (6, 2, 128), (2, 128), (2, HALF * C), (2, C, C)
    )
    grad_kernel, grad_second, grad_b_second, grad_first, grad_b_first, grad_b_kernel, grad_self = (
        pl.pallas_call(
            spread_far_kernel,
            out_shape=[grad_shape]
            + [jax.ShapeDtypeStruct(shape, F32) for shape in small_shapes],
            grid_spec=pltpu.PrefetchScalarGridSpec(
                num_scalar_prefetch=1,
                grid=(4,),
                in_specs=[vmem_spec(), vmem_spec(), pl.BlockSpec(memory_space=pl.ANY)],
                out_specs=[
                    pl.BlockSpec((2, 64, QUARTER * C), lambda part, core: (0, part, 1 - core[0]))
                ]
                + [vmem_spec() for _ in small_shapes],
                scratch_shapes=[pltpu.VMEM((2 * SMALL, 128), F32)],
            ),
            input_output_aliases={3: 0},
            compiler_params=params,
        )(core, whole, whole_far, grad_kernel)
    )
    return (
        out.T, input_grad.T, grad_first.transpose(1, 0, 2), grad_b_first, grad_second,
        grad_b_second, grad_kernel, grad_b_kernel, grad_self,
    )


def solution(mesh):
    fine = Mesh(mesh.devices.reshape(2, 4, 4, 2, 2), DP_AXES + ("tensor",))
    dp = DP_AXES
    placed = (
        P(dp, None), P(dp, None), P(dp), P(dp), P(dp), P(dp, None), P(dp, None), P(dp, None),
        P(None, None, "tensor"), P(None, "tensor"), P(None, "tensor", None), P(),
        P(None, None, "tensor"), P(None, "tensor"), P(), P(dp, None),
    )
    return jax.shard_map(
        per_device,
        mesh=fine,
        in_specs=placed,
        out_specs=(
            P(dp, None), P(dp, None), P(None, None, "tensor"), P(None, "tensor"),
            P(None, "tensor", None), P(), P(None, None, "tensor"), P(None, "tensor"), P(),
        ),
        check_vma=False,
    )
```

```python
import functools

import jax
import jax.numpy as jnp
from jax import lax
from jax.experimental import pallas as pl
from jax.experimental.pallas import tpu as pltpu
from jax.sharding import Mesh, PartitionSpec as P

C = 64
HALF = 32
HID = 256
N0, N1, N2 = 256, 64, 16
DEG = 8
E0, E1, E2 = N0 * DEG, N1 * DEG, N2 * DEG
EDGES = 2816
TILES = ((0, 1024), (1024, 1024), (2048, 768))
WIDE = EDGES // 2
PARTS = 2
SMALL = 320
COARSE = N1 + N2
BLOCK = 144
QUARTER = HALF // 2
PACK = C + 3 * HALF
VMEM_MIB = 24
AUG = HID + 16
BF = jnp.bfloat16
F32 = jnp.float32
ROW_AXES = ("yl", "z", "x")
DP_AXES = ROW_AXES + ("core",)


def mm(left, right, contract=(1, 0)):
    return lax.dot_general(
        left, right, (((contract[0],), (contract[1],)), ((), ())), preferred_element_type=F32
    )


def pieces(value, count):
    parts = []
    for _ in range(count):
        part = value.astype(BF)
        parts.append(part)
        value = value - part.astype(F32)
    return parts


def mm_hot(value, hot, contract, count=2):
    rows = value.shape[0]
    product = mm(jnp.concatenate(pieces(value, count), axis=0), hot, contract)
    total = product[:rows]
    for index in range(1, count):
        total = total + product[index * rows : (index + 1) * rows]
    return total


def hot(rows, index):
    lanes = index.shape[1]
    match = lax.broadcasted_iota(jnp.int32, (rows, lanes), 0) == index
    return jnp.where(match, 1.0, 0.0).astype(BF)


def owner_hot(rows, lanes):
    index = lax.broadcasted_iota(jnp.int32, (rows, lanes), 1) & (rows - 1)
    match = lax.broadcasted_iota(jnp.int32, (rows, lanes), 0) == index
    return jnp.where(match, 1.0, 0.0).astype(BF)


def gelu(value):
    inner = value * (0.7978845608028654 + 0.035677408136300125 * (value * value))
    return value * (0.5 + 0.5 * jnp.tanh(inner))


def gelu_both(value):
    square = value * value
    inner = value * (0.7978845608028654 + 0.035677408136300125 * square)
    share = 0.5 + 0.5 * jnp.tanh(inner)
    slope = share + (share * (1.0 - share)) * (
        value * (1.5957691216057308 + 0.21406444881780074 * square)
    )
    return value * share, slope


def level_rows(rows_ref):
    return (
        rows_ref[0:1, :], rows_ref[1:2, 0:N1], rows_ref[3:4, 0:N2], rows_ref[4:5, :]
    )


def gather_sources(state, half, hot_refs, parents_ref, rows_ref, weight_ref, vw_ref, vals):
    live, child_mid, child_top, share = level_rows(rows_ref)
    start = pl.multiple_of(half * HALF, HALF)
    wide = state.astype(F32)
    mid = mm((wide * live).astype(BF), parents_ref[0:N1, :], (1, 1)) / child_mid
    top = mm_hot(wide * share, parents_ref[N1:COARSE, :], (1, 1), 3) / child_top
    vals[:, 0:N0] = wide
    vals[:, N0 : N0 + N1] = mid
    vals[:, N0 + 128 : N0 + 128 + N2] = top
    place = pl.ds(start, HALF)
    values = (
        vals[place, 0:N0], vals[place, N0 : N0 + N1], vals[place, N0 + 128 : N0 + 128 + N2]
    )
    lanes = 0
    for hot_ref, value in zip(hot_refs, values):
        count = hot_ref.shape[1]
        vw_ref[:, lanes : lanes + count] = (
            mm(value.astype(BF), hot_ref[...]) * weight_ref[:, lanes : lanes + count]
        )
        lanes += count
    vw_ref[:, lanes:] = jnp.zeros((HALF, EDGES - lanes), F32)


def halves(body):
    def step(index, carry):
        body(pl.ds(pl.multiple_of(index * WIDE, WIDE), WIDE))
        return carry

    lax.fori_loop(0, 2, step, 0)


def channel_parts(body, parts):
    def step(index, carry):
        rows, channels = HALF * C // parts, HALF // parts
        body(
            pl.ds(pl.multiple_of(index * rows, rows), rows),
            pl.ds(pl.multiple_of(index * channels, channels), channels),
        )
        return carry

    lax.fori_loop(0, parts, step, 0)


def message_pass(
    layer, h2_ref, parents_ref, owner_ref, wkt_ref, bias_ref, vw_ref, up_ref, msg, *kept_refs
):
    bias = bias_ref[layer]
    bias = jnp.concatenate([bias, bias], axis=1)
    for start, width in TILES:
        lanes = slice(start, start + width)
        msg[:, lanes] = mm(bias, jnp.concatenate(pieces(vw_ref[:, lanes], 2), axis=0))

    def part(rows, channels):
        for start, width in TILES:
            lanes = slice(start, start + width)
            source = vw_ref[channels, lanes]
            kernels = mm(wkt_ref[rows, :], h2_ref[0:HID, lanes])
            for kept_ref in kept_refs:
                kept_ref[rows, lanes] = kernels.astype(BF)
            total = msg[:, lanes]
            for channel in range(HALF // PARTS):
                total = total + (
                    kernels[channel * C : (channel + 1) * C] * source[channel : channel + 1, :]
                )
            msg[:, lanes] = total

    channel_parts(part, PARTS)
    total_fine = msg[:, 0:N0]
    for slot in range(1, DEG):
        total_fine = total_fine + msg[:, slot * N0 : (slot + 1) * N0]
    coarse = mm_hot(msg[:, E0:EDGES], owner_ref[...], (1, 1))
    up_ref[...] = total_fine + mm_hot(coarse, parents_ref[...], (1, 0))


def first_columns(packed_ref, layer):
    return packed_ref[HID : HID + 16, layer * 128 : (layer + 1) * 128].astype(F32).T.astype(BF)


def second_rows(packed_ref, far_ref, layer):
    rows = slice(layer * 128, (layer + 1) * 128)
    return jnp.concatenate([packed_ref[rows, :], far_ref[rows, :]], axis=0)


def ones_rows(width):
    return jnp.where(lax.broadcasted_iota(jnp.int32, (16, width), 0) == 0, 1.0, 0.0).astype(BF)


def pack_kernel(second_ref, first_ref, bias_ref, packed_ref, second, first, bias, rows, sems):
    copies = [
        pltpu.make_async_copy(source, target, sems.at[index])
        for index, (source, target) in enumerate(
            ((second_ref, second), (first_ref, first), (bias_ref, bias))
        )
    ]
    for copy in copies:
        copy.start()
    rows[...] = jnp.zeros_like(rows)
    for copy in copies:
        copy.wait()
    packed_ref[0:128, :] = second[0]
    packed_ref[128:256, :] = second[1]
    bias_rows = bias[...].astype(F32)
    for layer in range(2):
        lanes = slice(layer * 128, (layer + 1) * 128)
        for row in range(6):
            rows[row : row + 1, lanes] = first[row].astype(F32)[layer : layer + 1]
        rows[6:7, lanes] = bias_rows[layer : layer + 1]
    packed_ref[256:272, :] = rows[...].astype(BF)


def prep_kernel(
    count_ref, half_ref, packed_ref, geometry_hbm, pm_hbm, pt_hbm, near0_hbm, near1_hbm, near2_hbm,
    node_hbm, bk_hbm, bs_hbm, wk_hbm,
    edge_ref, weight_ref, hot0_ref, hot1_ref, hot2_ref, parents_ref, owner_ref, rows_ref, wkt0_ref,
    wkt1_ref,    bias_rows_ref, bias_cols_ref, bs_cols_ref, hown_ref, sown_ref, vw_ref, node_ref,
    index_ref, pm_ref, pt_ref, geometry_ref, near0_ref, near1_ref, near2_ref, bk_ref, bs_ref, wk_ref, sems, vals, bias_rows,
):
    copies = [
        pltpu.make_async_copy(source, target, sems.at[index])
        for index, (source, target) in enumerate(
            (
                (geometry_hbm, geometry_ref), (pm_hbm, pm_ref), (pt_hbm, pt_ref),
                (near0_hbm, near0_ref), (near1_hbm, near1_ref), (near2_hbm, near2_ref),
                (node_hbm, node_ref), (bk_hbm, bk_ref), (bs_hbm, bs_ref), (wk_hbm, wk_ref),
            )
        )
    ]
    for copy in copies:
        copy.start()
    for copy in copies[:-1]:
        copy.wait()
    live = jnp.where(
        lax.broadcasted_iota(jnp.int32, (1, N0), 1) < count_ref[0], 1.0, 0.0
    ).astype(F32)
    parent = hot(N1, pm_ref[...])
    parent_top = hot(N2, pt_ref[...])
    live8 = jnp.broadcast_to(live, (16, N0))
    child_mid = mm(live8.astype(BF), parent, (1, 1))
    live_mid = jnp.where(child_mid > 0.5, 1.0, 0.0)
    child_top = mm(live_mid.astype(BF), parent_top, (1, 1))
    live_top = jnp.where(child_top > 0.5, 1.0, 0.0)
    child_mid = jnp.maximum(child_mid, 1.0)
    child_top = jnp.maximum(child_top, 1.0)
    rows_ref[...] = jnp.zeros_like(rows_ref)
    rows_ref[0:1, :] = live
    rows_ref[1:2, 0:N1] = child_mid[0:1]
    rows_ref[2:3, 0:N1] = live_mid[0:1]
    rows_ref[3:4, 0:N2] = child_top[0:1]
    share = mm_hot(live_mid / child_mid, parent, (1, 0), 3)[0:1] * live
    rows_ref[4:5, :] = share
    parents_ref[0:N1, :] = parent
    composite = mm(parent_top, parent).astype(BF)
    parents_ref[N1:COARSE, :] = composite
    row = lax.broadcasted_iota(jnp.int32, owner_ref.shape, 0)
    lane = lax.broadcasted_iota(jnp.int32, owner_ref.shape, 1)
    mid_own = (lane < E1) & (row == (lane & (N1 - 1)))
    top_own = (lane >= E1) & (lane < E1 + E2) & (row == N1 + (lane & (N2 - 1)))
    owner_ref[...] = jnp.where(mid_own | top_own, 1.0, 0.0).astype(BF)
    index_ref[...] = jnp.zeros_like(index_ref)
    for slot in range(DEG):
        row = slice(slot, slot + 1)
        index_ref[:, slot * N0 : (slot + 1) * N0] = near0_ref[row, :]
        index_ref[:, E0 + slot * N1 : E0 + (slot + 1) * N1] = near1_ref[row, :]
        start = E0 + E1 + slot * N2
        index_ref[:, start : start + N2] = near2_ref[row, :]
    vals[0:16, 0:N0] = jnp.zeros((16, N0), F32)
    vals[0:3, 0:N0] = geometry_ref[...]
    coords = vals[0:16, 0:N0]
    coords_mid = mm_hot(coords * live, parent, (1, 1), 3) / child_mid
    coords_top = mm_hot(coords * share, composite, (1, 1), 3) / child_top
    lane_row = lax.broadcasted_iota(jnp.int32, (16, 1), 0)

    def with_live(values, live_row):
        return jnp.where(lane_row == 3, live_row, values).astype(BF)

    fine_rows = with_live(coords, live)
    mid_rows = with_live(coords_mid, live_mid[0:1])
    top_rows = with_live(coords_top, live_top[0:1])

    def edges(own, near):
        low = jnp.where(lane_row < 3, own, 0.0)
        high = pltpu.roll(jnp.where(lane_row < 3, near, 0.0), 3, 0)
        return jnp.where(lane_row == 6, 1.0, low + high).astype(BF)

    fine = fine_rows.astype(F32)
    masks = []
    for slot in range(DEG):
        lanes = slice(slot * N0, (slot + 1) * N0)
        hot0_ref[:, lanes] = hot(N0, index_ref[:, lanes])
        near = mm(fine_rows, hot0_ref[:, lanes])
        edge_ref[:, lanes] = edges(fine, near)
        masks.append(live * near[3:4])
    total = masks[0]
    for mask in masks[1:]:
        total = total + mask
    total = jnp.maximum(total, 1.0)
    for slot in range(DEG):
        weight_ref[:, slot * N0 : (slot + 1) * N0] = masks[slot] / total

    def small_level(values, rows, start, lanes, hot_ref):
        own = mm(values, owner_hot(rows, lanes))
        hot_ref[...] = hot(rows, index_ref[:, start : start + lanes])
        near = mm(values, hot_ref[...])
        edge_ref[:, start : start + lanes] = edges(own, near)
        mask = own * near
        fold = jnp.where(
            (lax.broadcasted_iota(jnp.int32, (lanes, lanes), 0) & (rows - 1))
            == (lax.broadcasted_iota(jnp.int32, (lanes, lanes), 1) & (rows - 1)),
            1.0,
            0.0,
        ).astype(BF)
        total = jnp.maximum(mm(mask.astype(BF), fold), 1.0)
        weight_ref[:, start : start + lanes] = mask[3:4] / total[3:4]

    small_level(mid_rows, N1, E0, E1, hot1_ref)
    small_level(top_rows, N2, E0 + E1, E2, hot2_ref)
    rest = E0 + E1 + E2
    edge_ref[:, rest:] = jnp.zeros((16, EDGES - rest), BF)
    weight_ref[:, rest:] = jnp.zeros((1, EDGES - rest), F32)
    gather_sources(
        node_ref[...], half_ref[0], (hot0_ref, hot1_ref, hot2_ref), parents_ref, rows_ref,
        weight_ref, vw_ref, vals,
    )
    bias = bk_ref[...].astype(F32)
    copies[-1].wait()
    for layer in range(2):
        for part in range(8):
            (wkt0_ref, wkt1_ref)[layer][part * 256 : (part + 1) * 256, :] = wk_ref[
                layer, :, part * 256 : (part + 1) * 256
            ].T
        for row in range(HALF):
            bias_rows[row : row + 1, :] = bias[layer : layer + 1, row * C : (row + 1) * C]
        bias_rows_ref[layer] = bias_rows[...].astype(BF)
        bias_cols_ref[layer] = bias_rows[...].T.astype(BF)
    for layer in range(2):
        value, slope = gelu_both(mm(first_columns(packed_ref, layer), edge_ref[...]))
        hown_ref[layer] = value.astype(BF)
        sown_ref[layer] = slope.astype(BF)
    second_bias = jnp.concatenate([bs_ref[...].astype(F32), jnp.zeros((6, HID), F32)], axis=0)
    bs_cols_ref[...] = second_bias.T


def first_forward_kernel(
    parents_ref, owner_ref, packed_ref, far_ref, edge_ref, hown_ref, bs_ref, wkt_ref, bias_ref, vw_ref,
    h2_ref, up_ref, msg,
):
    second = second_rows(packed_ref, far_ref, 0).T
    first = first_columns(far_ref, 0)
    bias = bs_ref[:, 0:1]

    def body(lanes):
        away = gelu(mm(first, edge_ref[:, lanes])).astype(BF)
        one = jnp.concatenate([hown_ref[0, :, lanes], away], axis=0)
        h2_ref[0:HID, lanes] = gelu(mm(second, one) + bias).astype(BF)

    halves(body)
    h2_ref[HID:AUG, :] = ones_rows(EDGES)
    message_pass(
        0, h2_ref, parents_ref, owner_ref, wkt_ref, bias_ref, vw_ref, up_ref, msg,
    )


def mlp_kernel(
    layer, packed_ref, far_ref, edge_ref, bs_ref, hown_ref, sown_ref, h1_ref, s1_ref, s2_ref,
    *h2_refs
):
    second = second_rows(packed_ref, far_ref, layer).T
    first = first_columns(far_ref, layer)
    bias = bs_ref[:, layer : layer + 1]

    def body(lanes):
        value, slope = gelu_both(mm(first, edge_ref[:, lanes]))
        one = jnp.concatenate([hown_ref[layer, :, lanes], value.astype(BF)], axis=0)
        h1_ref[0:HID, lanes] = one
        s1_ref[0:128, lanes] = sown_ref[layer, :, lanes]
        s1_ref[128:HID, lanes] = slope.astype(BF)
        value, slope = gelu_both(mm(second, one) + bias)
        s2_ref[:, lanes] = slope.astype(BF)
        for h2_ref in h2_refs:
            h2_ref[0:HID, lanes] = value.astype(BF)

    halves(body)
    h1_ref[HID:AUG, :] = edge_ref[...]
    for h2_ref in h2_refs:
        h2_ref[HID:AUG, :] = ones_rows(EDGES)


def next_forward_kernel(
    half_ref, node_ref, self_ref, up_own_ref, up_far_ref, hot0_ref, hot1_ref, hot2_ref, parents_ref,
    owner_ref, rows_ref, weight_ref, h2_ref, wkt_ref, bias_ref,
    pre_ref, state_ref, up_ref, vw_ref, kept_ref, vals, msg,
):
    pre = mm(self_ref[0].astype(F32).T.astype(BF), node_ref[...])
    pre = pre + (up_own_ref[...] + up_far_ref[...])
    pre_ref[...] = pre
    state = (gelu(pre) * rows_ref[0:1, :]).astype(BF)
    state_ref[...] = state
    gather_sources(
        state, half_ref[0], (hot0_ref, hot1_ref, hot2_ref), parents_ref, rows_ref, weight_ref,
        vw_ref, vals,
    )
    message_pass(
        1, h2_ref, parents_ref, owner_ref, wkt_ref, bias_ref, vw_ref, up_ref, msg, kept_ref,
    )


def node_grads(
    layer, half, h, pre, grad, parents_ref, owner_ref, live, self_ref, own_ref, g_ref
):
    start = pl.multiple_of(half * HALF, HALF)
    _, slope = gelu_both(pre)
    grad_pre = slope * (live * grad)
    high, low = pieces(grad_pre, 2)
    grad_self = mm(h, high, (1, 1)) + mm(h, low, (1, 1))
    own_ref[288:320, 0:C] = grad_self[0:HALF]
    own_ref[288:320, C : 2 * C] = grad_self[HALF:C]
    self_half = self_ref[layer, pl.ds(start, HALF), :]
    self_in = mm(self_half, high) + mm(self_half, low)
    coarse = mm_hot(grad_pre, parents_ref[...], (1, 1), 3).astype(BF)
    g_ref[0:C, 0:N0] = grad_pre.astype(BF)
    g_ref[0:C, N0:] = mm(coarse, owner_ref[...]).astype(BF)
    return self_in


def grad_tile(g_ref, start, width):
    if start < E0:
        return jnp.concatenate([g_ref[0:C, 0:N0]] * (width // N0), axis=1)
    return g_ref[0:C, N0 : N0 + width]


def source_grads(self_in, hot_refs, parents_ref, rows_ref, dvw):
    live, child_mid, child_top, share = level_rows(rows_ref)
    sums = []
    lanes = 0
    for hot_ref in hot_refs:
        count = hot_ref.shape[1]
        total = mm_hot(dvw[:, lanes : lanes + count], hot_ref[...], (1, 1))
        sums.append(total.astype(BF).astype(F32))
        lanes += count
    fine, mid, top = sums
    return (
        self_in
        + fine
        + mm_hot(mid / child_mid, parents_ref[0:N1, :], (1, 0), 3) * live
        + mm_hot(top / child_top, parents_ref[N1:COARSE, :], (1, 0), 3) * share
    )


def fill_pack(core, vw_ref, pack_ref):
    place = pl.ds(pl.multiple_of((1 - core) * QUARTER, QUARTER), QUARTER)
    for index, (start, width) in enumerate(TILES):
        high, low = pieces(vw_ref[place, start : start + width], 2)
        base = C + index * HALF
        pack_ref[base : base + QUARTER, 0:width] = high
        pack_ref[base + QUARTER : base + HALF, 0:width] = low
    pack_ref[C + 2 * HALF : PACK, 768:1024] = jnp.zeros((HALF, 256), BF)


def far_source(pack_ref, index, width):
    base = C + index * HALF
    high = pack_ref[base : base + QUARTER, 0:width].astype(F32)
    return high + pack_ref[base + QUARTER : base + HALF, 0:width].astype(F32)


def fill_grad_kernels(g_ref, source, gk, start, width, rows):
    lanes = slice(start, start + width)
    grad = grad_tile(g_ref, start, width).astype(F32)
    for row in range(rows):
        gk[row * C : (row + 1) * C, lanes] = (grad * source[row : row + 1, :]).astype(BF)


def mlp_backward(
    layer, g_ref, vw_ref, wk_ref, h1_ref, s1_ref, s2_ref, packed_ref, far_ref, own_ref, away_ref,
    gk, both,
):
    second = second_rows(packed_ref, far_ref, layer)
    for start, width in TILES:
        lanes = slice(start, start + width)
        fill_grad_kernels(g_ref, vw_ref[:, lanes], gk, start, width, HALF)
        two = (s2_ref[:, lanes].astype(F32) * mm(wk_ref[layer], gk[:, lanes])).astype(BF)
        both[0:HID, lanes] = two
        both[HID:, lanes] = (s1_ref[:, lanes].astype(F32) * mm(second, two)).astype(BF)
    product = mm(h1_ref[...], both[...], (1, 1))
    grad_second = product[0:HID, 0:HID]
    grad_first = product[HID : HID + 7, HID:]
    grad_bias = product[HID + 6 : HID + 7, 0:HID]
    own_ref[0:128, :] = grad_second[0:128, 0:128]
    own_ref[128:256, :] = grad_second[0:128, 128:256]
    own_ref[272:273, :] = grad_bias[:, 0:128]
    own_ref[273:274, :] = grad_bias[:, 128:256]
    own_ref[274:281, :] = grad_first[:, 0:128]
    own_ref[281:288, :] = jnp.zeros((7, 128), F32)
    away_ref[0:128, :] = grad_second[128:256, 0:128].astype(BF)
    away_ref[128:256, :] = grad_second[128:256, 128:256].astype(BF)
    tail = jnp.concatenate(
        [grad_bias[:, 0:128], grad_bias[:, 128:256], grad_first[:, 128:256],
         jnp.zeros((7, 128), F32)],
        axis=0,
    )
    away_ref[256:272, :] = tail.astype(BF)


def kernel_weight_kernel(
    core_ref, *refs
):
    layer_refs = (refs[0:5], refs[5:10])
    bias_ref, joined_hbm, gk, joined_ref, sems = refs[10:]
    mine = pl.ds(pl.multiple_of(core_ref[0] * QUARTER, QUARTER), QUARTER)
    copies = []
    for layer in (1, 0):
        pack_ref, far_ref, vw_ref, h2_ref, h2_far_ref = layer_refs[layer]
        for index, (start, width) in enumerate(TILES):
            source = vw_ref[mine, start : start + width]
            fill_grad_kernels(pack_ref, source, gk, start, width, QUARTER)
        product = mm(h2_ref[...], gk[...], (1, 1))
        for index, (start, width) in enumerate(TILES):
            source = far_source(far_ref, index, width)
            fill_grad_kernels(far_ref, source, gk, start, width, QUARTER)
        product = product + mm(h2_far_ref[...], gk[...], (1, 1))
        for part in range(4):
            for block in range(8):
                joined_ref[layer, part * 8 + block] = product[
                    part * 64 : (part + 1) * 64, block * 128 : (block + 1) * 128
                ].astype(BF)
        copy = pltpu.make_async_copy(
            joined_ref.at[layer], joined_hbm.at[:, layer * 64 : (layer + 1) * 64, :], sems.at[layer]
        )
        copy.start()
        copies.append(copy)
        for block in range(8):
            row = layer * 8 + block
            bias_ref[row : row + 1, :] = product[HID : HID + 1, block * 128 : (block + 1) * 128]
    for copy in copies:
        copy.wait()


def last_node_kernel(
    half_ref, core_ref, state_ref, self_ref, up_own_ref, up_far_ref, cot_ref, hot0_ref, hot1_ref,
    hot2_ref, parents_ref, owner_ref, rows_ref, weight_ref, kept_ref, bias_ref, vw_ref,
    out_ref, own_ref, g_ref, dx_ref, dvw, wide,
):
    fill_pack(core_ref[0], vw_ref, g_ref)
    live = rows_ref[0:1, :]
    state = state_ref[...]
    pre = mm(self_ref[1].astype(F32).T.astype(BF), state)
    pre = pre + (up_own_ref[...] + up_far_ref[...])
    out_ref[...] = (gelu(pre) * live).astype(BF)
    self_in = node_grads(
        1, half_ref[0], state, pre, cot_ref[...].astype(F32), parents_ref, owner_ref, live,
        self_ref, own_ref, g_ref,
    )
    for start, width in TILES:
        wide[:, start : start + width] = grad_tile(g_ref, start, width)
    offset = mm(bias_ref[1], wide[...])
    for start, width in TILES:
        lanes = slice(start, start + width)
        grad = wide[:, lanes].astype(F32)
        for part in range(4):
            channels = slice(part * 8, (part + 1) * 8)
            kernels = kept_ref[part * 512 : (part + 1) * 512, lanes].astype(F32)
            total = jnp.sum(kernels.reshape(8, C, width) * grad[None], axis=1)
            dvw[channels, lanes] = (total + offset[channels, lanes]) * weight_ref[:, lanes]
    dx_ref[...] = source_grads(
        self_in, (hot0_ref, hot1_ref, hot2_ref), parents_ref, rows_ref, dvw
    )


def last_edge_kernel(
    core_ref, g_ref, vw_ref, wk_ref, h1_ref, s1_ref, s2_ref, packed_ref, far_ref, self_grad_ref,
    own_ref, away_ref, cross_ref, gk, both,
):
    mlp_backward(
        1, g_ref, vw_ref, wk_ref, h1_ref, s1_ref, s2_ref, packed_ref, far_ref, own_ref, away_ref,
        gk, both,
    )
    own_ref[256:272, :] = jnp.zeros((16, 128), F32)
    own_ref[288:320, :] = self_grad_ref[288:320, :]
    other = pl.ds(pl.multiple_of((1 - core_ref[0]) * 128, 128), 128)
    cross_ref[0:128, :] = own_ref[other, :].astype(BF)
    cross_ref[128:256, :] = away_ref[other, :]


def first_edge_kernel(
    half_ref, core_ref, node_ref, pre_ref, dx_own_ref, dx_far_ref, self_ref, parents_ref, owner_ref,
    rows_ref,
    vw_ref, wk_ref, h1_ref, s1_ref, s2_ref, packed_ref, far_ref,
    g_ref, self_in_ref, own_ref, away_ref, grad, gk, both,
):
    fill_pack(core_ref[0], vw_ref, g_ref)
    start = pl.multiple_of(half_ref[0] * HALF, HALF)
    grad[pl.ds(start, HALF), :] = dx_own_ref[...]
    grad[pl.ds(HALF - start, HALF), :] = dx_far_ref[...]
    self_in_ref[...] = node_grads(
        0, half_ref[0], node_ref[...], pre_ref[...], grad[...], parents_ref, owner_ref,
        rows_ref[0:1, :], self_ref, own_ref, g_ref,
    )
    own_ref[256:272, :] = jnp.zeros((16, 128), F32)
    mlp_backward(
        0, g_ref, vw_ref, wk_ref, h1_ref, s1_ref, s2_ref, packed_ref, far_ref, own_ref,
        away_ref, gk, both,
    )


def first_node_kernel(
    self_in_ref, hot0_ref, hot1_ref, hot2_ref, parents_ref, rows_ref, weight_ref, h2_ref, wkt_ref,
    bias_ref, g_ref,
    dx_ref, dvw,
):

    def part(rows, channels):
        for start, width in TILES:
            lanes = slice(start, start + width)
            grad = grad_tile(g_ref, start, width)
            offset = mm(bias_ref[0, channels, :], grad)
            kernels = mm(wkt_ref[rows, :], h2_ref[0:HID, lanes])
            product = kernels.reshape(HALF // PARTS, C, width) * grad.astype(F32)[None]
            dvw[channels, lanes] = (jnp.sum(product, axis=1) + offset) * weight_ref[:, lanes]

    channel_parts(part, PARTS)
    dx_ref[...] = source_grads(
        self_in_ref[...], (hot0_ref, hot1_ref, hot2_ref), parents_ref, rows_ref, dvw
    )


def pair_kernel(core_ref, own1_ref, away1_ref, cross_ref, away0_ref, mine1_ref, away_ref):
    away_ref[0:AUG, :] = away0_ref[...]
    mine = pl.ds(pl.multiple_of(core_ref[0] * 128, 128), 128)
    mine1_ref[...] = own1_ref[mine, :] + cross_ref[0:128, :].astype(F32)
    away_ref[AUG : AUG + 128, :] = (
        away1_ref[mine, :].astype(F32) + cross_ref[128:256, :].astype(F32)
    ).astype(BF)
    away_ref[AUG + 128 :, :] = away1_ref[256:272, :]


def join_kernel(
    core_ref, own0_ref, own1_ref, mine1_ref, away_ref, bias_ref, _, out_ref, rows, tail, sem
):
    far = away_ref[...].astype(F32)
    rows[0:256, :] = own0_ref[0:256, :] + far[0:256]
    rows[SMALL : SMALL + 128, :] = mine1_ref[...] + far[AUG : AUG + 128]
    for layer, (own_ref, base, place) in enumerate(
        ((own0_ref, 256, 256), (own1_ref, SMALL + 128, AUG + 128))
    ):
        rows[base : base + 16, :] = jnp.zeros((16, 128), F32)
        bias = pl.ds(pl.multiple_of(base + core_ref[0] * 8, 8), 8)
        rows[bias, :] = bias_ref[layer * 8 : (layer + 1) * 8, :]
        rows[base + 16 : base + 32, :] = own_ref[272:288, :] + far[place : place + 16]
        rows[base + 32 : base + 64, :] = own_ref[288:320, :]
    for block in range(32):
        tail[block] = rows[block * 16 : (block + 1) * 16, :].astype(BF)
    copy = pltpu.make_async_copy(tail, out_ref.at[:, 128:BLOCK, :], sem.at[0])
    copy.start()
    copy.wait()


def sum_kernel(parts_ref, out_ref):
    total = parts_ref[0].astype(F32)
    for peer in range(1, 32):
        total = total + parts_ref[peer].astype(F32)
    total = total.astype(BF)
    for peer in range(32):
        out_ref[peer] = total


def spread_blocks(side_ref, kernel_ref):
    part = pl.program_id(0)
    for block in range(8):
        for layer in range(2):
            kernel_ref[layer, :, block * 128 : (block + 1) * 128] = side_ref[
                part * 8 + block, layer * 64 : (layer + 1) * 64, :
            ].astype(F32)


def spread_own_kernel(core_ref, own_ref, kernel_ref):
    spread_blocks(own_ref, kernel_ref)


def spread_far_kernel(
    core_ref, own_ref, far_ref, _,
    kernel_ref, second_ref, second_bias_ref, first_ref, first_bias_ref, kernel_bias_ref, self_ref,
    rows,
):
    spread_blocks(far_ref, kernel_ref)

    @pl.when(pl.program_id(0) == 1)
    def _():
        spread_small(
            core_ref[0], own_ref, far_ref, second_ref, second_bias_ref, first_ref, first_bias_ref,
            kernel_bias_ref, self_ref, rows,
        )


def spread_small(
    core, own_ref, far_ref, second_ref, second_bias_ref, first_ref, first_bias_ref,
    kernel_bias_ref, self_ref, rows,
):
    for block in range(32):
        own = own_ref[block, 128:BLOCK, :].astype(F32)
        far = far_ref[block, 128:BLOCK, :].astype(F32)
        if SMALL // 16 <= block < (SMALL + 128) // 16:
            place = slice(block * 16 - SMALL, block * 16 - SMALL + 16)
            second_ref[1, place, pl.ds(pl.multiple_of(core * 128, 128), 128)] = own
            second_ref[1, place, pl.ds(pl.multiple_of((1 - core) * 128, 128), 128)] = far
        else:
            rows[block * 16 : (block + 1) * 16, :] = own + far
    second_ref[0, :, 0:128] = rows[0:128, :]
    second_ref[0, :, 128:256] = rows[128:256, :]
    for layer, base in enumerate((256, SMALL + 128)):
        for block in range(16):
            lanes = slice(block * 128, (block + 1) * 128)
            kernel_bias_ref[layer : layer + 1, lanes] = rows[base + block : base + block + 1, :]
        second_bias_ref[layer : layer + 1, 0:128] = rows[base + 16 : base + 17, :]
        second_bias_ref[layer : layer + 1, 128:256] = rows[base + 17 : base + 18, :]
        for row in range(6):
            first_ref[row, layer : layer + 1, :] = rows[base + 18 + row : base + 19 + row, :]
        first_bias_ref[layer : layer + 1, :] = rows[base + 24 : base + 25, :]
        self_ref[layer, 0:HALF, :] = rows[base + 32 : base + 64, 0:C]
        self_ref[layer, HALF:C, :] = rows[base + 32 : base + 64, C : 2 * C]


def input_kernel(half_ref, own_ref, far_ref, out_ref):
    start = pl.multiple_of(half_ref[0] * HALF, HALF)
    out_ref[pl.ds(start, HALF), :] = own_ref[...]
    out_ref[pl.ds(HALF - start, HALF), :] = far_ref[...]


def vmem_spec():
    return pl.BlockSpec(memory_space=pltpu.VMEM)


def smem_spec():
    return pl.BlockSpec(memory_space=pltpu.SMEM)


def call(kernel, outs, args, scalars=0, scratch=(), us=1, far=0, far_outs=0, aliases=None):
    count = len(args)
    specs = [smem_spec()] * scalars + [vmem_spec()] * (count - scalars - far)
    args = list(args[: count - far]) + [
        pltpu.with_memory_space_constraint(value, pltpu.HBM) for value in args[count - far :]
    ]
    return pl.pallas_call(
        kernel,
        out_shape=[
            pltpu.HBM(*out) if index >= len(outs) - far_outs else jax.ShapeDtypeStruct(*out)
            for index, out in enumerate(outs)
        ],
        in_specs=specs + [pl.BlockSpec(memory_space=pltpu.HBM)] * far,
        out_specs=[
            pl.BlockSpec(memory_space=pltpu.HBM) if index >= len(outs) - far_outs else vmem_spec()
            for index in range(len(outs))
        ],
        scratch_shapes=[
            pltpu.SemaphoreType.DMA(entry[0]) if entry[1] is None else pltpu.VMEM(*entry)
            for entry in scratch
        ],
        input_output_aliases=aliases or {},
        compiler_params=pltpu.CompilerParams(vmem_limit_bytes=VMEM_MIB << 20),
        cost_estimate=pl.CostEstimate(
            flops=us * 1000000000, bytes_accessed=1 << 20, transcendentals=0
        ),
    )(*args)


def swap(value, axis):
    return lax.ppermute(value, axis, [(0, 1), (1, 0)])


def per_device(
    node_input, geometry, counts, parent_mid, parent_top, neighbours_fine, neighbours_mid,
    neighbours_top, w_first, b_first, w_second, b_second, w_kernel, b_kernel, w_self, cotangent,
):
    half = lax.axis_index("tensor").astype(jnp.int32).reshape(1)
    core = lax.axis_index("core").astype(jnp.int32).reshape(1)
    counts, half, core, w_second = lax.optimization_barrier((counts, half, core, w_second))
    pm = parent_mid.reshape(1, N0)
    pt = parent_top.reshape(1, N1)
    node = node_input.T
    wide = (AUG, EDGES)
    edges = (HID, EDGES)
    sources = (HALF, EDGES)

    (packed,) = call(
        pack_kernel,
        [((AUG, HID), BF)],
        [w_second, w_first.transpose(1, 0, 2), b_first],
        scratch=[((2, 128, HID), BF), ((6, 2, 128), BF), ((2, 128), BF), ((16, HID), F32),
                 ((3,), None)],
        far=3,
    )
    far = swap(packed, "tensor")
    (
        edge, weight, hot0, hot1, hot2, parents, owner, rows, wkt0, wkt1, bias_rows, bias_cols,
        bs_cols,
        hown, sown, vw0, node,
    ) = call(
        prep_kernel,
        [((16, EDGES), BF), ((1, EDGES), F32), ((N0, E0), BF), ((N1, E1), BF), ((N2, E2), BF),
         ((COARSE, N0), BF), ((COARSE, EDGES - E0), BF), ((8, N0), F32), ((HALF * C, HID), BF), ((HALF * C, HID), BF), ((2, HALF, C), BF), ((2, C, HALF), BF), ((HID, 8), F32),
         ((2, 128, EDGES), BF), ((2, 128, EDGES), BF),
         (sources, F32), ((C, N0), BF)],
        [counts, half, packed, geometry.T, pm, pt, neighbours_fine.T, neighbours_mid.T,
         neighbours_top.T, node, b_kernel, b_second, w_kernel],
        scalars=2,
        far=10,
        scratch=[((1, EDGES), jnp.int32), ((1, N0), jnp.int32), ((1, N1), jnp.int32),
                 ((3, N0), F32), ((8, N0), jnp.int32), ((8, N1), jnp.int32), ((8, N2), jnp.int32),
                 ((2, HALF * C), BF), ((2, HID), BF), ((2, HID, HALF * C), BF), ((10,), None),
                 ((C, N0 + 256), F32), ((HALF, C), F32)],
        us=4,
    )
    h2_0, up0 = call(
        first_forward_kernel,
        [(wide, BF), ((C, N0), F32)],
        [parents, owner, packed, far, edge, hown, bs_cols, wkt0, bias_cols, vw0],
        scratch=[((C, EDGES), F32)],
        us=8,
    )
    up0_far = swap(up0, "tensor")
    h2_0_far = swap(h2_0, "core")

    def mlp(layer, outs):
        return call(
            functools.partial(mlp_kernel, layer), outs, [packed, far, edge, bs_cols, hown, sown], us=5
        )

    h1_1, s1_1, s2_1, h2_1 = mlp(1, [(wide, BF), (edges, BF), (edges, BF), (wide, BF)])
    pre0, state, up1, vw1, kept = call(
        next_forward_kernel,
        [((C, N0), F32), ((C, N0), BF), ((C, N0), F32), (sources, F32), ((HALF * C, EDGES), BF)],
        [half, node, w_self, up0, up0_far, hot0, hot1, hot2, parents, owner, rows, weight, h2_1, wkt1,
         bias_cols],
        scalars=1,
        scratch=[((C, N0 + 256), F32), ((C, EDGES), F32)],
        us=5,
    )
    up1_far = swap(up1, "tensor")
    h2_1_far = swap(h2_1, "core")
    up1, edge = lax.optimization_barrier((up1, edge))
    h1_0, s1_0, s2_0 = mlp(0, [(wide, BF), (edges, BF), (edges, BF)])
    h1_0, state = lax.optimization_barrier((h1_0, state))
    out, self_grad1, g1, dx1 = call(
        last_node_kernel,
        [((C, N0), BF), ((SMALL, 128), F32), ((PACK, 1024), BF), ((HALF, N0), F32)],
        [half, core, state, w_self, up1, up1_far, cotangent.T, hot0, hot1, hot2, parents, owner,
         rows, weight, kept, bias_rows, vw1],
        scalars=2,
        scratch=[(sources, F32), ((C, EDGES), BF)],
        us=5,
    )
    dx1_far = swap(dx1, "tensor")
    g1_far = swap(g1, "core")
    edge_scratch = [((HALF * C, EDGES), BF), ((2 * HID, EDGES), BF)]
    own1, away1, cross = call(
        last_edge_kernel,
        [((SMALL, 128), F32), ((AUG, 128), BF), ((256, 128), BF)],
        [core, g1, vw1, w_kernel, h1_1, s1_1, s2_1, packed, far, self_grad1],
        scalars=1,
        scratch=edge_scratch,
        us=5,
    )
    cross_far = swap(cross, "core")
    own1, dx1 = lax.optimization_barrier((own1, dx1))
    g0, self_in0, own0, away0 = call(
        first_edge_kernel,
        [((PACK, 1024), BF), ((HALF, N0), F32), ((SMALL, 128), F32), ((AUG, 128), BF)],
        [half, core, node, pre0, dx1, dx1_far, w_self, parents, owner, rows, vw0, w_kernel, h1_0, s1_0, s2_0,
         packed, far],
        scalars=2,
        scratch=[((C, N0), F32)] + edge_scratch,
        us=6,
    )
    mine1, away = call(
        pair_kernel,
        [((128, 128), F32), ((AUG + 144, 128), BF)],
        [core, own1, away1, cross_far, away0],
        scalars=1,
    )
    away_far = swap(away, "tensor")
    g0_far = swap(g0, "core")
    blocks = (32, BLOCK, 128)
    bias, joined = call(
        kernel_weight_kernel,
        [((16, 128), F32), (blocks, BF)],
        [core, g0, g0_far, vw0, h2_0, h2_0_far, g1, g1_far, vw1, h2_1, h2_1_far],
        scalars=1,
        scratch=[((QUARTER * C, EDGES), BF), ((2, 32, 64, 128), BF), ((2,), None)],
        us=8,
        far_outs=1,
    )
    (joined,) = call(
        join_kernel, [(blocks, BF)], [core, own0, own1, mine1, away_far, bias, joined],
        scalars=1,
        far=1,
        far_outs=1,
        scratch=[((512, 128), F32), ((32, 16, 128), BF), ((1,), None)],
        aliases={6: 0},
    )
    joined, g0 = lax.optimization_barrier((joined, g0))
    parts = lax.all_to_all(joined, ROW_AXES, 0, 0, tiled=True)
    (dx0,) = call(
        first_node_kernel,
        [((HALF, N0), F32)],
        [self_in0, hot0, hot1, hot2, parents, rows, weight, h2_0, wkt0, bias_rows, g0],
        scratch=[(sources, F32)],
        us=5,
    )
    (total,) = call(sum_kernel, [(blocks, BF)], [parts])
    dx0_far = swap(dx0, "tensor")
    total, dx0_far = lax.optimization_barrier((total, dx0_far))
    whole = lax.all_to_all(total, ROW_AXES, 0, 0, tiled=True)
    whole_far = swap(whole, "core")
    (input_grad,) = call(
        input_kernel, [((C, N0), F32)], [half, dx0, dx0_far], scalars=1
    )
    grad_shape = jax.ShapeDtypeStruct((2, HID, HALF * C), F32)
    params = pltpu.CompilerParams(vmem_limit_bytes=VMEM_MIB << 20)
    (grad_kernel,) = pl.pallas_call(
        spread_own_kernel,
        out_shape=[grad_shape],
        grid_spec=pltpu.PrefetchScalarGridSpec(
            num_scalar_prefetch=1,
            grid=(4,),
            in_specs=[vmem_spec()],
            out_specs=[
                pl.BlockSpec((2, 64, QUARTER * C), lambda part, core: (0, part, core[0]))
            ],
        ),
        compiler_params=params,
    )(core, whole)
    small_shapes = (
        (2, 128, HID), (2, HID), (6, 2, 128), (2, 128), (2, HALF * C), (2, C, C)
    )
    grad_kernel, grad_second, grad_b_second, grad_first, grad_b_first, grad_b_kernel, grad_self = (
        pl.pallas_call(
            spread_far_kernel,
            out_shape=[grad_shape]
            + [jax.ShapeDtypeStruct(shape, F32) for shape in small_shapes],
            grid_spec=pltpu.PrefetchScalarGridSpec(
                num_scalar_prefetch=1,
                grid=(4,),
                in_specs=[vmem_spec(), vmem_spec(), pl.BlockSpec(memory_space=pl.ANY)],
                out_specs=[
                    pl.BlockSpec((2, 64, QUARTER * C), lambda part, core: (0, part, 1 - core[0]))
                ]
                + [vmem_spec() for _ in small_shapes],
                scratch_shapes=[pltpu.VMEM((512, 128), F32)],
            ),
            input_output_aliases={3: 0},
            compiler_params=params,
        )(core, whole, whole_far, grad_kernel)
    )
    return (
        out.T, input_grad.T, grad_first.transpose(1, 0, 2), grad_b_first, grad_second,
        grad_b_second, grad_kernel, grad_b_kernel, grad_self,
    )


def solution(mesh):
    fine = Mesh(mesh.devices.reshape(2, 4, 4, 2, 2), DP_AXES + ("tensor",))
    dp = DP_AXES
    placed = (
        P(dp, None), P(dp, None), P(dp), P(dp), P(dp), P(dp, None), P(dp, None), P(dp, None),
        P(None, None, "tensor"), P(None, "tensor"), P(None, "tensor", None), P(),
        P(None, None, "tensor"), P(None, "tensor"), P(), P(dp, None),
    )
    return jax.shard_map(
        per_device,
        mesh=fine,
        in_specs=placed,
        out_specs=(
            P(dp, None), P(dp, None), P(None, None, "tensor"), P(None, "tensor"),
            P(None, "tensor", None), P(), P(None, None, "tensor"), P(None, "tensor"), P(),
        ),
        check_vma=False,
    )
```

```python
import functools

import jax
import jax.numpy as jnp
from jax import lax
from jax.experimental import pallas as pl
from jax.experimental.pallas import tpu as pltpu
from jax.sharding import Mesh, PartitionSpec as P

C = 64
HALF = 32
HID = 256
N0, N1, N2 = 256, 64, 16
DEG = 8
E0, E1, E2 = N0 * DEG, N1 * DEG, N2 * DEG
EDGES = 2816
TILES = ((0, 1024), (1024, 1024), (2048, 768))
WIDE = EDGES // 2
FILLED = E0 + E1 + E2
PARTS = 2
SMALL = 320
COARSE = N1 + N2
BLOCK = 144
QUARTER = HALF // 2
PACK = C + 3 * HALF
VMEM_MIB = 24
AUG = HID + 16
BF = jnp.bfloat16
F32 = jnp.float32
ROW_AXES = ("yl", "z", "x")
DP_AXES = ROW_AXES + ("core",)


def mm(left, right, contract=(1, 0)):
    return lax.dot_general(
        left, right, (((contract[0],), (contract[1],)), ((), ())), preferred_element_type=F32
    )


def pieces(value, count):
    parts = []
    for _ in range(count):
        part = value.astype(BF)
        parts.append(part)
        value = value - part.astype(F32)
    return parts


def mm_hot(value, hot, contract, count=2):
    rows = value.shape[0]
    product = mm(jnp.concatenate(pieces(value, count), axis=0), hot, contract)
    total = product[:rows]
    for index in range(1, count):
        total = total + product[index * rows : (index + 1) * rows]
    return total


def hot(rows, index):
    lanes = index.shape[1]
    match = lax.broadcasted_iota(jnp.int32, (rows, lanes), 0) == index
    return jnp.where(match, 1.0, 0.0).astype(BF)


def owner_hot(rows, lanes):
    index = lax.broadcasted_iota(jnp.int32, (rows, lanes), 1) & (rows - 1)
    match = lax.broadcasted_iota(jnp.int32, (rows, lanes), 0) == index
    return jnp.where(match, 1.0, 0.0).astype(BF)


def gelu(value):
    inner = value * (0.7978845608028654 + 0.035677408136300125 * (value * value))
    return value * (0.5 + 0.5 * jnp.tanh(inner))


def gelu_both(value):
    square = value * value
    inner = value * (0.7978845608028654 + 0.035677408136300125 * square)
    share = 0.5 + 0.5 * jnp.tanh(inner)
    slope = share + (share * (1.0 - share)) * (
        value * (1.5957691216057308 + 0.21406444881780074 * square)
    )
    return value * share, slope


def level_rows(rows_ref):
    return (
        rows_ref[0:1, :], rows_ref[1:2, 0:N1], rows_ref[3:4, 0:N2], rows_ref[4:5, :]
    )


def gather_sources(state, half, hot_refs, parents_ref, rows_ref, weight_ref, vw_ref, vals):
    live, child_mid, child_top, share = level_rows(rows_ref)
    start = pl.multiple_of(half * HALF, HALF)
    wide = state.astype(F32)
    mid = mm((wide * live).astype(BF), parents_ref[0:N1, :], (1, 1)) / child_mid
    top = mm_hot(wide * share, parents_ref[N1:COARSE, :], (1, 1), 3) / child_top
    vals[:, 0:N0] = wide
    vals[:, N0 : N0 + N1] = mid
    vals[:, N0 + 128 : N0 + 128 + N2] = top
    place = pl.ds(start, HALF)
    values = (
        vals[place, 0:N0], vals[place, N0 : N0 + N1], vals[place, N0 + 128 : N0 + 128 + N2]
    )
    lanes = 0
    for hot_ref, value in zip(hot_refs, values):
        count = hot_ref.shape[1]
        vw_ref[:, lanes : lanes + count] = (
            mm(value.astype(BF), hot_ref[...]) * weight_ref[:, lanes : lanes + count]
        )
        lanes += count
    vw_ref[:, lanes:] = jnp.zeros((HALF, EDGES - lanes), F32)


def halves(body):
    def step(index, carry):
        body(pl.ds(pl.multiple_of(index * WIDE, WIDE), WIDE))
        return carry

    lax.fori_loop(0, 2, step, 0)


def channel_parts(body, parts):
    def step(index, carry):
        rows, channels = HALF * C // parts, HALF // parts
        body(
            pl.ds(pl.multiple_of(index * rows, rows), rows),
            pl.ds(pl.multiple_of(index * channels, channels), channels),
        )
        return carry

    lax.fori_loop(0, parts, step, 0)


def message_pass(
    layer, h2_ref, parents_ref, owner_ref, wkt_ref, bias_ref, vw_ref, up_ref, msg, *kept_refs
):
    bias = bias_ref[layer]
    bias = jnp.concatenate([bias, bias], axis=1)
    for start, width in TILES:
        lanes = slice(start, start + width)
        msg[:, lanes] = mm(bias, jnp.concatenate(pieces(vw_ref[:, lanes], 2), axis=0))

    def part(rows, channels):
        for start, width in TILES:
            lanes = slice(start, start + width)
            source = vw_ref[channels, lanes]
            kernels = mm(wkt_ref[rows, :], h2_ref[0:HID, lanes])
            for kept_ref in kept_refs:
                kept_ref[rows, lanes] = kernels.astype(BF)
            total = msg[:, lanes]
            for channel in range(HALF // PARTS):
                total = total + (
                    kernels[channel * C : (channel + 1) * C] * source[channel : channel + 1, :]
                )
            msg[:, lanes] = total

    channel_parts(part, PARTS)
    total_fine = msg[:, 0:N0]
    for slot in range(1, DEG):
        total_fine = total_fine + msg[:, slot * N0 : (slot + 1) * N0]
    coarse = mm_hot(msg[:, E0:EDGES], owner_ref[...], (1, 1))
    up_ref[...] = total_fine + mm_hot(coarse, parents_ref[...], (1, 0))


def first_columns(packed_ref, layer):
    return packed_ref[HID : HID + 16, layer * 128 : (layer + 1) * 128].astype(F32).T.astype(BF)


def second_rows(packed_ref, far_ref, layer):
    rows = slice(layer * 128, (layer + 1) * 128)
    return jnp.concatenate([packed_ref[rows, :], far_ref[rows, :]], axis=0)


def ones_rows(width):
    return jnp.where(lax.broadcasted_iota(jnp.int32, (16, width), 0) == 0, 1.0, 0.0).astype(BF)


def pack_kernel(second_ref, first_ref, bias_ref, packed_ref, second, first, bias, rows, sems):
    copies = [
        pltpu.make_async_copy(source, target, sems.at[index])
        for index, (source, target) in enumerate(
            ((second_ref, second), (first_ref, first), (bias_ref, bias))
        )
    ]
    for copy in copies:
        copy.start()
    rows[...] = jnp.zeros_like(rows)
    for copy in copies:
        copy.wait()
    packed_ref[0:128, :] = second[0]
    packed_ref[128:256, :] = second[1]
    bias_rows = bias[...].astype(F32)
    for layer in range(2):
        lanes = slice(layer * 128, (layer + 1) * 128)
        for row in range(6):
            rows[row : row + 1, lanes] = first[row].astype(F32)[layer : layer + 1]
        rows[6:7, lanes] = bias_rows[layer : layer + 1]
    packed_ref[256:272, :] = rows[...].astype(BF)


def prep_kernel(
    count_ref, half_ref, packed_ref, geometry_hbm, pm_hbm, pt_hbm, near0_hbm, near1_hbm, near2_hbm,
    node_hbm, bk_hbm, bs_hbm, wk_hbm,
    edge_ref, weight_ref, hot0_ref, hot1_ref, hot2_ref, parents_ref, owner_ref, rows_ref, wkt0_ref,
    wkt1_ref,    bias_rows_ref, bias_cols_ref, bs_cols_ref, hown_ref, sown_ref, vw_ref, node_ref,
    index_ref, pm_ref, pt_ref, geometry_ref, near0_ref, near1_ref, near2_ref, bk_ref, bs_ref, wk_ref, sems, vals, bias_rows,
):
    copies = [
        pltpu.make_async_copy(source, target, sems.at[index])
        for index, (source, target) in enumerate(
            (
                (geometry_hbm, geometry_ref), (pm_hbm, pm_ref), (pt_hbm, pt_ref),
                (near0_hbm, near0_ref), (near1_hbm, near1_ref), (near2_hbm, near2_ref),
                (node_hbm, node_ref), (bk_hbm, bk_ref), (bs_hbm, bs_ref), (wk_hbm, wk_ref),
            )
        )
    ]
    for copy in copies:
        copy.start()
    for copy in copies[:-1]:
        copy.wait()
    live = jnp.where(
        lax.broadcasted_iota(jnp.int32, (1, N0), 1) < count_ref[0], 1.0, 0.0
    ).astype(F32)
    parent = hot(N1, pm_ref[...])
    parent_top = hot(N2, pt_ref[...])
    live8 = jnp.broadcast_to(live, (16, N0))
    child_mid = mm(live8.astype(BF), parent, (1, 1))
    live_mid = jnp.where(child_mid > 0.5, 1.0, 0.0)
    child_top = mm(live_mid.astype(BF), parent_top, (1, 1))
    live_top = jnp.where(child_top > 0.5, 1.0, 0.0)
    child_mid = jnp.maximum(child_mid, 1.0)
    child_top = jnp.maximum(child_top, 1.0)
    rows_ref[...] = jnp.zeros_like(rows_ref)
    rows_ref[0:1, :] = live
    rows_ref[1:2, 0:N1] = child_mid[0:1]
    rows_ref[2:3, 0:N1] = live_mid[0:1]
    rows_ref[3:4, 0:N2] = child_top[0:1]
    share = mm_hot(live_mid / child_mid, parent, (1, 0), 3)[0:1] * live
    rows_ref[4:5, :] = share
    parents_ref[0:N1, :] = parent
    composite = mm(parent_top, parent).astype(BF)
    parents_ref[N1:COARSE, :] = composite
    row = lax.broadcasted_iota(jnp.int32, owner_ref.shape, 0)
    lane = lax.broadcasted_iota(jnp.int32, owner_ref.shape, 1)
    mid_own = (lane < E1) & (row == (lane & (N1 - 1)))
    top_own = (lane >= E1) & (lane < E1 + E2) & (row == N1 + (lane & (N2 - 1)))
    owner_ref[...] = jnp.where(mid_own | top_own, 1.0, 0.0).astype(BF)
    index_ref[...] = jnp.zeros_like(index_ref)
    for slot in range(DEG):
        row = slice(slot, slot + 1)
        index_ref[:, slot * N0 : (slot + 1) * N0] = near0_ref[row, :]
        index_ref[:, E0 + slot * N1 : E0 + (slot + 1) * N1] = near1_ref[row, :]
        start = E0 + E1 + slot * N2
        index_ref[:, start : start + N2] = near2_ref[row, :]
    vals[0:16, 0:N0] = jnp.zeros((16, N0), F32)
    vals[0:3, 0:N0] = geometry_ref[...]
    coords = vals[0:16, 0:N0]
    coords_mid = mm_hot(coords * live, parent, (1, 1), 3) / child_mid
    coords_top = mm_hot(coords * share, composite, (1, 1), 3) / child_top
    lane_row = lax.broadcasted_iota(jnp.int32, (16, 1), 0)

    def with_live(values, live_row):
        return jnp.where(lane_row == 3, live_row, values).astype(BF)

    fine_rows = with_live(coords, live)
    mid_rows = with_live(coords_mid, live_mid[0:1])
    top_rows = with_live(coords_top, live_top[0:1])

    def edges(own, near):
        low = jnp.where(lane_row < 3, own, 0.0)
        high = pltpu.roll(jnp.where(lane_row < 3, near, 0.0), 3, 0)
        return jnp.where(lane_row == 6, 1.0, low + high).astype(BF)

    fine = fine_rows.astype(F32)
    masks = []
    for slot in range(DEG):
        lanes = slice(slot * N0, (slot + 1) * N0)
        hot0_ref[:, lanes] = hot(N0, index_ref[:, lanes])
        near = mm(fine_rows, hot0_ref[:, lanes])
        edge_ref[:, lanes] = edges(fine, near)
        masks.append(live * near[3:4])
    total = masks[0]
    for mask in masks[1:]:
        total = total + mask
    total = jnp.maximum(total, 1.0)
    for slot in range(DEG):
        weight_ref[:, slot * N0 : (slot + 1) * N0] = masks[slot] / total

    def small_level(values, rows, start, lanes, hot_ref):
        own = mm(values, owner_hot(rows, lanes))
        hot_ref[...] = hot(rows, index_ref[:, start : start + lanes])
        near = mm(values, hot_ref[...])
        edge_ref[:, start : start + lanes] = edges(own, near)
        mask = own * near
        fold = jnp.where(
            (lax.broadcasted_iota(jnp.int32, (lanes, lanes), 0) & (rows - 1))
            == (lax.broadcasted_iota(jnp.int32, (lanes, lanes), 1) & (rows - 1)),
            1.0,
            0.0,
        ).astype(BF)
        total = jnp.maximum(mm(mask.astype(BF), fold), 1.0)
        weight_ref[:, start : start + lanes] = mask[3:4] / total[3:4]

    small_level(mid_rows, N1, E0, E1, hot1_ref)
    small_level(top_rows, N2, E0 + E1, E2, hot2_ref)
    rest = E0 + E1 + E2
    edge_ref[:, rest:] = jnp.zeros((16, EDGES - rest), BF)
    weight_ref[:, rest:] = jnp.zeros((1, EDGES - rest), F32)
    gather_sources(
        node_ref[...], half_ref[0], (hot0_ref, hot1_ref, hot2_ref), parents_ref, rows_ref,
        weight_ref, vw_ref, vals,
    )
    bias = bk_ref[...].astype(F32)
    copies[-1].wait()
    for layer in range(2):
        for part in range(8):
            (wkt0_ref, wkt1_ref)[layer][part * 256 : (part + 1) * 256, :] = wk_ref[
                layer, :, part * 256 : (part + 1) * 256
            ].T
        for row in range(HALF):
            bias_rows[row : row + 1, :] = bias[layer : layer + 1, row * C : (row + 1) * C]
        bias_rows_ref[layer] = bias_rows[...].astype(BF)
        bias_cols_ref[layer] = bias_rows[...].T.astype(BF)
    for layer in range(2):
        value, slope = gelu_both(mm(first_columns(packed_ref, layer), edge_ref[...]))
        hown_ref[layer] = value.astype(BF)
        sown_ref[layer] = slope.astype(BF)
    second_bias = jnp.concatenate([bs_ref[...].astype(F32), jnp.zeros((6, HID), F32)], axis=0)
    bs_cols_ref[...] = second_bias.T


def first_forward_kernel(
    parents_ref, owner_ref, packed_ref, far_ref, edge_ref, hown_ref, bs_ref, wkt_ref, bias_ref, vw_ref,
    h2_ref, up_ref, msg,
):
    second = second_rows(packed_ref, far_ref, 0).T
    first = first_columns(far_ref, 0)
    bias = bs_ref[:, 0:1]

    def body(lanes):
        away = gelu(mm(first, edge_ref[:, lanes])).astype(BF)
        one = jnp.concatenate([hown_ref[0, :, lanes], away], axis=0)
        h2_ref[0:HID, lanes] = gelu(mm(second, one) + bias).astype(BF)

    halves(body)
    h2_ref[HID:AUG, :] = ones_rows(EDGES)
    message_pass(
        0, h2_ref, parents_ref, owner_ref, wkt_ref, bias_ref, vw_ref, up_ref, msg,
    )


def mlp_kernel(
    layer, packed_ref, far_ref, edge_ref, bs_ref, hown_ref, sown_ref, h1_ref, s1_ref, s2_ref,
    *h2_refs
):
    second = second_rows(packed_ref, far_ref, layer).T
    first = first_columns(far_ref, layer)
    bias = bs_ref[:, layer : layer + 1]

    def body(lanes):
        value, slope = gelu_both(mm(first, edge_ref[:, lanes]))
        one = jnp.concatenate([hown_ref[layer, :, lanes], value.astype(BF)], axis=0)
        h1_ref[0:HID, lanes] = one
        s1_ref[0:128, lanes] = sown_ref[layer, :, lanes]
        s1_ref[128:HID, lanes] = slope.astype(BF)
        value, slope = gelu_both(mm(second, one) + bias)
        s2_ref[:, lanes] = slope.astype(BF)
        for h2_ref in h2_refs:
            h2_ref[0:HID, lanes] = value.astype(BF)

    halves(body)
    h1_ref[HID:AUG, :] = edge_ref[...]
    for h2_ref in h2_refs:
        h2_ref[HID:AUG, :] = ones_rows(EDGES)


def next_forward_kernel(
    half_ref, node_ref, self_ref, up_own_ref, up_far_ref, hot0_ref, hot1_ref, hot2_ref, parents_ref,
    owner_ref, rows_ref, weight_ref, h2_ref, wkt_ref, bias_ref,
    pre_ref, state_ref, up_ref, vw_ref, kept_ref, vals, msg,
):
    pre = mm(self_ref[0].astype(F32).T.astype(BF), node_ref[...])
    pre = pre + (up_own_ref[...] + up_far_ref[...])
    pre_ref[...] = pre
    state = (gelu(pre) * rows_ref[0:1, :]).astype(BF)
    state_ref[...] = state
    gather_sources(
        state, half_ref[0], (hot0_ref, hot1_ref, hot2_ref), parents_ref, rows_ref, weight_ref,
        vw_ref, vals,
    )
    message_pass(
        1, h2_ref, parents_ref, owner_ref, wkt_ref, bias_ref, vw_ref, up_ref, msg, kept_ref,
    )


def node_grads(
    layer, half, h, pre, grad, parents_ref, owner_ref, live, self_ref, own_ref, g_ref
):
    start = pl.multiple_of(half * HALF, HALF)
    _, slope = gelu_both(pre)
    grad_pre = slope * (live * grad)
    high, low = pieces(grad_pre, 2)
    grad_self = mm(h, high, (1, 1)) + mm(h, low, (1, 1))
    own_ref[288:320, 0:C] = grad_self[0:HALF]
    own_ref[288:320, C : 2 * C] = grad_self[HALF:C]
    self_half = self_ref[layer, pl.ds(start, HALF), :]
    self_in = mm(self_half, high) + mm(self_half, low)
    coarse = mm_hot(grad_pre, parents_ref[...], (1, 1), 3).astype(BF)
    g_ref[0:C, 0:N0] = grad_pre.astype(BF)
    g_ref[0:C, N0:] = mm(coarse, owner_ref[...]).astype(BF)
    return self_in


def grad_tile(g_ref, start, width):
    if start < E0:
        return jnp.concatenate([g_ref[0:C, 0:N0]] * (width // N0), axis=1)
    return g_ref[0:C, N0 : N0 + width]


def source_grads(self_in, hot_refs, parents_ref, rows_ref, dvw):
    live, child_mid, child_top, share = level_rows(rows_ref)
    sums = []
    lanes = 0
    for hot_ref in hot_refs:
        count = hot_ref.shape[1]
        total = mm_hot(dvw[:, lanes : lanes + count], hot_ref[...], (1, 1))
        sums.append(total.astype(BF).astype(F32))
        lanes += count
    fine, mid, top = sums
    return (
        self_in
        + fine
        + mm_hot(mid / child_mid, parents_ref[0:N1, :], (1, 0), 3) * live
        + mm_hot(top / child_top, parents_ref[N1:COARSE, :], (1, 0), 3) * share
    )


def fill_pack(core, vw_ref, pack_ref):
    place = pl.ds(pl.multiple_of((1 - core) * QUARTER, QUARTER), QUARTER)
    for index, (start, width) in enumerate(TILES):
        high, low = pieces(vw_ref[place, start : start + width], 2)
        base = C + index * HALF
        pack_ref[base : base + QUARTER, 0:width] = high
        pack_ref[base + QUARTER : base + HALF, 0:width] = low
    pack_ref[C + 2 * HALF : PACK, 768:1024] = jnp.zeros((HALF, 256), BF)


def far_source(pack_ref, index, width):
    base = C + index * HALF
    high = pack_ref[base : base + QUARTER, 0:width].astype(F32)
    return high + pack_ref[base + QUARTER : base + HALF, 0:width].astype(F32)


def fill_grad_kernels(g_ref, source, gk, start, width, rows):
    lanes = slice(start, start + width)
    grad = grad_tile(g_ref, start, width).astype(F32)
    for row in range(rows):
        gk[row * C : (row + 1) * C, lanes] = (grad * source[row : row + 1, :]).astype(BF)


def mlp_backward(
    layer, g_ref, vw_ref, wk_ref, h1_ref, s1_ref, s2_ref, packed_ref, far_ref, own_ref, away_ref,
    gk, both,
):
    second = second_rows(packed_ref, far_ref, layer)
    both[:, FILLED:] = jnp.zeros((2 * HID, EDGES - FILLED), BF)
    for start, width in TILES:
        width = min(width, FILLED - start)
        lanes = slice(start, start + width)
        fill_grad_kernels(g_ref, vw_ref[:, lanes], gk, start, width, HALF)
        two = (s2_ref[:, lanes].astype(F32) * mm(wk_ref[layer], gk[:, lanes])).astype(BF)
        both[0:HID, lanes] = two
        both[HID:, lanes] = (s1_ref[:, lanes].astype(F32) * mm(second, two)).astype(BF)
    product = mm(h1_ref[...], both[...], (1, 1))
    grad_second = product[0:HID, 0:HID]
    grad_first = product[HID : HID + 7, HID:]
    grad_bias = product[HID + 6 : HID + 7, 0:HID]
    own_ref[0:128, :] = grad_second[0:128, 0:128]
    own_ref[128:256, :] = grad_second[0:128, 128:256]
    own_ref[272:273, :] = grad_bias[:, 0:128]
    own_ref[273:274, :] = grad_bias[:, 128:256]
    own_ref[274:281, :] = grad_first[:, 0:128]
    own_ref[281:288, :] = jnp.zeros((7, 128), F32)
    away_ref[0:128, :] = grad_second[128:256, 0:128].astype(BF)
    away_ref[128:256, :] = grad_second[128:256, 128:256].astype(BF)
    tail = jnp.concatenate(
        [grad_bias[:, 0:128], grad_bias[:, 128:256], grad_first[:, 128:256],
         jnp.zeros((7, 128), F32)],
        axis=0,
    )
    away_ref[256:272, :] = tail.astype(BF)


def kernel_weight_kernel(
    core_ref, *refs
):
    layer_refs = (refs[0:5], refs[5:10])
    bias_ref, joined_hbm, gk, joined_ref, sems = refs[10:]
    mine = pl.ds(pl.multiple_of(core_ref[0] * QUARTER, QUARTER), QUARTER)
    copies = []
    for layer in (1, 0):
        pack_ref, far_ref, vw_ref, h2_ref, h2_far_ref = layer_refs[layer]
        for index, (start, width) in enumerate(TILES):
            source = vw_ref[mine, start : start + width]
            fill_grad_kernels(pack_ref, source, gk, start, width, QUARTER)
        product = mm(h2_ref[...], gk[...], (1, 1))
        for index, (start, width) in enumerate(TILES):
            source = far_source(far_ref, index, width)
            fill_grad_kernels(far_ref, source, gk, start, width, QUARTER)
        product = product + mm(h2_far_ref[...], gk[...], (1, 1))
        for part in range(4):
            for block in range(8):
                joined_ref[layer, part * 8 + block] = product[
                    part * 64 : (part + 1) * 64, block * 128 : (block + 1) * 128
                ].astype(BF)
        copy = pltpu.make_async_copy(
            joined_ref.at[layer], joined_hbm.at[:, layer * 64 : (layer + 1) * 64, :], sems.at[layer]
        )
        copy.start()
        copies.append(copy)
        for block in range(8):
            row = layer * 8 + block
            bias_ref[row : row + 1, :] = product[HID : HID + 1, block * 128 : (block + 1) * 128]
    for copy in copies:
        copy.wait()


def last_node_kernel(
    half_ref, core_ref, state_ref, self_ref, up_own_ref, up_far_ref, cot_ref, hot0_ref, hot1_ref,
    hot2_ref, parents_ref, owner_ref, rows_ref, weight_ref, kept_ref, bias_ref, vw_ref,
    out_ref, own_ref, g_ref, dx_ref, dvw, wide,
):
    fill_pack(core_ref[0], vw_ref, g_ref)
    live = rows_ref[0:1, :]
    state = state_ref[...]
    pre = mm(self_ref[1].astype(F32).T.astype(BF), state)
    pre = pre + (up_own_ref[...] + up_far_ref[...])
    out_ref[...] = (gelu(pre) * live).astype(BF)
    self_in = node_grads(
        1, half_ref[0], state, pre, cot_ref[...].astype(F32), parents_ref, owner_ref, live,
        self_ref, own_ref, g_ref,
    )
    for start, width in TILES:
        wide[:, start : start + width] = grad_tile(g_ref, start, width)
    offset = mm(bias_ref[1], wide[...])
    for start, width in TILES:
        lanes = slice(start, start + width)
        grad = wide[:, lanes].astype(F32)
        for part in range(4):
            channels = slice(part * 8, (part + 1) * 8)
            kernels = kept_ref[part * 512 : (part + 1) * 512, lanes].astype(F32)
            total = jnp.sum(kernels.reshape(8, C, width) * grad[None], axis=1)
            dvw[channels, lanes] = (total + offset[channels, lanes]) * weight_ref[:, lanes]
    dx_ref[...] = source_grads(
        self_in, (hot0_ref, hot1_ref, hot2_ref), parents_ref, rows_ref, dvw
    )


def last_edge_kernel(
    core_ref, g_ref, vw_ref, wk_ref, h1_ref, s1_ref, s2_ref, packed_ref, far_ref, self_grad_ref,
    own_ref, away_ref, cross_ref, gk, both,
):
    mlp_backward(
        1, g_ref, vw_ref, wk_ref, h1_ref, s1_ref, s2_ref, packed_ref, far_ref, own_ref, away_ref,
        gk, both,
    )
    own_ref[256:272, :] = jnp.zeros((16, 128), F32)
    own_ref[288:320, :] = self_grad_ref[288:320, :]
    other = pl.ds(pl.multiple_of((1 - core_ref[0]) * 128, 128), 128)
    cross_ref[0:128, :] = own_ref[other, :].astype(BF)
    cross_ref[128:256, :] = away_ref[other, :]


def first_edge_kernel(
    half_ref, core_ref, node_ref, pre_ref, dx_own_ref, dx_far_ref, self_ref, parents_ref, owner_ref,
    rows_ref,
    vw_ref, wk_ref, h1_ref, s1_ref, s2_ref, packed_ref, far_ref,
    g_ref, self_in_ref, own_ref, away_ref, grad, gk, both,
):
    fill_pack(core_ref[0], vw_ref, g_ref)
    start = pl.multiple_of(half_ref[0] * HALF, HALF)
    grad[pl.ds(start, HALF), :] = dx_own_ref[...]
    grad[pl.ds(HALF - start, HALF), :] = dx_far_ref[...]
    self_in_ref[...] = node_grads(
        0, half_ref[0], node_ref[...], pre_ref[...], grad[...], parents_ref, owner_ref,
        rows_ref[0:1, :], self_ref, own_ref, g_ref,
    )
    own_ref[256:272, :] = jnp.zeros((16, 128), F32)
    mlp_backward(
        0, g_ref, vw_ref, wk_ref, h1_ref, s1_ref, s2_ref, packed_ref, far_ref, own_ref,
        away_ref, gk, both,
    )


def first_node_kernel(
    self_in_ref, hot0_ref, hot1_ref, hot2_ref, parents_ref, rows_ref, weight_ref, h2_ref, wkt_ref,
    bias_ref, g_ref,
    dx_ref, dvw,
):

    def part(rows, channels):
        for start, width in TILES:
            lanes = slice(start, start + width)
            grad = grad_tile(g_ref, start, width)
            offset = mm(bias_ref[0, channels, :], grad)
            kernels = mm(wkt_ref[rows, :], h2_ref[0:HID, lanes])
            product = kernels.reshape(HALF // PARTS, C, width) * grad.astype(F32)[None]
            dvw[channels, lanes] = (jnp.sum(product, axis=1) + offset) * weight_ref[:, lanes]

    channel_parts(part, PARTS)
    dx_ref[...] = source_grads(
        self_in_ref[...], (hot0_ref, hot1_ref, hot2_ref), parents_ref, rows_ref, dvw
    )


def pair_kernel(core_ref, own1_ref, away1_ref, cross_ref, away0_ref, mine1_ref, away_ref):
    away_ref[0:AUG, :] = away0_ref[...]
    mine = pl.ds(pl.multiple_of(core_ref[0] * 128, 128), 128)
    mine1_ref[...] = own1_ref[mine, :] + cross_ref[0:128, :].astype(F32)
    away_ref[AUG : AUG + 128, :] = (
        away1_ref[mine, :].astype(F32) + cross_ref[128:256, :].astype(F32)
    ).astype(BF)
    away_ref[AUG + 128 :, :] = away1_ref[256:272, :]


def join_kernel(
    core_ref, own0_ref, own1_ref, mine1_ref, away_ref, bias_ref, _, out_ref, rows, tail, sem
):
    far = away_ref[...].astype(F32)
    rows[0:256, :] = own0_ref[0:256, :] + far[0:256]
    rows[SMALL : SMALL + 128, :] = mine1_ref[...] + far[AUG : AUG + 128]
    for layer, (own_ref, base, place) in enumerate(
        ((own0_ref, 256, 256), (own1_ref, SMALL + 128, AUG + 128))
    ):
        rows[base : base + 16, :] = jnp.zeros((16, 128), F32)
        bias = pl.ds(pl.multiple_of(base + core_ref[0] * 8, 8), 8)
        rows[bias, :] = bias_ref[layer * 8 : (layer + 1) * 8, :]
        rows[base + 16 : base + 32, :] = own_ref[272:288, :] + far[place : place + 16]
        rows[base + 32 : base + 64, :] = own_ref[288:320, :]
    for block in range(32):
        tail[block] = rows[block * 16 : (block + 1) * 16, :].astype(BF)
    copy = pltpu.make_async_copy(tail, out_ref.at[:, 128:BLOCK, :], sem.at[0])
    copy.start()
    copy.wait()


def sum_kernel(parts_ref, out_ref):
    total = parts_ref[0].astype(F32)
    for peer in range(1, 32):
        total = total + parts_ref[peer].astype(F32)
    total = total.astype(BF)
    for peer in range(32):
        out_ref[peer] = total


def spread_blocks(side_ref, kernel_ref):
    part = pl.program_id(0)
    for block in range(8):
        for layer in range(2):
            kernel_ref[layer, :, block * 128 : (block + 1) * 128] = side_ref[
                part * 8 + block, layer * 64 : (layer + 1) * 64, :
            ].astype(F32)


def spread_own_kernel(core_ref, own_ref, kernel_ref):
    spread_blocks(own_ref, kernel_ref)


def spread_far_kernel(
    core_ref, own_ref, far_ref, _,
    kernel_ref, second_ref, second_bias_ref, first_ref, first_bias_ref, kernel_bias_ref, self_ref,
    rows,
):
    spread_blocks(far_ref, kernel_ref)

    @pl.when(pl.program_id(0) == 1)
    def _():
        spread_small(
            core_ref[0], own_ref, far_ref, second_ref, second_bias_ref, first_ref, first_bias_ref,
            kernel_bias_ref, self_ref, rows,
        )


def spread_small(
    core, own_ref, far_ref, second_ref, second_bias_ref, first_ref, first_bias_ref,
    kernel_bias_ref, self_ref, rows,
):
    for block in range(32):
        own = own_ref[block, 128:BLOCK, :].astype(F32)
        far = far_ref[block, 128:BLOCK, :].astype(F32)
        if SMALL // 16 <= block < (SMALL + 128) // 16:
            place = slice(block * 16 - SMALL, block * 16 - SMALL + 16)
            second_ref[1, place, pl.ds(pl.multiple_of(core * 128, 128), 128)] = own
            second_ref[1, place, pl.ds(pl.multiple_of((1 - core) * 128, 128), 128)] = far
        else:
            rows[block * 16 : (block + 1) * 16, :] = own + far
    second_ref[0, :, 0:128] = rows[0:128, :]
    second_ref[0, :, 128:256] = rows[128:256, :]
    for layer, base in enumerate((256, SMALL + 128)):
        for block in range(16):
            lanes = slice(block * 128, (block + 1) * 128)
            kernel_bias_ref[layer : layer + 1, lanes] = rows[base + block : base + block + 1, :]
        second_bias_ref[layer : layer + 1, 0:128] = rows[base + 16 : base + 17, :]
        second_bias_ref[layer : layer + 1, 128:256] = rows[base + 17 : base + 18, :]
        for row in range(6):
            first_ref[row, layer : layer + 1, :] = rows[base + 18 + row : base + 19 + row, :]
        first_bias_ref[layer : layer + 1, :] = rows[base + 24 : base + 25, :]
        self_ref[layer, 0:HALF, :] = rows[base + 32 : base + 64, 0:C]
        self_ref[layer, HALF:C, :] = rows[base + 32 : base + 64, C : 2 * C]


def input_kernel(half_ref, own_ref, far_ref, out_ref):
    start = pl.multiple_of(half_ref[0] * HALF, HALF)
    out_ref[pl.ds(start, HALF), :] = own_ref[...]
    out_ref[pl.ds(HALF - start, HALF), :] = far_ref[...]


def vmem_spec():
    return pl.BlockSpec(memory_space=pltpu.VMEM)


def smem_spec():
    return pl.BlockSpec(memory_space=pltpu.SMEM)


def call(kernel, outs, args, scalars=0, scratch=(), us=1, far=0, far_outs=0, aliases=None):
    count = len(args)
    specs = [smem_spec()] * scalars + [vmem_spec()] * (count - scalars - far)
    args = list(args[: count - far]) + [
        pltpu.with_memory_space_constraint(value, pltpu.HBM) for value in args[count - far :]
    ]
    return pl.pallas_call(
        kernel,
        out_shape=[
            pltpu.HBM(*out) if index >= len(outs) - far_outs else jax.ShapeDtypeStruct(*out)
            for index, out in enumerate(outs)
        ],
        in_specs=specs + [pl.BlockSpec(memory_space=pltpu.HBM)] * far,
        out_specs=[
            pl.BlockSpec(memory_space=pltpu.HBM) if index >= len(outs) - far_outs else vmem_spec()
            for index in range(len(outs))
        ],
        scratch_shapes=[
            pltpu.SemaphoreType.DMA(entry[0]) if entry[1] is None else pltpu.VMEM(*entry)
            for entry in scratch
        ],
        input_output_aliases=aliases or {},
        compiler_params=pltpu.CompilerParams(vmem_limit_bytes=VMEM_MIB << 20),
        cost_estimate=pl.CostEstimate(
            flops=us * 1000000000, bytes_accessed=1 << 20, transcendentals=0
        ),
    )(*args)


def swap(value, axis):
    return lax.ppermute(value, axis, [(0, 1), (1, 0)])


def per_device(
    node_input, geometry, counts, parent_mid, parent_top, neighbours_fine, neighbours_mid,
    neighbours_top, w_first, b_first, w_second, b_second, w_kernel, b_kernel, w_self, cotangent,
):
    half = lax.axis_index("tensor").astype(jnp.int32).reshape(1)
    core = lax.axis_index("core").astype(jnp.int32).reshape(1)
    counts, half, core, w_second = lax.optimization_barrier((counts, half, core, w_second))
    pm = parent_mid.reshape(1, N0)
    pt = parent_top.reshape(1, N1)
    node = node_input.T
    wide = (AUG, EDGES)
    edges = (HID, EDGES)
    sources = (HALF, EDGES)

    (packed,) = call(
        pack_kernel,
        [((AUG, HID), BF)],
        [w_second, w_first.transpose(1, 0, 2), b_first],
        scratch=[((2, 128, HID), BF), ((6, 2, 128), BF), ((2, 128), BF), ((16, HID), F32),
                 ((3,), None)],
        far=3,
    )
    far = swap(packed, "tensor")
    (
        edge, weight, hot0, hot1, hot2, parents, owner, rows, wkt0, wkt1, bias_rows, bias_cols,
        bs_cols,
        hown, sown, vw0, node,
    ) = call(
        prep_kernel,
        [((16, EDGES), BF), ((1, EDGES), F32), ((N0, E0), BF), ((N1, E1), BF), ((N2, E2), BF),
         ((COARSE, N0), BF), ((COARSE, EDGES - E0), BF), ((8, N0), F32), ((HALF * C, HID), BF), ((HALF * C, HID), BF), ((2, HALF, C), BF), ((2, C, HALF), BF), ((HID, 8), F32),
         ((2, 128, EDGES), BF), ((2, 128, EDGES), BF),
         (sources, F32), ((C, N0), BF)],
        [counts, half, packed, geometry.T, pm, pt, neighbours_fine.T, neighbours_mid.T,
         neighbours_top.T, node, b_kernel, b_second, w_kernel],
        scalars=2,
        far=10,
        scratch=[((1, EDGES), jnp.int32), ((1, N0), jnp.int32), ((1, N1), jnp.int32),
                 ((3, N0), F32), ((8, N0), jnp.int32), ((8, N1), jnp.int32), ((8, N2), jnp.int32),
                 ((2, HALF * C), BF), ((2, HID), BF), ((2, HID, HALF * C), BF), ((10,), None),
                 ((C, N0 + 256), F32), ((HALF, C), F32)],
        us=4,
    )
    h2_0, up0 = call(
        first_forward_kernel,
        [(wide, BF), ((C, N0), F32)],
        [parents, owner, packed, far, edge, hown, bs_cols, wkt0, bias_cols, vw0],
        scratch=[((C, EDGES), F32)],
        us=8,
    )
    up0_far = swap(up0, "tensor")
    h2_0_far = swap(h2_0, "core")

    def mlp(layer, outs):
        return call(
            functools.partial(mlp_kernel, layer), outs, [packed, far, edge, bs_cols, hown, sown], us=5
        )

    h1_1, s1_1, s2_1, h2_1 = mlp(1, [(wide, BF), (edges, BF), (edges, BF), (wide, BF)])
    pre0, state, up1, vw1, kept = call(
        next_forward_kernel,
        [((C, N0), F32), ((C, N0), BF), ((C, N0), F32), (sources, F32), ((HALF * C, EDGES), BF)],
        [half, node, w_self, up0, up0_far, hot0, hot1, hot2, parents, owner, rows, weight, h2_1, wkt1,
         bias_cols],
        scalars=1,
        scratch=[((C, N0 + 256), F32), ((C, EDGES), F32)],
        us=5,
    )
    up1_far = swap(up1, "tensor")
    h2_1_far = swap(h2_1, "core")
    up1, edge = lax.optimization_barrier((up1, edge))
    h1_0, s1_0, s2_0 = mlp(0, [(wide, BF), (edges, BF), (edges, BF)])
    h1_0, state = lax.optimization_barrier((h1_0, state))
    out, self_grad1, g1, dx1 = call(
        last_node_kernel,
        [((C, N0), BF), ((SMALL, 128), F32), ((PACK, 1024), BF), ((HALF, N0), F32)],
        [half, core, state, w_self, up1, up1_far, cotangent.T, hot0, hot1, hot2, parents, owner,
         rows, weight, kept, bias_rows, vw1],
        scalars=2,
        scratch=[(sources, F32), ((C, EDGES), BF)],
        us=5,
    )
    dx1_far = swap(dx1, "tensor")
    g1_far = swap(g1, "core")
    edge_scratch = [((HALF * C, EDGES), BF), ((2 * HID, EDGES), BF)]
    own1, away1, cross = call(
        last_edge_kernel,
        [((SMALL, 128), F32), ((AUG, 128), BF), ((256, 128), BF)],
        [core, g1, vw1, w_kernel, h1_1, s1_1, s2_1, packed, far, self_grad1],
        scalars=1,
        scratch=edge_scratch,
        us=5,
    )
    cross_far = swap(cross, "core")
    own1, dx1 = lax.optimization_barrier((own1, dx1))
    g0, self_in0, own0, away0 = call(
        first_edge_kernel,
        [((PACK, 1024), BF), ((HALF, N0), F32), ((SMALL, 128), F32), ((AUG, 128), BF)],
        [half, core, node, pre0, dx1, dx1_far, w_self, parents, owner, rows, vw0, w_kernel, h1_0, s1_0, s2_0,
         packed, far],
        scalars=2,
        scratch=[((C, N0), F32)] + edge_scratch,
        us=6,
    )
    mine1, away = call(
        pair_kernel,
        [((128, 128), F32), ((AUG + 144, 128), BF)],
        [core, own1, away1, cross_far, away0],
        scalars=1,
    )
    away_far = swap(away, "tensor")
    g0_far = swap(g0, "core")
    blocks = (32, BLOCK, 128)
    bias, joined = call(
        kernel_weight_kernel,
        [((16, 128), F32), (blocks, BF)],
        [core, g0, g0_far, vw0, h2_0, h2_0_far, g1, g1_far, vw1, h2_1, h2_1_far],
        scalars=1,
        scratch=[((QUARTER * C, EDGES), BF), ((2, 32, 64, 128), BF), ((2,), None)],
        us=8,
        far_outs=1,
    )
    (joined,) = call(
        join_kernel, [(blocks, BF)], [core, own0, own1, mine1, away_far, bias, joined],
        scalars=1,
        far=1,
        far_outs=1,
        scratch=[((512, 128), F32), ((32, 16, 128), BF), ((1,), None)],
        aliases={6: 0},
    )
    joined, g0 = lax.optimization_barrier((joined, g0))
    parts = lax.all_to_all(joined, ROW_AXES, 0, 0, tiled=True)
    (dx0,) = call(
        first_node_kernel,
        [((HALF, N0), F32)],
        [self_in0, hot0, hot1, hot2, parents, rows, weight, h2_0, wkt0, bias_rows, g0],
        scratch=[(sources, F32)],
        us=5,
    )
    (total,) = call(sum_kernel, [(blocks, BF)], [parts])
    dx0_far = swap(dx0, "tensor")
    total, dx0_far = lax.optimization_barrier((total, dx0_far))
    whole = lax.all_to_all(total, ROW_AXES, 0, 0, tiled=True)
    whole_far = swap(whole, "core")
    (input_grad,) = call(
        input_kernel, [((C, N0), F32)], [half, dx0, dx0_far], scalars=1
    )
    grad_shape = jax.ShapeDtypeStruct((2, HID, HALF * C), F32)
    params = pltpu.CompilerParams(vmem_limit_bytes=VMEM_MIB << 20)
    (grad_kernel,) = pl.pallas_call(
        spread_own_kernel,
        out_shape=[grad_shape],
        grid_spec=pltpu.PrefetchScalarGridSpec(
            num_scalar_prefetch=1,
            grid=(4,),
            in_specs=[vmem_spec()],
            out_specs=[
                pl.BlockSpec((2, 64, QUARTER * C), lambda part, core: (0, part, core[0]))
            ],
        ),
        compiler_params=params,
    )(core, whole)
    small_shapes = (
        (2, 128, HID), (2, HID), (6, 2, 128), (2, 128), (2, HALF * C), (2, C, C)
    )
    grad_kernel, grad_second, grad_b_second, grad_first, grad_b_first, grad_b_kernel, grad_self = (
        pl.pallas_call(
            spread_far_kernel,
            out_shape=[grad_shape]
            + [jax.ShapeDtypeStruct(shape, F32) for shape in small_shapes],
            grid_spec=pltpu.PrefetchScalarGridSpec(
                num_scalar_prefetch=1,
                grid=(4,),
                in_specs=[vmem_spec(), vmem_spec(), pl.BlockSpec(memory_space=pl.ANY)],
                out_specs=[
                    pl.BlockSpec((2, 64, QUARTER * C), lambda part, core: (0, part, 1 - core[0]))
                ]
                + [vmem_spec() for _ in small_shapes],
                scratch_shapes=[pltpu.VMEM((512, 128), F32)],
            ),
            input_output_aliases={3: 0},
            compiler_params=params,
        )(core, whole, whole_far, grad_kernel)
    )
    return (
        out.T, input_grad.T, grad_first.transpose(1, 0, 2), grad_b_first, grad_second,
        grad_b_second, grad_kernel, grad_b_kernel, grad_self,
    )


def solution(mesh):
    fine = Mesh(mesh.devices.reshape(2, 4, 4, 2, 2), DP_AXES + ("tensor",))
    dp = DP_AXES
    placed = (
        P(dp, None), P(dp, None), P(dp), P(dp), P(dp), P(dp, None), P(dp, None), P(dp, None),
        P(None, None, "tensor"), P(None, "tensor"), P(None, "tensor", None), P(),
        P(None, None, "tensor"), P(None, "tensor"), P(), P(dp, None),
    )
    return jax.shard_map(
        per_device,
        mesh=fine,
        in_specs=placed,
        out_specs=(
            P(dp, None), P(dp, None), P(None, None, "tensor"), P(None, "tensor"),
            P(None, "tensor", None), P(), P(None, None, "tensor"), P(None, "tensor"), P(),
        ),
        check_vma=False,
    )
```
